512 devices in a mesh: rows: 8 (over x, core), cols: 64 (over y, z).
Axes of the slice: x: 4, y: 8, z: 8, core: 2. Of those that a mesh axis runs over, the one named last changes fastest.
Arguments:
- blocks: bfloat16 [8, 64, 96, 128, 128], P('rows', 'cols'), may hold values from -0.0048828125 to 0.0048828125
- block_row: int32 [8, 64, 96], P('rows', 'cols'), may hold values from 0 to 7
- block_col: int32 [8, 64, 96], P('rows', 'cols'), may hold values from 0 to 15
- counts: int32 [8, 64], P('rows', 'cols'), may hold values from 32 to 96, as said below
- start_block: bfloat16 [131072, 256], P(('cols', 'rows')), may hold values from -6 to 6
Outputs:
- basis: float32 [131072, 256], P(('cols', 'rows'))
- factor: float32 [256, 256], replicated
The draws below stay inside these ranges and needn't reach their ends.
Inputs may be any that keep to these rules, and one draw needn't show every extreme that they name: `counts`: some tile has all 96 slots live.
All inputs are finite; a program needn't handle non-finite values.
Results may differ from the reference program's by a relative error of at most 0.0044.
Values may be sent and summed in bfloat16 or wider, within the bound.
A program may use at most 64 MiB of HBM per device.

```python
import math
import jax
import jax.numpy as jnp
from jax import lax

K = 256
BS = 128
UT = 1024
IT = 2048
NB = 96
UB = 8
IB = 16
ITEMS = 131072
N_ROWS = 8
N_COLS = 64


def draw_counts(key, part):
    key = jax.random.fold_in(key, 7)
    base = jax.random.randint(key, (N_ROWS * N_COLS,), max(1, NB // 3), NB + 1)
    pick = jax.random.randint(jax.random.fold_in(key, 1), (), 0, N_ROWS * N_COLS)
    base = base.at[pick].set(NB)
    return base.reshape(N_ROWS, N_COLS).astype(jnp.int32)


def touch_ends(array, rng, least, top_value):
    extent = array.shape
    place = [jax.random.randint(jax.random.fold_in(rng, axis), (), 0, extent[axis]) for axis in range(len(extent))]
    array = array.at[tuple(place)].set(least)
    longest = extent.index(max(extent))
    place[longest] = (place[longest] + 1) % extent[longest]
    return array.at[tuple(place)].set(top_value)


def level_of(key, extent, cuts, least, largest):
    gain = 1.0
    for position, shards_of in cuts:
        draws = jax.random.uniform(jax.random.fold_in(jax.random.fold_in(key, 6), position), (shards_of,), jnp.float32, least / len(cuts), largest / len(cuts))
        gain = gain * jnp.repeat(jnp.exp(draws), extent[position] // shards_of).reshape((-1,) + (1,) * (len(extent) - 1 - position))
    return gain


def normal_values(rng, dims, width, bound, cuts=(), kind=jnp.bfloat16):
    drawn = width * jax.random.normal(rng, dims, jnp.float32)
    if cuts:
        drawn = drawn * level_of(rng, dims, cuts, -0.22, 0.18)
    return jnp.clip(drawn, -bound, bound).astype(kind)


def setup_inputs(seed: int = 0) -> dict:
    seeds = jax.random.split(jax.random.key(seed), 6)
    blocks = normal_values(seeds[0], (N_ROWS, N_COLS, NB, BS, BS), ((NB * N_COLS * BS * NB * N_ROWS * BS * IT * N_COLS // (UB * IB)) ** -0.25), 0.0048828125, ((0, 8), (1, 64)))
    block_row = touch_ends(jax.random.randint(seeds[1], (N_ROWS, N_COLS, NB), 0, UB), jax.random.fold_in(seeds[1], 1), 0, UB - 1).astype(jnp.int32)
    block_col = touch_ends(jax.random.randint(seeds[2], (N_ROWS, N_COLS, NB), 0, IB), jax.random.fold_in(seeds[2], 1), 0, IB - 1).astype(jnp.int32)
    counts = draw_counts(jax.random.fold_in(seeds[5], 71), 0)
    start_block = normal_values(seeds[4], (ITEMS, K), 1.0, 6.0, ((0, 512),))
    return {"blocks": blocks, "block_row": block_row, "block_col": block_col, "counts": counts, "start_block": start_block}


def tile_forward(tiles, rows_idx, cols_idx, live, panel):
    group = math.gcd(NB, 32)
    active = (jnp.arange(NB) < live).astype(jnp.float32)
    panel_blocks = panel.reshape(IB, BS, K)

    def step(carry, index):
        start = index * group
        tiles_g = lax.dynamic_slice_in_dim(tiles, start, group, 0).astype(jnp.float32)
        rows_g = lax.dynamic_slice_in_dim(rows_idx, start, group, 0)
        cols_g = lax.dynamic_slice_in_dim(cols_idx, start, group, 0)
        act_g = lax.dynamic_slice_in_dim(active, start, group, 0)
        pieces = jnp.take(panel_blocks, cols_g, axis=0).astype(jnp.float32)
        product = jnp.einsum('nab,nbk->nak', tiles_g, pieces)
        onehot = (rows_g[:, None] == jnp.arange(UB)[None, :]).astype(jnp.float32) * act_g[:, None]
        return (carry + jnp.einsum('nu,nak->uak', onehot, product, precision=lax.Precision.HIGHEST), None)
    total, _ = lax.scan(step, jnp.zeros((UB, BS, K), jnp.float32), jnp.arange(NB // group))
    return total.reshape(UT, K)

def tile_backward(tiles, rows_idx, cols_idx, live, user_tile):
    group = math.gcd(NB, 32)
    active = (jnp.arange(NB) < live).astype(jnp.float32)
    user_blocks = user_tile.reshape(UB, BS, K)

    def step(carry, index):
        start = index * group
        tiles_g = lax.dynamic_slice_in_dim(tiles, start, group, 0).astype(jnp.float32)
        rows_g = lax.dynamic_slice_in_dim(rows_idx, start, group, 0)
        cols_g = lax.dynamic_slice_in_dim(cols_idx, start, group, 0)
        act_g = lax.dynamic_slice_in_dim(active, start, group, 0)
        pieces = jnp.take(user_blocks, rows_g, axis=0).astype(jnp.float32)
        product = jnp.einsum('nab,nak->nbk', tiles_g, pieces)
        onehot = (cols_g[:, None] == jnp.arange(IB)[None, :]).astype(jnp.float32) * act_g[:, None]
        return (carry + jnp.einsum('ni,nbk->ibk', onehot, product, precision=lax.Precision.HIGHEST), None)
    total, _ = lax.scan(step, jnp.zeros((IB, BS, K), jnp.float32), jnp.arange(NB // group))
    return total.reshape(IT, K)

def reference(blocks, block_row, block_col, counts, start_block):
    panels = start_block.reshape(N_COLS, IT, K)

    def user_row(row):

        def one_tile(col):
            return tile_forward(blocks[row, col], block_row[row, col], block_col[row, col], counts[row, col], panels[col])
        return jnp.sum(lax.map(one_tile, jnp.arange(N_COLS)), axis=0).astype(jnp.bfloat16)
    users = lax.map(user_row, jnp.arange(N_ROWS))

    def item_col(col):

        def one_tile(row):
            return tile_backward(blocks[row, col], block_row[row, col], block_col[row, col], counts[row, col], users[row])
        return jnp.sum(lax.map(one_tile, jnp.arange(N_ROWS)), axis=0)
    items = lax.map(item_col, jnp.arange(N_COLS)).reshape(ITEMS, K)
    gram = jnp.dot(items.T, items, precision=lax.Precision.HIGHEST)
    lower = jnp.linalg.cholesky(gram)
    basis = jax.scipy.linalg.solve_triangular(lower, items.T, lower=True).T
    return (basis, lower.T)
```

```python
import functools

import jax
import jax.numpy as jnp
from jax import lax
from jax.experimental import pallas as pl
from jax.experimental.pallas import tpu as pltpu
from jax.sharding import PartitionSpec as P

MESH = pl.DeviceIdType.MESH
F32 = jnp.float32
BF16 = jnp.bfloat16
HIGH = lax.Precision.HIGHEST
LIMIT = 48 * 1024 * 1024
NB = 96
GROUP = 8
STEP = 24
X, Y, Z = 4, 8, 8


def vmem():
    return pl.BlockSpec(memory_space=pltpu.VMEM)


def smem():
    return pl.BlockSpec(memory_space=pltpu.SMEM)


def remote(src, dst, send, recv, device):
    return pltpu.make_async_remote_copy(
        src_ref=src, dst_ref=dst, send_sem=send, recv_sem=recv, device_id=device, device_id_type=MESH
    )


def places():
    row = lax.axis_index("rows")
    col = lax.axis_index("cols")
    return row, col, lax.div(col, Z), lax.rem(col, Z)


def each(count, body):
    def step(i, carry):
        body(i)
        return carry

    lax.fori_loop(1, count, step, 0)


def ring(me, i, count):
    return lax.rem(me + i, count)


def greet(makers):
    barrier = pltpu.get_barrier_semaphore()
    total = 0
    for count, device in makers:
        each(
            count,
            lambda i, device=device: pl.semaphore_signal(
                barrier, inc=1, device_id=device(i), device_id_type=MESH
            ),
        )
        total += count - 1
    pl.semaphore_wait(barrier, total)


def gather_kernel(own_ref, out_ref, send, recv):
    row, col, _, _ = places()
    chip, core = lax.div(row, 2), lax.rem(row, 2)
    partner = (chip * 2 + 1 - core, col)

    def peer(i):
        return (ring(chip, i, X) * 2 + core, col)

    barrier = pltpu.get_barrier_semaphore()
    pl.semaphore_signal(barrier, inc=1, device_id=partner, device_id_type=MESH)
    for i in range(1, X):
        pl.semaphore_signal(barrier, inc=1, device_id=peer(i), device_id_type=MESH)
    pl.semaphore_wait(barrier, X)

    sent = []
    for i in (2, 1, 3):
        copy = remote(own_ref, out_ref.at[row], send.at[i], recv.at[i], peer(i))
        copy.start()
        sent.append(copy)
    copy = remote(own_ref, out_ref.at[row], send.at[0], recv.at[0], partner)
    copy.start()
    sent.append(copy)
    out_ref[row] = own_ref[...]
    for i in (1, 3, 2):
        source = ring(chip, X - i, X) * 2 + core
        block = out_ref.at[source]
        remote(own_ref, block, send.at[i], recv.at[i], peer(i)).wait_recv()
        copy = remote(block, block, send.at[X + i], recv.at[X + i], partner)
        copy.start()
        sent.append(copy)
    for i in (0, 1, 3, 2):
        source = ring(chip, X - i, X) * 2 + 1 - core
        j = i if i == 0 else X + i
        remote(own_ref, out_ref.at[source], send.at[j], recv.at[j], partner).wait_recv()
    for copy in sent:
        copy.wait_send()


def gather_panel(own):
    return pl.pallas_call(
        gather_kernel,
        out_shape=jax.ShapeDtypeStruct((8, 256, 256), BF16),
        in_specs=[vmem()],
        out_specs=vmem(),
        scratch_shapes=[pltpu.SemaphoreType.DMA((8,)), pltpu.SemaphoreType.DMA((8,))],
        compiler_params=pltpu.CompilerParams(
            collective_id=0, has_side_effects=True, vmem_limit_bytes=LIMIT
        ),
        name="gather_panel",
    )(own)


def forward_kernel(rows_ref, cols_ref, count_ref, tiles_ref, panel_ref, out_ref, acc_ref):
    step = pl.program_id(0)

    @pl.when(step == 0)
    def _():
        acc_ref[...] = jnp.zeros_like(acc_ref)

    count = count_ref[0]

    def group(g, carry):
        products = []
        for j in range(GROUP):
            at = g * GROUP + j
            slot = step * STEP + at
            tile = jnp.where(slot < count, tiles_ref[at], jnp.zeros((128, 128), BF16))
            products.append(
                jnp.dot(tile, panel_ref[cols_ref[slot]], preferred_element_type=F32)
            )
        for j in range(GROUP):
            slot = step * STEP + g * GROUP + j
            acc_ref[rows_ref[slot]] += products[j]
        return carry

    lax.fori_loop(0, STEP // GROUP, group, 0)

    @pl.when(step == NB // STEP - 1)
    def _():
        for u in range(8):
            for h in range(2):
                out_ref[h, u] = acc_ref[u, :, h * 128 : (h + 1) * 128].astype(BF16)


def backward_kernel(rows_ref, cols_ref, count_ref, tiles_ref, users_ref, out_ref, wide_ref):
    step = pl.program_id(0)

    @pl.when(step == 0)
    def _():
        out_ref[...] = jnp.zeros_like(out_ref)
        for u in range(8):
            for h in range(2):
                wide_ref[u, :, h * 128 : (h + 1) * 128] = users_ref[h, u]

    count = count_ref[0]

    def group(g, carry):
        products = []
        for j in range(GROUP):
            at = g * GROUP + j
            slot = step * STEP + at
            tile = jnp.where(slot < count, tiles_ref[at], jnp.zeros((128, 128), BF16))
            products.append(
                lax.dot_general(
                    tile, wide_ref[rows_ref[slot]], (((0,), (0,)), ((), ())), preferred_element_type=F32
                )
            )
        for j in range(GROUP):
            slot = step * STEP + g * GROUP + j
            out_ref[cols_ref[slot]] += products[j]
        return carry

    lax.fori_loop(0, STEP // GROUP, group, 0)


def sparse_call(kernel, rows, cols, count, tiles, operand, out, scratch, name):
    zeros = (0,) * operand.ndim
    zeros_out = (0,) * len(out.shape)
    return pl.pallas_call(
        kernel,
        grid=(NB // STEP,),
        out_shape=out,
        in_specs=[
            smem(),
            smem(),
            smem(),
            pl.BlockSpec((STEP, 128, 128), lambda i: (i, 0, 0)),
            pl.BlockSpec(operand.shape, lambda i: zeros),
        ],
        out_specs=pl.BlockSpec(out.shape, lambda i: zeros_out),
        scratch_shapes=[scratch],
        compiler_params=pltpu.CompilerParams(
            dimension_semantics=("arbitrary",), vmem_limit_bytes=LIMIT
        ),
        name=name,
    )(rows, cols, count, tiles, operand)


def users_kernel(part_ref, out_ref, got1, sum1, got2, mine, wide, send, recv):
    row, col, y, z = places()
    me = (y, z)

    def along(axis, i):
        if axis == 0:
            return ring(y, i, Y), (row, ring(y, i, Y) * Z + z)
        return ring(z, i, Z), (row, y * Z + ring(z, i, Z))

    greet([(Y, lambda i: along(0, i)[1]), (Z, lambda i: along(1, i)[1])])

    def exchange(stage, jobs):
        for half, (axis, source, landing) in enumerate(jobs):
            def start(i, half=half, axis=axis, source=source, landing=landing):
                target, device = along(axis, i)
                remote(
                    source(target), landing.at[me[axis]],
                    send.at[stage, half, i], recv.at[stage, half, i], device,
                ).start()

            each(8, start)

    def arrived(stage, jobs):
        for half, (axis, source, landing) in enumerate(jobs):
            def wait(i, half=half, axis=axis, source=source, landing=landing):
                origin = ring(me[axis], 8 - i, 8)
                target, device = along(axis, i)
                remote(
                    source(target), landing.at[origin],
                    send.at[stage, half, i], recv.at[stage, half, i], device,
                ).wait_recv()

            each(8, wait)

    def departed(stage, jobs):
        for half, (axis, source, landing) in enumerate(jobs):
            def wait(i, half=half, axis=axis, source=source, landing=landing):
                target, device = along(axis, i)
                remote(
                    source(target), landing.at[me[axis]],
                    send.at[stage, half, i], recv.at[stage, half, i], device,
                ).wait_send()

            each(8, wait)

    first = [(h, lambda t, h=h: part_ref.at[h, t], got1.at[h]) for h in range(2)]
    exchange(0, first)
    for h in range(2):
        got1[h, me[h]] = part_ref[h, me[h]]
    arrived(0, first)
    for h in range(2):
        total = got1[h, 0].astype(F32)
        for k in range(1, 8):
            total = total + got1[h, k].astype(F32)
        sum1[h] = total.reshape(8, 16, 128)

    second = [(1 - h, lambda t, h=h: sum1.at[h, t], got2.at[h]) for h in range(2)]
    exchange(1, second)
    for h in range(2):
        got2[h, me[1 - h]] = sum1[h, me[1 - h]]
    arrived(1, second)
    for h in range(2):
        total = got2[h, 0]
        for k in range(1, 8):
            total = total + got2[h, k]
        mine[h] = total.astype(BF16)

    third = [(1 - h, lambda t, h=h: mine.at[h], wide.at[h]) for h in range(2)]
    exchange(2, third)
    for h in range(2):
        wide[h, me[1 - h]] = mine[h]
    arrived(2, third)

    fourth = [(h, lambda t, h=h: wide.at[h], out_ref.at[h]) for h in range(2)]
    exchange(3, fourth)
    for h in range(2):
        out_ref[h, me[h]] = wide[h]
    arrived(3, fourth)
    for stage, jobs in enumerate((first, second, third, fourth)):
        departed(stage, jobs)


def sum_users(part):
    return pl.pallas_call(
        users_kernel,
        out_shape=jax.ShapeDtypeStruct((2, 8, 8, 16, 128), BF16),
        in_specs=[vmem()],
        out_specs=vmem(),
        scratch_shapes=[
            pltpu.VMEM((2, 8, 128, 128), BF16),
            pltpu.VMEM((2, 8, 16, 128), F32),
            pltpu.VMEM((2, 8, 16, 128), F32),
            pltpu.VMEM((2, 16, 128), BF16),
            pltpu.VMEM((2, 8, 16, 128), BF16),
            pltpu.SemaphoreType.DMA((4, 2, 8)),
            pltpu.SemaphoreType.DMA((4, 2, 8)),
        ],
        compiler_params=pltpu.CompilerParams(
            collective_id=1, has_side_effects=True, vmem_limit_bytes=LIMIT
        ),
        name="sum_users",
    )(part)


def items_kernel(
    terms_ref, items_ref, gram_ref, near, pack, far, cut, got1, sum1, got2, sum2, got3, sum3, wide,
    send_a, recv_a, send_b, recv_b, send, recv,
):
    row, col, y, z = places()
    chip, core = lax.div(row, 2), lax.rem(row, 2)
    partner = (chip * 2 + 1 - core, col)
    spots = {"r": row, "y": y, "z": z}

    def along(axis, i):
        target = ring(spots[axis], i, 8)
        if axis == "r":
            return target, (target, col)
        if axis == "y":
            return target, (row, target * Z + z)
        return target, (row, y * Z + target)

    greet([(8, lambda i, axis=axis: along(axis, i)[1]) for axis in "ryz"])

    close = []
    for i in (1, 3, 2, 0):
        chunk = ring(chip, i, X) * 2 + 1 - core
        copy = remote(terms_ref.at[chunk], near.at[i], send_a.at[i], recv_a.at[i], partner)
        copy.start()
        close.append(copy)
    hops = []
    for n, i in enumerate((1, 3, 2)):
        close[n].wait_recv()
        chunk = ring(chip, i, X) * 2 + core
        pack[i] = (terms_ref[chunk] + near[i]).astype(BF16)
        copy = remote(pack.at[i], far.at[i], send_b.at[i], recv_b.at[i], (chunk, col))
        copy.start()
        hops.append(copy)
    close[3].wait_recv()
    items = terms_ref[row] + near[0]
    for n, i in enumerate((1, 3, 2)):
        hops[n].wait_recv()
        items = items + far[i].astype(F32)
    items_ref[...] = items

    gram = lax.dot_general(
        items, items, (((0,), (0,)), ((), ())), precision=HIGH, preferred_element_type=F32
    )
    for k in range(32):
        for c in range(2):
            cut[k // 4, (k % 4) * 2 + c] = gram[8 * k : 8 * k + 8, 128 * c : 128 * c + 128]

    def move(stage, axis, source, landing):
        here = spots[axis]

        def start(i):
            target, device = along(axis, i)
            remote(
                source(target), landing.at[here], send.at[stage, i], recv.at[stage, i], device
            ).start()

        def wait(i):
            target, device = along(axis, i)
            remote(
                source(target), landing.at[ring(here, 8 - i, 8)], send.at[stage, i], recv.at[stage, i], device
            ).wait_recv()

        each(8, start)
        landing[here] = source(here)[...]
        each(8, wait)

    def left(stage, axis, source, landing):
        def wait(i):
            target, device = along(axis, i)
            remote(
                source(target), landing.at[spots[axis]], send.at[stage, i], recv.at[stage, i], device
            ).wait_send()

        each(8, wait)

    def summed(got):
        total = got[0]
        for k in range(1, 8):
            total = total + got[k]
        return total

    jobs = [
        ("r", lambda t: cut.at[t], got1),
        ("y", lambda t: sum1.at[t], got2),
        ("z", lambda t: sum2, got3),
        ("y", lambda t: sum3, wide),
        ("r", lambda t: wide, gram_ref),
    ]
    move(0, *jobs[0])
    sum1[...] = summed(got1)
    move(1, *jobs[1])
    sum2[...] = summed(got2)
    move(2, *jobs[2])
    sum3[...] = summed(got3)
    move(3, *jobs[3])
    move(4, *jobs[4])
    for copy in close + hops:
        copy.wait_send()
    for stage, job in enumerate(jobs):
        left(stage, *job)


def sum_items(terms):
    tile = (8, 128)
    return pl.pallas_call(
        items_kernel,
        out_shape=(
            jax.ShapeDtypeStruct((256, 256), F32),
            jax.ShapeDtypeStruct((8, 8) + tile, F32),
        ),
        in_specs=[vmem()],
        out_specs=(vmem(), vmem()),
        scratch_shapes=[
            pltpu.VMEM((X, 256, 256), F32),
            pltpu.VMEM((X, 256, 256), BF16),
            pltpu.VMEM((X, 256, 256), BF16),
            pltpu.VMEM((8, 8) + tile, F32),
            pltpu.VMEM((8, 8) + tile, F32),
            pltpu.VMEM((8,) + tile, F32),
            pltpu.VMEM((8,) + tile, F32),
            pltpu.VMEM(tile, F32),
            pltpu.VMEM((8,) + tile, F32),
            pltpu.VMEM(tile, F32),
            pltpu.VMEM((8,) + tile, F32),
            pltpu.SemaphoreType.DMA((X,)),
            pltpu.SemaphoreType.DMA((X,)),
            pltpu.SemaphoreType.DMA((X,)),
            pltpu.SemaphoreType.DMA((X,)),
            pltpu.SemaphoreType.DMA((5, 8)),
            pltpu.SemaphoreType.DMA((5, 8)),
        ],
        compiler_params=pltpu.CompilerParams(
            collective_id=2, has_side_effects=True, vmem_limit_bytes=LIMIT
        ),
        name="sum_items",
    )(terms)


PANEL = 32
N = 256


def factor_kernel(gram_ref, items_ref, basis_ref, factor_ref, a_ref, d_ref):
    for k in range(32):
        for c in range(2):
            a_ref[8 * k : 8 * k + 8, 128 * c : 128 * c + 128] = gram_ref[k // 4, (k % 4) * 2 + c]

    def panel(q, carry):
        base = q * PANEL
        rows = pl.ds(pl.multiple_of(base, PANEL), PANEL)
        w = pltpu.roll(a_ref[rows, :], lax.rem(N - base, N), 1)
        d = jnp.zeros((PANEL, 128), F32)
        for t in range(PANEL // 8):
            low = 8 * t
            part = w[low:, :]
            size = PANEL - low
            lane = lax.broadcasted_iota(jnp.int32, (size, N), 1)
            sub = lax.broadcasted_iota(jnp.int32, (size, N), 0) + low
            sub1 = sub[:, :128]
            columns = [
                jnp.broadcast_to(part[:, low + b : low + b + 1], (size, 128)) for b in range(8)
            ]
            d_part = d[low:, :]
            for a in range(8):
                r = low + a
                pivot = columns[a][a : a + 1, :]
                m = jnp.where(sub1 > r, columns[a] * (1.0 / pivot), 0.0)
                for b in range(a + 1, 8):
                    columns[b] = columns[b] - m * columns[b][a : a + 1, :]
                line = jnp.where(lane[:1] == r, 1.0, part[a : a + 1, :])
                kept = jnp.where((lane == r) & (sub > r), 0.0, part)
                part = kept - jnp.concatenate([m, m], axis=1) * line
                d_part = jnp.where(sub1 == r, pivot, d_part)
            w = part if low == 0 else jnp.concatenate([w[:low], part], axis=0)
            d = d_part if low == 0 else jnp.concatenate([d[:low], d_part], axis=0)
        d_ref[rows, :] = d
        lane = lax.broadcasted_iota(jnp.int32, (PANEL, N), 1)
        sub = lax.broadcasted_iota(jnp.int32, (PANEL, N), 0)
        d2 = jnp.concatenate([d, d], axis=1)
        ahead = (lane >= PANEL) & (lane < N - base)
        scaled = jnp.where(ahead, w / d2, 0.0)
        right = jnp.where((lane < PANEL) & (lane >= sub), jnp.where(lane == sub, 1.0, 0.0), w)
        a_ref[rows, :] = pltpu.roll(w, base, 1)
        scaled = pltpu.roll(scaled, base, 1)
        right = pltpu.roll(right, base, 1)
        update = lax.dot_general(
            scaled, right, (((0,), (0,)), ((), ())), precision=HIGH, preferred_element_type=F32
        )
        full_lane = lax.broadcasted_iota(jnp.int32, (N, N), 1)
        full_sub = lax.broadcasted_iota(jnp.int32, (N, N), 0)
        done = (full_sub >= base + PANEL) & (full_lane >= base) & (full_lane < base + PANEL)
        a_ref[...] = jnp.where(done, 0.0, a_ref[...]) - update
        return carry

    lax.fori_loop(0, N // PANEL, panel, 0)

    lane = lax.broadcasted_iota(jnp.int32, (N, N), 1)
    sub = lax.broadcasted_iota(jnp.int32, (N, N), 0)
    scale = 1.0 / jnp.sqrt(d_ref[...])
    scale = jnp.concatenate([scale, scale], axis=1)
    full = a_ref[...]
    factor_ref[...] = jnp.where(lane >= sub, full, 0.0) * scale
    inverse = jnp.where(lane < sub, full, jnp.where(lane == sub, 1.0, 0.0)) * scale
    basis_ref[...] = lax.dot_general(
        items_ref[...], inverse, (((1,), (1,)), ((), ())), precision=HIGH, preferred_element_type=F32
    )


def factor_call(gram, items):
    return pl.pallas_call(
        factor_kernel,
        out_shape=(
            jax.ShapeDtypeStruct((256, 256), F32),
            jax.ShapeDtypeStruct((256, 256), F32),
        ),
        in_specs=[vmem(), vmem()],
        out_specs=(vmem(), vmem()),
        scratch_shapes=[pltpu.VMEM((N, N), F32), pltpu.VMEM((N, 128), F32)],
        compiler_params=pltpu.CompilerParams(vmem_limit_bytes=LIMIT),
        name="factor",
    )(gram, items)


def local(blocks, block_row, block_col, counts, start_block):
    tiles = blocks[0, 0]
    rows = block_row[0, 0]
    cols = block_col[0, 0]
    count = counts[0]
    panel = gather_panel(start_block).reshape(16, 128, 256)
    part = sparse_call(
        forward_kernel, rows, cols, count, tiles, panel,
        jax.ShapeDtypeStruct((2, 8, 128, 128), BF16), pltpu.VMEM((8, 128, 256), F32), "forward",
    )
    users = sum_users(part).reshape(2, 8, 128, 128)
    terms = sparse_call(
        backward_kernel, rows, cols, count, tiles, users,
        jax.ShapeDtypeStruct((16, 128, 256), F32), pltpu.VMEM((8, 128, 256), BF16), "backward",
    )
    items, gram = sum_items(terms.reshape(8, 256, 256))
    return factor_call(gram, items)


def solution(mesh):
    return jax.shard_map(
        local,
        mesh=mesh,
        in_specs=(
            P("rows", "cols", None, None, None),
            P("rows", "cols", None),
            P("rows", "cols", None),
            P("rows", "cols"),
            P(("cols", "rows"), None),
        ),
        out_specs=(P(("cols", "rows"), None), P()),
        check_vma=False,
    )
```

```python
import jax
import jax.numpy as jnp
from jax import lax
from jax.experimental import pallas as pl
from jax.experimental.pallas import tpu as pltpu
from jax.sharding import PartitionSpec as P

MESH = pl.DeviceIdType.MESH
F32 = jnp.float32
BF16 = jnp.bfloat16
HIGH = lax.Precision.HIGHEST
LIMIT = 48 * 1024 * 1024
NB = 96
GROUP = 8
STEP = 24
X, Y, Z = 4, 8, 8


def vmem():
    return pl.BlockSpec(memory_space=pltpu.VMEM)


def smem():
    return pl.BlockSpec(memory_space=pltpu.SMEM)


def remote(src, dst, send, recv, device):
    return pltpu.make_async_remote_copy(
        src_ref=src, dst_ref=dst, send_sem=send, recv_sem=recv, device_id=device, device_id_type=MESH
    )


def places():
    row = lax.axis_index("rows")
    col = lax.axis_index("cols")
    return row, col, lax.div(col, Z), lax.rem(col, Z)


def each(count, body):
    def step(i, carry):
        body(i)
        return carry

    lax.fori_loop(1, count, step, 0)


def ring(me, i, count):
    return lax.rem(me + i, count)


def greet(makers):
    barrier = pltpu.get_barrier_semaphore()
    total = 0
    for count, device in makers:
        each(
            count,
            lambda i, device=device: pl.semaphore_signal(
                barrier, inc=1, device_id=device(i), device_id_type=MESH
            ),
        )
        total += count - 1
    pl.semaphore_wait(barrier, total)


def dense_kernel(rows_ref, cols_ref, count_ref, tiles_ref, out_ref, acc_ref):
    step = pl.program_id(0)

    @pl.when(step == 0)
    def _():
        acc_ref[...] = jnp.zeros_like(acc_ref)

    count = count_ref[0]

    def group(g, carry):
        for j in range(GROUP):
            at = g * GROUP + j
            slot = step * STEP + at
            tile = jnp.where(slot < count, tiles_ref[at].astype(F32), 0.0)
            place = cols_ref[slot]
            acc_ref[lax.div(place, 2), lax.rem(place, 2), rows_ref[slot]] += tile
        return carry

    lax.fori_loop(0, STEP // GROUP, group, 0)

    @pl.when(step == NB // STEP - 1)
    def _():
        def chunk(q, carry):
            for u in range(8):
                for e in range(2):
                    out_ref[q, u * 128 : (u + 1) * 128, e * 128 : (e + 1) * 128] = acc_ref[
                        q, e, u
                    ].astype(BF16)
            return carry

        lax.fori_loop(0, 8, chunk, 0)


def dense_tile(rows, cols, count, tiles):
    return pl.pallas_call(
        dense_kernel,
        grid=(NB // STEP,),
        out_shape=jax.ShapeDtypeStruct((8, 1024, 256), BF16),
        in_specs=[smem(), smem(), smem(), pl.BlockSpec((STEP, 128, 128), lambda i: (i, 0, 0))],
        out_specs=pl.BlockSpec((8, 1024, 256), lambda i: (0, 0, 0)),
        scratch_shapes=[pltpu.VMEM((8, 2, 8, 128, 128), F32)],
        compiler_params=pltpu.CompilerParams(
            dimension_semantics=("arbitrary",), vmem_limit_bytes=LIMIT
        ),
        name="dense_tile",
    )(rows, cols, count, tiles)


HALF = 128


def krylov_kernel(
    own_ref, tile_ref, items_ref, gram_ref,
    panel, acc, part, got1, sum1, got2, mine, wide, turned, users,
    give, near, pack, relay, far, cut, gram1, gsum1, gram2, gsum2, gram3, gsum3, gwide,
    send_p, recv_p, send_u, recv_u, send_a, recv_a, send_b, recv_b, send_g, recv_g,
):
    row, col, y, z = places()
    chip, core = lax.div(row, 2), lax.rem(row, 2)
    other = 1 - core
    partner = (chip * 2 + other, col)
    spots = {"r": row, "y": y, "z": z}

    def spot(i, which):
        return ring(chip, i, X) * 2 + which

    def beside(i):
        return (spot(i, core), col)

    def along(axis, i):
        target = ring(spots[axis], i, 8)
        if axis == "r":
            return target, (target, col)
        if axis == "y":
            return target, (row, target * Z + z)
        return target, (row, y * Z + target)

    greet([(8, lambda i, axis=axis: along(axis, i)[1]) for axis in "ryz"])

    sent = []

    def push(n, src, dst, device):
        copy = remote(src, dst, send_p.at[n], recv_p.at[n], device)
        copy.start()
        sent.append(copy)

    def landed(n, dst):
        remote(dst, dst, send_p.at[n], recv_p.at[n], partner).wait_recv()

    def product(q):
        return jnp.dot(tile_ref[q], panel[q], preferred_element_type=F32)

    push(1, own_ref, panel.at[row], beside(1))
    push(2, own_ref, panel.at[row], beside(3))
    push(0, own_ref, panel.at[row], partner)
    acc[...] = jnp.dot(tile_ref[row], own_ref[...], preferred_element_type=F32)
    landed(0, panel.at[spot(0, other)])
    acc[...] += product(spot(0, other))
    low, high = pl.ds(0, HALF), pl.ds(HALF, HALF)
    prev, nxt, over = spot(3, core), spot(1, core), spot(2, core)
    landed(1, panel.at[prev])
    push(3, panel.at[prev, low], panel.at[prev, low], beside(1))
    push(5, panel.at[prev], panel.at[prev], partner)
    landed(2, panel.at[nxt])
    push(4, panel.at[nxt, high], panel.at[nxt, high], beside(3))
    push(6, panel.at[nxt], panel.at[nxt], partner)
    acc[...] += product(prev)
    acc[...] += product(nxt)
    landed(5, panel.at[spot(3, other)])
    acc[...] += product(spot(3, other))
    landed(6, panel.at[spot(1, other)])
    acc[...] += product(spot(1, other))
    landed(3, panel.at[over, low])
    push(7, panel.at[over, low], panel.at[over, low], partner)
    landed(4, panel.at[over, high])
    push(8, panel.at[over, high], panel.at[over, high], partner)
    acc[...] += product(over)
    last = spot(2, other)
    landed(7, panel.at[last, low])
    landed(8, panel.at[last, high])
    total = acc[...] + product(last)
    for u in range(8):
        for h in range(2):
            part[h, u] = total[u * 128 : (u + 1) * 128, h * 128 : (h + 1) * 128].astype(BF16)

    def walk(axis, source, landing, sends, recvs, what):
        here = spots[axis]

        def step(i):
            target, device = along(axis, i)
            place = here if what != "arrive" else ring(here, 8 - i, 8)
            copy = remote(source(target), landing.at[place], sends.at[i], recvs.at[i], device)
            if what == "start":
                copy.start()
            elif what == "arrive":
                copy.wait_recv()
            else:
                copy.wait_send()

        each(8, step)

    stages = []

    def exchange(jobs):
        stage = len(stages)
        stages.append(jobs)
        for h, job in enumerate(jobs):
            walk(*job, send_u.at[stage, h], recv_u.at[stage, h], "start")

    def arrived(h):
        stage = len(stages) - 1
        walk(*stages[stage][h], send_u.at[stage, h], recv_u.at[stage, h], "arrive")

    me, first, second = (y, z), ("y", "z"), ("z", "y")
    exchange([(first[h], lambda t, h=h: part.at[h, t], got1.at[h]) for h in range(2)])
    for h in range(2):
        got1[h, me[h]] = part[h, me[h]]
    for h in range(2):
        arrived(h)
        total = got1[h, 0].astype(F32)
        for k in range(1, 8):
            total = total + got1[h, k].astype(F32)
        sum1[h] = total.reshape(8, 16, 128)
    exchange([(second[h], lambda t, h=h: sum1.at[h, t], got2.at[h]) for h in range(2)])
    for h in range(2):
        got2[h, me[1 - h]] = sum1[h, me[1 - h]]
    for h in range(2):
        arrived(h)
        total = got2[h, 0]
        for k in range(1, 8):
            total = total + got2[h, k]
        mine[h] = total.astype(BF16)
    exchange([(second[h], lambda t, h=h: mine.at[h], wide.at[h]) for h in range(2)])
    for h in range(2):
        wide[h, me[1 - h]] = mine[h]
    for h in range(2):
        arrived(h)
        turned[h] = wide[h].reshape(128, 128).astype(F32).T.astype(BF16)
    exchange([(first[h], lambda t, h=h: turned.at[h], users.at[h]) for h in range(2)])
    for h in range(2):
        users[h, me[h]] = turned[h]
    for h in range(2):
        arrived(h)

    def term(q):
        left = jnp.concatenate(
            [jnp.concatenate([users[h, u] for u in range(8)], axis=1) for h in range(2)], axis=0
        )
        return jnp.dot(left, tile_ref[q], preferred_element_type=F32)

    def start(n, src, dst, device):
        copy = remote(src, dst, send_b.at[n], recv_b.at[n], device)
        copy.start()
        sent.append(copy)

    def met(n, dst):
        remote(dst, dst, send_b.at[n], recv_b.at[n], partner).wait_recv()

    close = {}
    for i in (2, 1, 3, 0):
        give[i] = term(spot(i, other))
        close[i] = remote(give.at[i], near.at[i], send_a.at[i], recv_a.at[i], partner)
        close[i].start()
        sent.append(close[i])

    t2 = term(spot(2, core))
    close[2].wait_recv()
    pack[2] = (t2 + near[2]).astype(BF16)
    start(0, pack.at[2, low], relay.at[0], beside(1))
    start(1, pack.at[2, high], relay.at[1], beside(3))
    t1 = term(spot(1, core))
    close[1].wait_recv()
    near[1] = t1 + near[1]
    pack[1, HALF:] = near[1, HALF:].astype(BF16)
    start(2, pack.at[1, high], far.at[0, high], beside(1))
    t3 = term(spot(3, core))
    close[3].wait_recv()
    near[3] = t3 + near[3]
    pack[3, :HALF] = near[3, :HALF].astype(BF16)
    start(3, pack.at[3, low], far.at[1, low], beside(3))
    t0 = term(row)
    close[0].wait_recv()
    near[0] = t0 + near[0]
    met(0, relay.at[0])
    pack[1, :HALF] = (near[1, :HALF] + relay[0].astype(F32)).astype(BF16)
    start(4, pack.at[1, low], far.at[0, low], beside(1))
    met(1, relay.at[1])
    pack[3, HALF:] = (near[3, HALF:] + relay[1].astype(F32)).astype(BF16)
    start(5, pack.at[3, high], far.at[1, high], beside(3))
    met(2, far.at[0, high])
    met(3, far.at[1, low])
    met(4, far.at[0, low])
    met(5, far.at[1, high])
    items = near[0] + far[0].astype(F32) + far[1].astype(F32)
    items_ref[...] = items

    gram = lax.dot_general(
        items, items, (((1,), (1,)), ((), ())), precision=HIGH, preferred_element_type=F32
    )
    for k in range(32):
        for c in range(2):
            cut[k // 4, (k % 4) * 2 + c] = gram[8 * k : 8 * k + 8, 128 * c : 128 * c + 128]

    def summed(got):
        total = got[0]
        for k in range(1, 8):
            total = total + got[k]
        return total

    jobs = [
        ("r", lambda t: cut.at[t], gram1),
        ("y", lambda t: gsum1.at[t], gram2),
        ("z", lambda t: gsum2, gram3),
        ("y", lambda t: gsum3, gwide),
        ("r", lambda t: gwide, gram_ref),
    ]

    def move(n):
        axis, source, landing = jobs[n]
        walk(*jobs[n], send_g.at[n], recv_g.at[n], "start")
        landing[spots[axis]] = source(spots[axis])[...]
        walk(*jobs[n], send_g.at[n], recv_g.at[n], "arrive")

    move(0)
    gsum1[...] = summed(gram1)
    move(1)
    gsum2[...] = summed(gram2)
    move(2)
    gsum3[...] = summed(gram3)
    move(3)
    move(4)

    for copy in sent:
        copy.wait_send()
    for stage, pair in enumerate(stages):
        for h, job in enumerate(pair):
            walk(*job, send_u.at[stage, h], recv_u.at[stage, h], "leave")
    for n, job in enumerate(jobs):
        walk(*job, send_g.at[n], recv_g.at[n], "leave")


def krylov(own, tile):
    cell = (8, 128)
    dma = pltpu.SemaphoreType.DMA
    pairs = [(9,), (4, 2, 8), (X,), (6,), (5, 8)]
    return pl.pallas_call(
        krylov_kernel,
        out_shape=(
            jax.ShapeDtypeStruct((256, 256), F32),
            jax.ShapeDtypeStruct((8, 8) + cell, F32),
        ),
        in_specs=[vmem(), vmem()],
        out_specs=(vmem(), vmem()),
        scratch_shapes=[
            pltpu.VMEM((8, 256, 256), BF16),
            pltpu.VMEM((1024, 256), F32),
            pltpu.VMEM((2, 8, 128, 128), BF16),
            pltpu.VMEM((2, 8, 128, 128), BF16),
            pltpu.VMEM((2, 8, 16, 128), F32),
            pltpu.VMEM((2, 8, 16, 128), F32),
            pltpu.VMEM((2, 16, 128), BF16),
            pltpu.VMEM((2, 8, 16, 128), BF16),
            pltpu.VMEM((2, 128, 128), BF16),
            pltpu.VMEM((2, 8, 128, 128), BF16),
            pltpu.VMEM((X, 256, 256), F32),
            pltpu.VMEM((X, 256, 256), F32),
            pltpu.VMEM((X, 256, 256), BF16),
            pltpu.VMEM((2, HALF, 256), BF16),
            pltpu.VMEM((2, 256, 256), BF16),
            pltpu.VMEM((8, 8) + cell, F32),
            pltpu.VMEM((8, 8) + cell, F32),
            pltpu.VMEM((8,) + cell, F32),
            pltpu.VMEM((8,) + cell, F32),
            pltpu.VMEM(cell, F32),
            pltpu.VMEM((8,) + cell, F32),
            pltpu.VMEM(cell, F32),
            pltpu.VMEM((8,) + cell, F32),
        ]
        + [dma(shape) for shape in pairs for _ in range(2)],
        compiler_params=pltpu.CompilerParams(
            collective_id=0, has_side_effects=True, vmem_limit_bytes=LIMIT
        ),
        name="krylov",
    )(own, tile)


PANEL = 32
N = 256


def factor_kernel(gram_ref, items_ref, basis_ref, factor_ref, a_ref, d_ref):
    for k in range(32):
        for c in range(2):
            a_ref[8 * k : 8 * k + 8, 128 * c : 128 * c + 128] = gram_ref[k // 4, (k % 4) * 2 + c]

    def panel(q, carry):
        base = q * PANEL
        rows = pl.ds(pl.multiple_of(base, PANEL), PANEL)
        w = pltpu.roll(a_ref[rows, :], lax.rem(N - base, N), 1)
        d = jnp.zeros((PANEL, 128), F32)
        for t in range(PANEL // 8):
            low = 8 * t
            part = w[low:, :]
            size = PANEL - low
            lane = lax.broadcasted_iota(jnp.int32, (size, N), 1)
            sub = lax.broadcasted_iota(jnp.int32, (size, N), 0) + low
            sub1 = sub[:, :128]
            columns = [
                jnp.broadcast_to(part[:, low + b : low + b + 1], (size, 128)) for b in range(8)
            ]
            d_part = d[low:, :]
            for a in range(8):
                r = low + a
                pivot = columns[a][a : a + 1, :]
                m = jnp.where(sub1 > r, columns[a] * (1.0 / pivot), 0.0)
                for b in range(a + 1, 8):
                    columns[b] = columns[b] - m * columns[b][a : a + 1, :]
                line = jnp.where(lane[:1] == r, 1.0, part[a : a + 1, :])
                kept = jnp.where((lane == r) & (sub > r), 0.0, part)
                part = kept - jnp.concatenate([m, m], axis=1) * line
                d_part = jnp.where(sub1 == r, pivot, d_part)
            w = part if low == 0 else jnp.concatenate([w[:low], part], axis=0)
            d = d_part if low == 0 else jnp.concatenate([d[:low], d_part], axis=0)
        d_ref[rows, :] = d
        lane = lax.broadcasted_iota(jnp.int32, (PANEL, N), 1)
        sub = lax.broadcasted_iota(jnp.int32, (PANEL, N), 0)
        d2 = jnp.concatenate([d, d], axis=1)
        ahead = (lane >= PANEL) & (lane < N - base)
        scaled = jnp.where(ahead, w / d2, 0.0)
        right = jnp.where((lane < PANEL) & (lane >= sub), jnp.where(lane == sub, 1.0, 0.0), w)
        a_ref[rows, :] = pltpu.roll(w, base, 1)
        scaled = pltpu.roll(scaled, base, 1)
        right = pltpu.roll(right, base, 1)
        update = lax.dot_general(
            scaled, right, (((0,), (0,)), ((), ())), precision=HIGH, preferred_element_type=F32
        )
        full_lane = lax.broadcasted_iota(jnp.int32, (N, N), 1)
        full_sub = lax.broadcasted_iota(jnp.int32, (N, N), 0)
        done = (full_sub >= base + PANEL) & (full_lane >= base) & (full_lane < base + PANEL)
        a_ref[...] = jnp.where(done, 0.0, a_ref[...]) - update
        return carry

    lax.fori_loop(0, N // PANEL, panel, 0)

    lane = lax.broadcasted_iota(jnp.int32, (N, N), 1)
    sub = lax.broadcasted_iota(jnp.int32, (N, N), 0)
    scale = 1.0 / jnp.sqrt(d_ref[...])
    scale = jnp.concatenate([scale, scale], axis=1)
    full = a_ref[...]
    factor_ref[...] = jnp.where(lane >= sub, full, 0.0) * scale
    inverse = jnp.where(lane < sub, full, jnp.where(lane == sub, 1.0, 0.0)) * scale
    basis_ref[...] = jnp.dot(
        inverse, items_ref[...], precision=HIGH, preferred_element_type=F32
    ).T


def factor_call(gram, items):
    return pl.pallas_call(
        factor_kernel,
        out_shape=(
            jax.ShapeDtypeStruct((256, 256), F32),
            jax.ShapeDtypeStruct((256, 256), F32),
        ),
        in_specs=[vmem(), vmem()],
        out_specs=(vmem(), vmem()),
        scratch_shapes=[pltpu.VMEM((N, N), F32), pltpu.VMEM((N, 128), F32)],
        compiler_params=pltpu.CompilerParams(vmem_limit_bytes=LIMIT),
        name="factor",
    )(gram, items)


def local(blocks, block_row, block_col, counts, start_block):
    tile = dense_tile(block_row[0, 0], block_col[0, 0], counts[0], blocks[0, 0])
    items, gram = krylov(start_block, tile)
    return factor_call(gram, items)


def solution(mesh):
    return jax.shard_map(
        local,
        mesh=mesh,
        in_specs=(
            P("rows", "cols", None, None, None),
            P("rows", "cols", None),
            P("rows", "cols", None),
            P("rows", "cols"),
            P(("cols", "rows"), None),
        ),
        out_specs=(P(("cols", "rows"), None), P()),
        check_vma=False,
    )
```

```python
import jax
import jax.numpy as jnp
from jax import lax
from jax.experimental import pallas as pl
from jax.experimental.pallas import tpu as pltpu
from jax.sharding import PartitionSpec as P

MESH = pl.DeviceIdType.MESH
F32 = jnp.float32
BF16 = jnp.bfloat16
HIGH = lax.Precision.HIGHEST
LIMIT = 63 * 1024 * 1024
NB = 96
GROUP = 8
STEP = 24
X, Y, Z = 4, 8, 8


def vmem():
    return pl.BlockSpec(memory_space=pltpu.VMEM)


def smem():
    return pl.BlockSpec(memory_space=pltpu.SMEM)


def remote(src, dst, send, recv, device):
    return pltpu.make_async_remote_copy(
        src_ref=src, dst_ref=dst, send_sem=send, recv_sem=recv, device_id=device, device_id_type=MESH
    )


def places():
    row = lax.axis_index("rows")
    col = lax.axis_index("cols")
    return row, col, lax.div(col, Z), lax.rem(col, Z)


def each(count, body):
    def step(i, carry):
        body(i)
        return carry

    lax.fori_loop(1, count, step, 0)


def ring(me, i, count):
    return lax.rem(me + i, count)


def greet(makers):
    barrier = pltpu.get_barrier_semaphore()
    total = 0
    for count, device in makers:
        each(
            count,
            lambda i, device=device: pl.semaphore_signal(
                barrier, inc=1, device_id=device(i), device_id_type=MESH
            ),
        )
        total += count - 1
    pl.semaphore_wait(barrier, total)


def dense_kernel(rows_ref, cols_ref, count_ref, tiles_ref, out_ref, acc_ref, pack_ref, sem):
    step = pl.program_id(0)

    @pl.when(step == 0)
    def _():
        acc_ref[...] = jnp.zeros_like(acc_ref)

    count = count_ref[0]

    def group(g, carry):
        for j in range(GROUP):
            at = g * GROUP + j
            slot = step * STEP + at
            tile = jnp.where(slot < count, tiles_ref[at].astype(F32), 0.0)
            place = cols_ref[slot]
            acc_ref[lax.div(place, 2), lax.rem(place, 2), rows_ref[slot]] += tile
        return carry

    lax.fori_loop(0, STEP // GROUP, group, 0)

    @pl.when(step == NB // STEP - 1)
    def _():
        def out_copy(q):
            return pltpu.make_async_copy(pack_ref.at[q], out_ref.at[q], sem.at[q])

        def chunk(q, carry):
            for u in range(8):
                for e in range(2):
                    pack_ref[q, u * 128 : (u + 1) * 128, e * 128 : (e + 1) * 128] = acc_ref[
                        q, e, u
                    ].astype(BF16)
            out_copy(q).start()
            return carry

        def finish(q, carry):
            out_copy(q).wait()
            return carry

        lax.fori_loop(0, 8, chunk, 0)
        lax.fori_loop(0, 8, finish, 0)


def dense_tile(rows, cols, count, tiles):
    return pl.pallas_call(
        dense_kernel,
        grid=(NB // STEP,),
        out_shape=jax.ShapeDtypeStruct((8, 1024, 256), BF16),
        in_specs=[smem(), smem(), smem(), pl.BlockSpec((STEP, 128, 128), lambda i: (i, 0, 0))],
        out_specs=pl.BlockSpec(memory_space=pl.ANY),
        scratch_shapes=[
            pltpu.VMEM((8, 2, 8, 128, 128), F32),
            pltpu.VMEM((8, 1024, 256), BF16),
            pltpu.SemaphoreType.DMA((8,)),
        ],
        compiler_params=pltpu.CompilerParams(
            dimension_semantics=("arbitrary",), vmem_limit_bytes=LIMIT
        ),
        name="dense_tile",
    )(rows, cols, count, tiles)


HALF = 128
FAR_FIRST = (4, 3, 5, 2, 6, 1, 7)


def krylov_kernel(
    own_ref, dense_ref, items_ref, gram_ref,
    tile, panel, acc, part, got1, sum1, got2, mine, wide, turned, users,
    give, near, pack, relay, far, cut, gram1, gsum1, gram2, gsum2, gram3, gsum3, gwide,
    load, send_p, recv_p, send_u, recv_u, send_a, recv_a, send_b, recv_b, send_g, recv_g,
):
    row, col, y, z = places()
    chip, core = lax.div(row, 2), lax.rem(row, 2)
    other = 1 - core
    partner = (chip * 2 + other, col)
    spots = {"r": row, "y": y, "z": z}
    low, high = pl.ds(0, HALF), pl.ds(HALF, HALF)

    def spot(i, which):
        return ring(chip, i, X) * 2 + which

    def beside(i):
        return (spot(i, core), col)

    def along(axis, i):
        target = ring(spots[axis], i, 8)
        if axis == "r":
            return target, (target, col)
        if axis == "y":
            return target, (row, target * Z + z)
        return target, (row, y * Z + target)

    order = [(i, which) for i in (0, 3, 1, 2) for which in (core, other)]
    fetches = [
        pltpu.make_async_copy(dense_ref.at[spot(*at)], tile.at[spot(*at)], load.at[n])
        for n, at in enumerate(order)
    ]
    mine_copy = pltpu.make_async_copy(own_ref, panel.at[row], load.at[8])
    mine_copy.start()
    for fetch in fetches:
        fetch.start()

    greet([(8, lambda i, axis=axis: along(axis, i)[1]) for axis in "ryz"])

    pending = []

    def push(src, dst, sends, recvs, n, device):
        copy = remote(src, dst, sends.at[n], recvs.at[n], device)
        copy.start()
        pending.append(copy)

    def landed(dst, sends, recvs, n):
        remote(dst, dst, sends.at[n], recvs.at[n], partner).wait_recv()

    def drain(keep=0):
        while len(pending) > keep:
            pending.pop(0).wait_send()

    p = (send_p, recv_p)
    done = []

    def product(i, which):
        n = len(done)
        done.append(n)
        fetches[n].wait()
        q = spot(*order[n])
        return jnp.dot(tile[q], panel[q], preferred_element_type=F32)

    push(own_ref, panel.at[row], *p, 1, beside(1))
    push(own_ref, panel.at[row], *p, 2, beside(3))
    push(own_ref, panel.at[row], *p, 0, partner)
    mine_copy.wait()
    acc[...] = product(0, core)
    landed(panel.at[spot(0, other)], *p, 0)
    acc[...] += product(0, other)
    prev, nxt, over = spot(3, core), spot(1, core), spot(2, core)
    landed(panel.at[prev], *p, 1)
    push(panel.at[prev, low], panel.at[prev, low], *p, 3, beside(1))
    landed(panel.at[nxt], *p, 2)
    push(panel.at[nxt, high], panel.at[nxt, high], *p, 4, beside(3))
    push(panel.at[prev], panel.at[prev], *p, 5, partner)
    push(panel.at[nxt], panel.at[nxt], *p, 6, partner)
    acc[...] += product(3, core)
    landed(panel.at[spot(3, other)], *p, 5)
    acc[...] += product(3, other)
    landed(panel.at[over, low], *p, 3)
    push(panel.at[over, low], panel.at[over, low], *p, 7, partner)
    landed(panel.at[over, high], *p, 4)
    push(panel.at[over, high], panel.at[over, high], *p, 8, partner)
    acc[...] += product(1, core)
    landed(panel.at[spot(1, other)], *p, 6)
    acc[...] += product(1, other)
    acc[...] += product(2, core)
    last = spot(2, other)
    landed(panel.at[last, low], *p, 7)
    landed(panel.at[last, high], *p, 8)
    total = acc[...] + product(2, other)
    for u in range(8):
        for h in range(2):
            part[h, u] = total[u * 128 : (u + 1) * 128, h * 128 : (h + 1) * 128].astype(BF16)

    def scatter(axis, source, landing, sends, recvs, i):
        target, device = along(axis, i)
        push(source(target), landing.at[spots[axis]], sends, recvs, i, device)

    def gathered(axis, landing, sends, recvs):
        for i in FAR_FIRST[::-1]:
            landed(landing.at[ring(spots[axis], 8 - i, 8)], sends, recvs, i)

    def u(stage, h):
        return send_u.at[stage, h], recv_u.at[stage, h]

    me, first, second = (y, z), ("y", "z"), ("z", "y")
    for i in FAR_FIRST:
        for h in range(2):
            scatter(first[h], lambda t, h=h: part.at[h, t], got1.at[h], *u(0, h), i)
    for h in range(2):
        got1[h, me[h]] = part[h, me[h]]
    drain(14)
    for h in range(2):
        gathered(first[h], got1.at[h], *u(0, h))
        total = got1[h, 0].astype(F32)
        for k in range(1, 8):
            total = total + got1[h, k].astype(F32)
        sum1[h] = total.reshape(8, 16, 128)
        for i in FAR_FIRST:
            scatter(second[h], lambda t, h=h: sum1.at[h, t], got2.at[h], *u(1, h), i)
        got2[h, me[1 - h]] = sum1[h, me[1 - h]]
    drain(14)
    for h in range(2):
        gathered(second[h], got2.at[h], *u(1, h))
        total = got2[h, 0]
        for k in range(1, 8):
            total = total + got2[h, k]
        mine[h] = total.astype(BF16)
        for i in FAR_FIRST:
            scatter(second[h], lambda t, h=h: mine.at[h], wide.at[h], *u(2, h), i)
        wide[h, me[1 - h]] = mine[h]
    drain(14)

    def up(h, d, src, dst):
        push(src, dst, *u(3, h), d - 1, along(first[h], 1)[1])

    def down(h, d, src, dst):
        push(src, dst, *u(3, h), d + 3, along(first[h], 7)[1])

    for h in range(2):
        gathered(second[h], wide.at[h], *u(2, h))
        turned[h] = wide[h].reshape(128, 128).astype(F32).T.astype(BF16)
        up(h, 1, turned.at[h], users.at[h, me[h]])
        down(h, 1, turned.at[h], users.at[h, me[h]])
        users[h, me[h]] = turned[h]
    drain(4)
    upper, lower = pl.ds(0, 64), pl.ds(64, 64)
    for d in range(1, 4):
        for h in range(2):
            below = users.at[h, ring(me[h], 8 - d, 8)]
            landed(below, *u(3, h), d - 1)
            if d == 3:
                below = below.at[upper]
            up(h, d + 1, below, below)
            above = users.at[h, ring(me[h], d, 8)]
            landed(above, *u(3, h), d + 3)
            if d == 3:
                above = above.at[lower]
            down(h, d + 1, above, above)
    for h in range(2):
        across = users.at[h, ring(me[h], 4, 8)]
        landed(across.at[upper], *u(3, h), 3)
        landed(across.at[lower], *u(3, h), 7)

    def term(i, which):
        left = jnp.concatenate(
            [jnp.concatenate([users[h, k] for k in range(8)], axis=1) for h in range(2)], axis=0
        )
        return jnp.dot(left, tile[spot(i, which)], preferred_element_type=F32)

    a, b = (send_a, recv_a), (send_b, recv_b)

    def lend(i):
        give[i] = term(i, other)
        push(give.at[i], near.at[i], *a, i, partner)

    lend(2)
    lend(1)
    value = term(2, core)
    landed(near.at[2], *a, 2)
    pack[2] = (value + near[2]).astype(BF16)
    push(pack.at[2, low], relay.at[0], *b, 0, beside(1))
    push(pack.at[2, high], relay.at[1], *b, 1, beside(3))
    lend(3)
    value = term(1, core)
    landed(near.at[1], *a, 1)
    near[1] = value + near[1]
    pack[1, HALF:] = near[1, HALF:].astype(BF16)
    push(pack.at[1, high], far.at[0, high], *b, 2, beside(1))
    lend(0)
    value = term(3, core)
    landed(near.at[3], *a, 3)
    near[3] = value + near[3]
    pack[3, :HALF] = near[3, :HALF].astype(BF16)
    push(pack.at[3, low], far.at[1, low], *b, 3, beside(3))
    landed(relay.at[0], *b, 0)
    pack[1, :HALF] = (near[1, :HALF] + relay[0].astype(F32)).astype(BF16)
    push(pack.at[1, low], far.at[0, low], *b, 4, beside(1))
    landed(relay.at[1], *b, 1)
    pack[3, HALF:] = (near[3, HALF:] + relay[1].astype(F32)).astype(BF16)
    push(pack.at[3, high], far.at[1, high], *b, 5, beside(3))
    value = term(0, core)
    landed(near.at[0], *a, 0)
    near[0] = value + near[0]
    drain(2)
    landed(far.at[0, high], *b, 2)
    landed(far.at[1, low], *b, 3)
    landed(far.at[0, low], *b, 4)
    landed(far.at[1, high], *b, 5)
    items = near[0] + far[0].astype(F32) + far[1].astype(F32)
    items_ref[...] = items

    gram = lax.dot_general(
        items, items, (((1,), (1,)), ((), ())), precision=HIGH, preferred_element_type=F32
    )
    for k in range(16):
        for c in range(2):
            cut[k // 2, (k % 2) * 2 + c] = gram[
                16 * k : 16 * k + 16, 128 * c : 128 * c + 128
            ].astype(BF16)

    def g(n):
        return send_g.at[n], recv_g.at[n]

    def move(n, axis, source, landing):
        for i in FAR_FIRST:
            scatter(axis, source, landing, *g(n), i)
        landing[spots[axis]] = source(spots[axis])[...]
        drain(7)
        gathered(axis, landing, *g(n))

    def summed(got):
        total = got[0]
        for k in range(1, 8):
            total = total + got[k]
        return total

    move(0, "r", lambda t: cut.at[t], gram1)
    total = gram1[0].astype(F32)
    for k in range(1, 8):
        total = total + gram1[k].astype(F32)
    gsum1[...] = total.reshape(8, 8, 128)
    move(1, "y", lambda t: gsum1.at[t], gram2)
    gsum2[...] = summed(gram2)
    move(2, "z", lambda t: gsum2, gram3)
    gsum3[...] = summed(gram3)
    move(3, "y", lambda t: gsum3, gwide)
    for i in (2, 1, 3):
        push(gwide, gram_ref.at[row], *g(4), i, beside(i))
    push(gwide, gram_ref.at[row], *g(4), 0, partner)
    gram_ref[row] = gwide[...]
    drain(4)
    for i in (3, 1, 2):
        block = gram_ref.at[spot(4 - i, core)]
        landed(block, *g(4), i)
        push(block, block, *g(4), 4 + i, partner)
    landed(gram_ref.at[spot(0, other)], *g(4), 0)
    for i in (3, 1, 2):
        landed(gram_ref.at[spot(4 - i, other)], *g(4), 4 + i)
    drain()


def krylov(own, tile):
    cell = (8, 128)
    dma = pltpu.SemaphoreType.DMA
    pairs = [(9,), (4, 2, 8), (X,), (6,), (5, 8)]
    return pl.pallas_call(
        krylov_kernel,
        out_shape=(
            jax.ShapeDtypeStruct((256, 256), F32),
            jax.ShapeDtypeStruct((8, 8) + cell, F32),
        ),
        in_specs=[pl.BlockSpec(memory_space=pl.ANY), pl.BlockSpec(memory_space=pl.ANY)],
        out_specs=(vmem(), vmem()),
        scratch_shapes=[
            pltpu.VMEM((8, 1024, 256), BF16),
            pltpu.VMEM((8, 256, 256), BF16),
            pltpu.VMEM((1024, 256), F32),
            pltpu.VMEM((2, 8, 128, 128), BF16),
            pltpu.VMEM((2, 8, 128, 128), BF16),
            pltpu.VMEM((2, 8, 16, 128), F32),
            pltpu.VMEM((2, 8, 16, 128), F32),
            pltpu.VMEM((2, 16, 128), BF16),
            pltpu.VMEM((2, 8, 16, 128), BF16),
            pltpu.VMEM((2, 128, 128), BF16),
            pltpu.VMEM((2, 8, 128, 128), BF16),
            pltpu.VMEM((X, 256, 256), F32),
            pltpu.VMEM((X, 256, 256), F32),
            pltpu.VMEM((X, 256, 256), BF16),
            pltpu.VMEM((2, HALF, 256), BF16),
            pltpu.VMEM((2, 256, 256), BF16),
            pltpu.VMEM((8, 4, 16, 128), BF16),
            pltpu.VMEM((8, 4, 16, 128), BF16),
            pltpu.VMEM((8,) + cell, F32),
            pltpu.VMEM((8,) + cell, F32),
            pltpu.VMEM(cell, F32),
            pltpu.VMEM((8,) + cell, F32),
            pltpu.VMEM(cell, F32),
            pltpu.VMEM((8,) + cell, F32),
            dma((9,)),
        ]
        + [dma(shape) for shape in pairs for _ in range(2)],
        compiler_params=pltpu.CompilerParams(
            collective_id=0, has_side_effects=True, vmem_limit_bytes=LIMIT
        ),
        name="krylov",
    )(own, tile)


PANEL = 32
N = 256


def factor_kernel(gram_ref, items_ref, basis_ref, factor_ref, a_ref, d_ref):
    for k in range(32):
        for c in range(2):
            a_ref[8 * k : 8 * k + 8, 128 * c : 128 * c + 128] = gram_ref[
                k // 4, (k // 2 % 2) * 4 + c * 2 + k % 2
            ]

    def panel(q, carry):
        base = q * PANEL
        rows = pl.ds(pl.multiple_of(base, PANEL), PANEL)
        w = pltpu.roll(a_ref[rows, :], lax.rem(N - base, N), 1)
        d = jnp.zeros((PANEL, 128), F32)
        for t in range(PANEL // 8):
            low = 8 * t
            part = w[low:, :]
            size = PANEL - low
            lane = lax.broadcasted_iota(jnp.int32, (size, N), 1)
            sub = lax.broadcasted_iota(jnp.int32, (size, N), 0) + low
            sub1 = sub[:, :128]
            columns = [
                jnp.broadcast_to(part[:, low + b : low + b + 1], (size, 128)) for b in range(8)
            ]
            d_part = d[low:, :]
            for a in range(0, 8, 2):
                r = low + a
                one, two = columns[a], columns[a + 1]
                p11, p12 = one[a : a + 1, :], two[a : a + 1, :]
                p21, p22 = one[a + 1 : a + 2, :], two[a + 1 : a + 2, :]
                inv1 = 1.0 / p11
                inv2 = p11 * (1.0 / (p11 * p22 - p21 * p12))
                ratio = p21 * inv1
                m1 = jnp.where(sub1 > r, one * inv1, 0.0)
                m2 = jnp.where(sub1 > r + 1, (two - m1 * p12) * inv2, 0.0)
                for b in range(a + 2, 8):
                    top = columns[b][a : a + 1, :]
                    next_top = columns[b][a + 1 : a + 2, :] - ratio * top
                    columns[b] = columns[b] - m1 * top - m2 * next_top
                lane1 = lane[:1]
                line1 = jnp.where(lane1 == r, 1.0, part[a : a + 1, :])
                ratio2 = jnp.concatenate([ratio, ratio], axis=1)
                line2 = jnp.where(lane1 == r, 0.0, part[a + 1 : a + 2, :]) - ratio2 * line1
                line1 = jnp.where(lane1 == r + 1, 0.0, line1)
                line2 = jnp.where(lane1 == r + 1, 1.0, line2)
                gone = ((lane == r) & (sub > r)) | ((lane == r + 1) & (sub > r + 1))
                part = (
                    jnp.where(gone, 0.0, part)
                    - jnp.concatenate([m1, m1], axis=1) * line1
                    - jnp.concatenate([m2, m2], axis=1) * line2
                )
                d_part = jnp.where(sub1 == r, p11, d_part)
                d_part = jnp.where(sub1 == r + 1, p22 - ratio * p12, d_part)
            w = part if low == 0 else jnp.concatenate([w[:low], part], axis=0)
            d = d_part if low == 0 else jnp.concatenate([d[:low], d_part], axis=0)
        d_ref[rows, :] = d
        lane = lax.broadcasted_iota(jnp.int32, (PANEL, N), 1)
        sub = lax.broadcasted_iota(jnp.int32, (PANEL, N), 0)
        d2 = jnp.concatenate([d, d], axis=1)
        ahead = (lane >= PANEL) & (lane < N - base)
        scaled = jnp.where(ahead, w / d2, 0.0)
        right = jnp.where((lane < PANEL) & (lane >= sub), jnp.where(lane == sub, 1.0, 0.0), w)
        a_ref[rows, :] = pltpu.roll(w, base, 1)
        scaled = pltpu.roll(scaled, base, 1)
        right = pltpu.roll(right, base, 1)
        update = lax.dot_general(
            scaled, right, (((0,), (0,)), ((), ())), precision=HIGH, preferred_element_type=F32
        )
        full_lane = lax.broadcasted_iota(jnp.int32, (N, N), 1)
        full_sub = lax.broadcasted_iota(jnp.int32, (N, N), 0)
        done = (full_sub >= base + PANEL) & (full_lane >= base) & (full_lane < base + PANEL)
        a_ref[...] = jnp.where(done, 0.0, a_ref[...]) - update
        return carry

    lax.fori_loop(0, N // PANEL, panel, 0)

    lane = lax.broadcasted_iota(jnp.int32, (N, N), 1)
    sub = lax.broadcasted_iota(jnp.int32, (N, N), 0)
    pivots = d_ref[...]
    scale = 1.0 / jnp.sqrt(pivots)
    scale = jnp.concatenate([scale, scale], axis=1)
    full = jnp.where(lane == sub, jnp.concatenate([pivots, pivots], axis=1), a_ref[...])
    factor_ref[...] = jnp.where(lane >= sub, full, 0.0) * scale
    inverse = jnp.where(lane < sub, full, jnp.where(lane == sub, 1.0, 0.0)) * scale
    basis_ref[...] = jnp.dot(
        inverse, items_ref[...], precision=HIGH, preferred_element_type=F32
    ).T


def factor_call(gram, items):
    return pl.pallas_call(
        factor_kernel,
        out_shape=(
            jax.ShapeDtypeStruct((256, 256), F32),
            jax.ShapeDtypeStruct((256, 256), F32),
        ),
        in_specs=[vmem(), vmem()],
        out_specs=(vmem(), vmem()),
        scratch_shapes=[pltpu.VMEM((N, N), F32), pltpu.VMEM((N, 128), F32)],
        compiler_params=pltpu.CompilerParams(vmem_limit_bytes=LIMIT),
        name="factor",
    )(gram, items)


def local(blocks, block_row, block_col, counts, start_block):
    tile = dense_tile(block_row[0, 0], block_col[0, 0], counts[0], blocks[0, 0])
    items, gram = krylov(start_block, tile)
    return factor_call(gram, items)


def solution(mesh):
    return jax.shard_map(
        local,
        mesh=mesh,
        in_specs=(
            P("rows", "cols", None, None, None),
            P("rows", "cols", None),
            P("rows", "cols", None),
            P("rows", "cols"),
            P(("cols", "rows"), None),
        ),
        out_specs=(P(("cols", "rows"), None), P()),
        check_vma=False,
    )
```

```python
import jax
import jax.numpy as jnp
from jax import lax
from jax.experimental import pallas as pl
from jax.experimental.pallas import tpu as pltpu
from jax.sharding import PartitionSpec as P

MESH = pl.DeviceIdType.MESH
F32 = jnp.float32
BF16 = jnp.bfloat16
HIGH = lax.Precision.HIGHEST
LIMIT = 63 * 1024 * 1024
ROOM = 53 * 1024 * 1024
NB = 96
GROUP = 8
STEP = 24
X, Y, Z = 4, 8, 8


def vmem():
    return pl.BlockSpec(memory_space=pltpu.VMEM)


def smem():
    return pl.BlockSpec(memory_space=pltpu.SMEM)


def remote(src, dst, send, recv, device):
    return pltpu.make_async_remote_copy(
        src_ref=src, dst_ref=dst, send_sem=send, recv_sem=recv, device_id=device, device_id_type=MESH
    )


def places():
    row = lax.axis_index("rows")
    col = lax.axis_index("cols")
    return row, col, lax.div(col, Z), lax.rem(col, Z)


def each(count, body):
    def step(i, carry):
        body(i)
        return carry

    lax.fori_loop(1, count, step, 0)


def ring(me, i, count):
    return lax.rem(me + i, count)


def greet(makers):
    barrier = pltpu.get_barrier_semaphore()
    total = 0
    for count, device in makers:
        each(
            count,
            lambda i, device=device: pl.semaphore_signal(
                barrier, inc=1, device_id=device(i), device_id_type=MESH
            ),
        )
        total += count - 1
    pl.semaphore_wait(barrier, total)


def dense_kernel(rows_ref, cols_ref, count_ref, tiles_ref, out_ref, acc_ref, pack_ref, sem):
    step = pl.program_id(0)

    @pl.when(step == 0)
    def _():
        acc_ref[...] = jnp.zeros_like(acc_ref)

    count = count_ref[0]

    def group(g, carry):
        for j in range(0, GROUP, 2):
            spots, tiles = [], []
            for k in range(2):
                at = g * GROUP + j + k
                slot = step * STEP + at
                col = cols_ref[slot]
                spots.append((lax.div(col, 2), lax.rem(col, 2), rows_ref[slot]))
                tiles.append(jnp.where(slot < count, tiles_ref[at].astype(F32), 0.0))
            same = (spots[0][0] == spots[1][0]) & (spots[0][1] == spots[1][1])
            same = same & (spots[0][2] == spots[1][2])
            one = acc_ref[spots[0]] + tiles[0]
            two = jnp.where(same, one, acc_ref[spots[1]]) + tiles[1]
            acc_ref[spots[0]] = one
            acc_ref[spots[1]] = two
        return carry

    lax.fori_loop(0, STEP // GROUP, group, 0)

    @pl.when(step == NB // STEP - 1)
    def _():
        def out_copy(q):
            return pltpu.make_async_copy(pack_ref.at[q], out_ref.at[q], sem.at[q])

        def chunk(q, carry):
            def block(u, inner):
                rows = pl.ds(pl.multiple_of(u * 128, 128), 128)
                for e in range(2):
                    pack_ref[q, rows, e * 128 : (e + 1) * 128] = acc_ref[q, e, u].astype(BF16)
                return inner

            lax.fori_loop(0, 8, block, 0)
            out_copy(q).start()
            return carry

        def finish(q, carry):
            out_copy(q).wait()
            return carry

        lax.fori_loop(0, 8, chunk, 0)
        lax.fori_loop(0, 8, finish, 0)


def dense_tile(rows, cols, count, tiles):
    return pl.pallas_call(
        dense_kernel,
        grid=(NB // STEP,),
        out_shape=jax.ShapeDtypeStruct((8, 1024, 256), BF16),
        in_specs=[smem(), smem(), smem(), pl.BlockSpec((STEP, 128, 128), lambda i: (i, 0, 0))],
        out_specs=pl.BlockSpec(memory_space=pl.ANY),
        scratch_shapes=[
            pltpu.VMEM((8, 2, 8, 128, 128), F32),
            pltpu.VMEM((8, 1024, 256), BF16),
            pltpu.SemaphoreType.DMA((8,)),
        ],
        compiler_params=pltpu.CompilerParams(
            dimension_semantics=("arbitrary",), vmem_limit_bytes=LIMIT
        ),
        name="dense_tile",
    )(rows, cols, count, tiles)


HALF = 128
def table(digits):
    return sum(digit * 8**n for n, digit in enumerate(digits))


FORWARD = (0, 1, 6, 7, 2, 3, 4, 5)
BACKWARD = (5, 3, 4, 7, 2, 1, 6, 0)


def krylov_kernel(
    own_ref, dense_ref, items_ref, gram_ref,
    tile, panel, acc, part, got1, sum1, got2, mine, wide, turned, users,
    value, near, pack, relay, far, cut, gram1, gsum1, gram2, gsum2, gram3, gsum3, gwide,
    load, send_p, recv_p, send_u, recv_u, send_a, recv_a, send_b, recv_b, send_g, recv_g,
):
    row, col, y, z = places()
    chip, core = lax.div(row, 2), lax.rem(row, 2)
    other = 1 - core
    partner = (chip * 2 + other, col)
    spots = {"r": row, "y": y, "z": z}
    low, high = pl.ds(0, HALF), pl.ds(HALF, HALF)

    def spot(i, which):
        return ring(chip, i, X) * 2 + which

    def place(digit):
        return spot(lax.div(digit, 2), lax.rem(core + lax.rem(digit, 2), 2))

    def beside(i):
        return (spot(i, core), col)

    def along(axis, i):
        target = ring(spots[axis], i, 8)
        if axis == "r":
            return target, (target, col)
        if axis == "y":
            return target, (row, target * Z + z)
        return target, (row, y * Z + target)

    def fetch(digit):
        q = place(digit)
        return pltpu.make_async_copy(dense_ref.at[q], tile.at[q], load.at[digit])

    def fetch_next(n, digits):
        fetch(lax.rem(digits, 8)).start()
        return lax.div(digits, 8)

    mine_copy = pltpu.make_async_copy(own_ref, panel.at[row], load.at[8])
    mine_copy.start()
    lax.fori_loop(0, 8, fetch_next, table(FORWARD))

    greet([(8, lambda i, axis=axis: along(axis, i)[1]) for axis in "ryz"])

    def landed(dst, sends, recvs, n):
        remote(dst, dst, sends.at[n], recvs.at[n], partner).wait_recv()

    def far_first(body):
        def step(n, carry):
            body(4 + lax.div(n + 1, 2) * (1 - 2 * lax.rem(n, 2)))
            return carry

        lax.fori_loop(0, 7, step, 0)

    prev, nxt, over = spot(3, core), spot(1, core), spot(2, core)
    last = spot(2, other)
    p = (send_p, recv_p)
    hops = [
        (own_ref, panel.at[row], partner),
        (own_ref, panel.at[row], beside(1)),
        (own_ref, panel.at[row], beside(3)),
        (panel.at[prev, low], panel.at[prev, low], beside(1)),
        (panel.at[nxt, high], panel.at[nxt, high], beside(3)),
        (panel.at[prev], panel.at[prev], partner),
        (panel.at[nxt], panel.at[nxt], partner),
        (panel.at[over, low], panel.at[over, low], partner),
        (panel.at[over, high], panel.at[over, high], partner),
    ]

    def hop(n):
        src, dst, device = hops[n]
        return remote(src, dst, send_p.at[n], recv_p.at[n], device)

    for n in (1, 2, 0):
        hop(n).start()
    acc[...] = jnp.zeros_like(acc)
    mine_copy.wait()

    def multiply(n, digits):
        digit = lax.rem(digits, 8)
        fetch(digit).wait()

        @pl.when(n == 1)
        def _():
            landed(panel.at[spot(0, other)], *p, 0)

        @pl.when(n == 2)
        def _():
            landed(panel.at[prev], *p, 1)
            hop(3).start()
            landed(panel.at[nxt], *p, 2)
            hop(4).start()
            hop(5).start()
            hop(6).start()

        @pl.when(n == 3)
        def _():
            landed(panel.at[spot(3, other)], *p, 5)

        @pl.when(n == 4)
        def _():
            landed(panel.at[over, low], *p, 3)
            hop(7).start()
            landed(panel.at[over, high], *p, 4)
            hop(8).start()

        @pl.when(n == 5)
        def _():
            landed(panel.at[spot(1, other)], *p, 6)

        @pl.when(n == 7)
        def _():
            landed(panel.at[last, low], *p, 7)
            landed(panel.at[last, high], *p, 8)

        q = place(digit)
        acc[...] += jnp.dot(tile[q], panel[q], preferred_element_type=F32)
        return lax.div(digits, 8)

    lax.fori_loop(0, 8, multiply, table(FORWARD))

    def walk(axis, source, landing, send, recv, what):
        if what == "start":
            def step(i):
                target, device = along(axis, i)
                remote(source(target), landing.at[spots[axis]], send, recv, device).start()

            far_first(step)
        else:
            seven = landing.at[pl.ds(0, 7)]
            whole = remote(seven, seven, send, recv, partner)
            if what == "arrive":
                whole.wait_recv()
            else:
                whole.wait_send()

    def u(stage, h):
        return send_u.at[stage, h], recv_u.at[stage, h]

    me, first, second = (y, z), ("y", "z"), ("z", "y")
    jobs = [
        [(first[h], lambda t, h=h: part.at[h, t], got1.at[h]) for h in range(2)],
        [(second[h], lambda t, h=h: sum1.at[h, t], got2.at[h]) for h in range(2)],
        [(second[h], lambda t, h=h: mine.at[h], wide.at[h]) for h in range(2)],
        [(first[h], lambda t, h=h: turned.at[h], users.at[h]) for h in range(2)],
    ]

    def users_step(stage, h, what):
        walk(*jobs[stage][h], *u(stage, h), what)

    for h in range(2):
        def narrow(k, carry, h=h):
            rows = pl.ds(pl.multiple_of(k * 128, 128), 128)
            part[h, k] = acc[rows, h * 128 : (h + 1) * 128].astype(BF16)
            return carry

        lax.fori_loop(0, 8, narrow, 0)
        users_step(0, h, "start")
    for h in range(2):
        got1[h, me[h]] = part[h, me[h]]
    for n in range(9):
        hop(n).wait_send()
    for h in range(2):
        users_step(0, h, "arrive")
        total = got1[h, 0].astype(F32)
        for k in range(1, 8):
            total = total + got1[h, k].astype(F32)
        sum1[h] = total.reshape(8, 16, 128)
        users_step(1, h, "start")
        got2[h, me[1 - h]] = sum1[h, me[1 - h]]
    for h in range(2):
        users_step(0, h, "leave")
    for h in range(2):
        users_step(1, h, "arrive")
        total = got2[h, 0]
        for k in range(1, 8):
            total = total + got2[h, k]
        mine[h] = total.astype(BF16)
        users_step(2, h, "start")
        wide[h, me[1 - h]] = mine[h]
    for h in range(2):
        users_step(1, h, "leave")

    for h in range(2):
        users_step(2, h, "arrive")
        turned[h] = wide[h].reshape(128, 128).astype(F32).T.astype(BF16)
        users_step(3, h, "start")
        users[h, me[h]] = turned[h]
    for h in range(2):
        users_step(2, h, "leave")
    for h in range(2):
        users_step(3, h, "arrive")

    a, b = (send_a, recv_a), (send_b, recv_b)

    def lend(i):
        return remote(value.at[2 * i + 1], near.at[i], send_a.at[i], recv_a.at[i], partner)

    moves = [
        (pack.at[2, low], relay.at[0], beside(1)),
        (pack.at[2, high], relay.at[1], beside(3)),
        (pack.at[1, high], far.at[0, high], beside(1)),
        (pack.at[3, low], far.at[1, low], beside(3)),
        (pack.at[1, low], far.at[0, low], beside(1)),
        (pack.at[3, high], far.at[1, high], beside(3)),
    ]

    def pass_on(n):
        src, dst, device = moves[n]
        return remote(src, dst, send_b.at[n], recv_b.at[n], device)

    def meet(i):
        landed(near.at[i], *a, i)
        near[i] = value[2 * i] + near[i]

    def transposed(n, digits):
        digit = lax.rem(digits, 8)
        left = jnp.concatenate(
            [jnp.concatenate([users[h, k] for k in range(8)], axis=1) for h in range(2)], axis=0
        )
        value[digit] = jnp.dot(left, tile[place(digit)], preferred_element_type=F32)
        for step, i in ((0, 2), (1, 1), (3, 3), (5, 0)):
            @pl.when(n == step)
            def _(i=i):
                lend(i).start()

        @pl.when(n == 2)
        def _():
            meet(2)
            pack[2] = near[2].astype(BF16)
            pass_on(0).start()
            pass_on(1).start()

        @pl.when(n == 4)
        def _():
            meet(1)
            pack[1, HALF:] = near[1, HALF:].astype(BF16)
            pass_on(2).start()

        @pl.when(n == 6)
        def _():
            meet(3)
            pack[3, :HALF] = near[3, :HALF].astype(BF16)
            pass_on(3).start()

        return lax.div(digits, 8)

    lax.fori_loop(0, 8, transposed, table(BACKWARD))
    landed(relay.at[0], *b, 0)
    pack[1, :HALF] = (near[1, :HALF] + relay[0].astype(F32)).astype(BF16)
    pass_on(4).start()
    landed(relay.at[1], *b, 1)
    pack[3, HALF:] = (near[3, HALF:] + relay[1].astype(F32)).astype(BF16)
    pass_on(5).start()
    meet(0)

    for h in range(2):
        users_step(3, h, "leave")
    for i in range(X):
        lend(i).wait_send()
    landed(far.at[0, high], *b, 2)
    landed(far.at[1, low], *b, 3)
    landed(far.at[0, low], *b, 4)
    landed(far.at[1, high], *b, 5)
    items = near[0] + far[0].astype(F32) + far[1].astype(F32)
    items_ref[...] = items

    gram = lax.dot_general(
        items, items, (((1,), (1,)), ((), ())), precision=HIGH, preferred_element_type=F32
    )
    for k in range(16):
        for c in range(2):
            cut[k // 2, (k % 2) * 2 + c] = gram[
                16 * k : 16 * k + 16, 128 * c : 128 * c + 128
            ].astype(BF16)

    def g(n):
        return send_g.at[n], recv_g.at[n]

    spread = [
        ("r", lambda t: cut.at[t], gram1),
        ("y", lambda t: gsum1.at[t], gram2),
        ("z", lambda t: gsum2, gram3),
        ("y", lambda t: gsum3, gwide),
        ("r", lambda t: gwide, gram_ref),
    ]

    def move(n):
        axis, source, landing = spread[n]
        walk(*spread[n], *g(n), "start")
        landing[spots[axis]] = source(spots[axis])[...]
        if n:
            walk(*spread[n - 1], *g(n - 1), "leave")
        else:
            for k in range(6):
                pass_on(k).wait_send()
        walk(*spread[n], *g(n), "arrive")

    def summed(got):
        total = got[0].astype(F32)
        for k in range(1, 8):
            total = total + got[k].astype(F32)
        return total

    move(0)
    gsum1[...] = summed(gram1).reshape(8, 8, 128)
    move(1)
    gsum2[...] = summed(gram2)
    move(2)
    gsum3[...] = summed(gram3)
    move(3)

    move(4)
    walk(*spread[4], *g(4), "leave")


def krylov(own, tile):
    cell = (8, 128)
    dma = pltpu.SemaphoreType.DMA
    pairs = [(9,), (4, 2), (X,), (6,), (5,)]
    return pl.pallas_call(
        krylov_kernel,
        out_shape=(
            jax.ShapeDtypeStruct((256, 256), F32),
            jax.ShapeDtypeStruct((8, 8) + cell, F32),
        ),
        in_specs=[pl.BlockSpec(memory_space=pl.ANY), pl.BlockSpec(memory_space=pl.ANY)],
        out_specs=(vmem(), vmem()),
        scratch_shapes=[
            pltpu.VMEM((8, 1024, 256), BF16),
            pltpu.VMEM((8, 256, 256), BF16),
            pltpu.VMEM((1024, 256), F32),
            pltpu.VMEM((2, 8, 128, 128), BF16),
            pltpu.VMEM((2, 8, 128, 128), BF16),
            pltpu.VMEM((2, 8, 16, 128), F32),
            pltpu.VMEM((2, 8, 16, 128), F32),
            pltpu.VMEM((2, 16, 128), BF16),
            pltpu.VMEM((2, 8, 16, 128), BF16),
            pltpu.VMEM((2, 128, 128), BF16),
            pltpu.VMEM((2, 8, 128, 128), BF16),
            pltpu.VMEM((8, 256, 256), F32),
            pltpu.VMEM((X, 256, 256), F32),
            pltpu.VMEM((X, 256, 256), BF16),
            pltpu.VMEM((2, HALF, 256), BF16),
            pltpu.VMEM((2, 256, 256), BF16),
            pltpu.VMEM((8, 4, 16, 128), BF16),
            pltpu.VMEM((8, 4, 16, 128), BF16),
            pltpu.VMEM((8,) + cell, F32),
            pltpu.VMEM((8,) + cell, F32),
            pltpu.VMEM(cell, F32),
            pltpu.VMEM((8,) + cell, F32),
            pltpu.VMEM(cell, F32),
            pltpu.VMEM((8,) + cell, F32),
            dma((9,)),
        ]
        + [dma(shape) for shape in pairs for _ in range(2)],
        compiler_params=pltpu.CompilerParams(
            collective_id=0, has_side_effects=True, vmem_limit_bytes=ROOM
        ),
        name="krylov",
    )(own, tile)


PANEL = 32
N = 256


def factor_kernel(gram_ref, items_ref, basis_ref, factor_ref, a_ref, d_ref):
    for k in range(32):
        for c in range(2):
            a_ref[8 * k : 8 * k + 8, 128 * c : 128 * c + 128] = gram_ref[
                k // 4, (k // 2 % 2) * 4 + c * 2 + k % 2
            ]

    def panel(q, carry):
        base = q * PANEL
        rows = pl.ds(pl.multiple_of(base, PANEL), PANEL)
        w = pltpu.roll(a_ref[rows, :], lax.rem(N - base, N), 1)
        d = jnp.zeros((PANEL, 128), F32)
        for t in range(PANEL // 8):
            low = 8 * t
            part = w[low:, :]
            size = PANEL - low
            lane = lax.broadcasted_iota(jnp.int32, (size, N), 1)
            sub = lax.broadcasted_iota(jnp.int32, (size, N), 0) + low
            sub1 = sub[:, :128]
            columns = [
                jnp.broadcast_to(part[:, low + b : low + b + 1], (size, 128)) for b in range(8)
            ]
            d_part = d[low:, :]
            for a in range(0, 8, 2):
                r = low + a
                one, two = columns[a], columns[a + 1]
                p11, p12 = one[a : a + 1, :], two[a : a + 1, :]
                p21, p22 = one[a + 1 : a + 2, :], two[a + 1 : a + 2, :]
                inv1 = 1.0 / p11
                inv2 = p11 * (1.0 / (p11 * p22 - p21 * p12))
                ratio = p21 * inv1
                m1 = jnp.where(sub1 > r, one * inv1, 0.0)
                m2 = jnp.where(sub1 > r + 1, (two - m1 * p12) * inv2, 0.0)
                for b in range(a + 2, 8):
                    top = columns[b][a : a + 1, :]
                    next_top = columns[b][a + 1 : a + 2, :] - ratio * top
                    columns[b] = columns[b] - m1 * top - m2 * next_top
                lane1 = lane[:1]
                line1 = jnp.where(lane1 == r, 1.0, part[a : a + 1, :])
                ratio2 = jnp.concatenate([ratio, ratio], axis=1)
                line2 = jnp.where(lane1 == r, 0.0, part[a + 1 : a + 2, :]) - ratio2 * line1
                line1 = jnp.where(lane1 == r + 1, 0.0, line1)
                line2 = jnp.where(lane1 == r + 1, 1.0, line2)
                gone = ((lane == r) & (sub > r)) | ((lane == r + 1) & (sub > r + 1))
                part = (
                    jnp.where(gone, 0.0, part)
                    - jnp.concatenate([m1, m1], axis=1) * line1
                    - jnp.concatenate([m2, m2], axis=1) * line2
                )
                d_part = jnp.where(sub1 == r, p11, d_part)
                d_part = jnp.where(sub1 == r + 1, p22 - ratio * p12, d_part)
            w = part if low == 0 else jnp.concatenate([w[:low], part], axis=0)
            d = d_part if low == 0 else jnp.concatenate([d[:low], d_part], axis=0)
        d_ref[rows, :] = d
        lane = lax.broadcasted_iota(jnp.int32, (PANEL, N), 1)
        sub = lax.broadcasted_iota(jnp.int32, (PANEL, N), 0)
        d2 = jnp.concatenate([d, d], axis=1)
        ahead = (lane >= PANEL) & (lane < N - base)
        scaled = jnp.where(ahead, w / d2, 0.0)
        right = jnp.where((lane < PANEL) & (lane >= sub), jnp.where(lane == sub, 1.0, 0.0), w)
        a_ref[rows, :] = pltpu.roll(w, base, 1)
        scaled = pltpu.roll(scaled, base, 1)
        right = pltpu.roll(right, base, 1)
        update = lax.dot_general(
            scaled, right, (((0,), (0,)), ((), ())), precision=HIGH, preferred_element_type=F32
        )
        full_lane = lax.broadcasted_iota(jnp.int32, (N, N), 1)
        full_sub = lax.broadcasted_iota(jnp.int32, (N, N), 0)
        done = (full_sub >= base + PANEL) & (full_lane >= base) & (full_lane < base + PANEL)
        a_ref[...] = jnp.where(done, 0.0, a_ref[...]) - update
        return carry

    lax.fori_loop(0, N // PANEL, panel, 0)

    lane = lax.broadcasted_iota(jnp.int32, (N, N), 1)
    sub = lax.broadcasted_iota(jnp.int32, (N, N), 0)
    pivots = d_ref[...]
    scale = 1.0 / jnp.sqrt(pivots)
    scale = jnp.concatenate([scale, scale], axis=1)
    full = jnp.where(lane == sub, jnp.concatenate([pivots, pivots], axis=1), a_ref[...])
    factor_ref[...] = jnp.where(lane >= sub, full, 0.0) * scale
    inverse = jnp.where(lane < sub, full, jnp.where(lane == sub, 1.0, 0.0)) * scale
    basis_ref[...] = jnp.dot(
        inverse, items_ref[...], precision=HIGH, preferred_element_type=F32
    ).T


def factor_call(gram, items):
    return pl.pallas_call(
        factor_kernel,
        out_shape=(
            jax.ShapeDtypeStruct((256, 256), F32),
            jax.ShapeDtypeStruct((256, 256), F32),
        ),
        in_specs=[vmem(), vmem()],
        out_specs=(vmem(), vmem()),
        scratch_shapes=[pltpu.VMEM((N, N), F32), pltpu.VMEM((N, 128), F32)],
        compiler_params=pltpu.CompilerParams(vmem_limit_bytes=ROOM),
        name="factor",
    )(gram, items)


def local(blocks, block_row, block_col, counts, start_block):
    tile = dense_tile(block_row[0, 0], block_col[0, 0], counts[0], blocks[0, 0])
    items, gram = krylov(start_block, tile)
    return factor_call(gram, items)


def solution(mesh):
    return jax.shard_map(
        local,
        mesh=mesh,
        in_specs=(
            P("rows", "cols", None, None, None),
            P("rows", "cols", None),
            P("rows", "cols", None),
            P("rows", "cols"),
            P(("cols", "rows"), None),
        ),
        out_specs=(P(("cols", "rows"), None), P()),
        check_vma=False,
    )
```

```python
import jax
import jax.numpy as jnp
from jax import lax
from jax.experimental import pallas as pl
from jax.experimental.pallas import tpu as pltpu
from jax.sharding import PartitionSpec as P

MESH = pl.DeviceIdType.MESH
F32 = jnp.float32
BF16 = jnp.bfloat16
HIGH = lax.Precision.HIGHEST
LIMIT = 63 * 1024 * 1024
ROOM = 53 * 1024 * 1024
NB = 96
GROUP = 8
STEP = 24
X, Y, Z = 4, 8, 8


def vmem():
    return pl.BlockSpec(memory_space=pltpu.VMEM)


def smem():
    return pl.BlockSpec(memory_space=pltpu.SMEM)


def remote(src, dst, send, recv, device):
    return pltpu.make_async_remote_copy(
        src_ref=src, dst_ref=dst, send_sem=send, recv_sem=recv, device_id=device, device_id_type=MESH
    )


def places():
    row = lax.axis_index("rows")
    col = lax.axis_index("cols")
    return row, col, lax.div(col, Z), lax.rem(col, Z)


def each(count, body):
    def step(i, carry):
        body(i)
        return carry

    lax.fori_loop(1, count, step, 0)


def ring(me, i, count):
    return lax.rem(me + i, count)


def greet(makers):
    barrier = pltpu.get_barrier_semaphore()
    total = 0
    for count, device in makers:
        each(
            count,
            lambda i, device=device: pl.semaphore_signal(
                barrier, inc=1, device_id=device(i), device_id_type=MESH
            ),
        )
        total += count - 1
    pl.semaphore_wait(barrier, total)


def dense_kernel(rows_ref, cols_ref, count_ref, tiles_ref, out_ref, acc_ref, pack_ref, seen_ref, sem):
    step = pl.program_id(0)

    @pl.when(step == 0)
    def _():
        def clear(k, carry):
            seen_ref[k] = 0
            return carry

        lax.fori_loop(0, 128, clear, 0)

    count = count_ref[0]

    def group(g, carry):
        for j in range(GROUP):
            at = g * GROUP + j
            slot = step * STEP + at
            tile = jnp.where(slot < count, tiles_ref[at].astype(F32), 0.0)
            place = cols_ref[slot] * 8 + rows_ref[slot]
            acc_ref[place] = jnp.where(seen_ref[place] > 0, acc_ref[place], 0.0) + tile
            seen_ref[place] = 1
        return carry

    lax.fori_loop(0, STEP // GROUP, group, 0)

    @pl.when(step == NB // STEP - 1)
    def _():
        def out_copy(q):
            return pltpu.make_async_copy(pack_ref.at[q], out_ref.at[q], sem.at[q])

        def chunk(q, carry):
            def block(u, inner):
                rows = pl.ds(pl.multiple_of(u * 128, 128), 128)
                for e in range(2):
                    place = q * 16 + e * 8 + u
                    total = jnp.where(seen_ref[place] > 0, acc_ref[place], 0.0)
                    pack_ref[q, rows, e * 128 : (e + 1) * 128] = total.astype(BF16)
                return inner

            lax.fori_loop(0, 8, block, 0)
            out_copy(q).start()
            return carry

        def finish(q, carry):
            out_copy(q).wait()
            return carry

        lax.fori_loop(0, 8, chunk, 0)
        lax.fori_loop(0, 8, finish, 0)


def dense_tile(rows, cols, count, tiles):
    return pl.pallas_call(
        dense_kernel,
        grid=(NB // STEP,),
        out_shape=jax.ShapeDtypeStruct((8, 1024, 256), BF16),
        in_specs=[smem(), smem(), smem(), pl.BlockSpec((STEP, 128, 128), lambda i: (i, 0, 0))],
        out_specs=pl.BlockSpec(memory_space=pl.ANY),
        scratch_shapes=[
            pltpu.VMEM((128, 128, 128), F32),
            pltpu.VMEM((8, 1024, 256), BF16),
            pltpu.SMEM((128,), jnp.int32),
            pltpu.SemaphoreType.DMA((8,)),
        ],
        compiler_params=pltpu.CompilerParams(
            dimension_semantics=("arbitrary",), vmem_limit_bytes=LIMIT
        ),
        name="dense_tile",
    )(rows, cols, count, tiles)


HALF = 128
def table(digits):
    return sum(digit * 8**n for n, digit in enumerate(digits))


FORWARD = (0, 1, 6, 7, 2, 3, 4, 5)
BACKWARD = (5, 3, 4, 7, 2, 1, 6, 0)


def krylov_kernel(
    own_ref, dense_ref, items_ref, gram_ref,
    tile, panel, acc, part, got1, sum1, got2, mine, wide, turned, users,
    value, near, pack, relay, far, cut, gram1, gsum1, gram2, gsum2, gram3, gsum3, gwide,
    load, send_p, recv_p, send_u, recv_u, send_a, recv_a, send_b, recv_b, send_g, recv_g,
):
    row, col, y, z = places()
    chip, core = lax.div(row, 2), lax.rem(row, 2)
    other = 1 - core
    partner = (chip * 2 + other, col)
    spots = {"r": row, "y": y, "z": z}
    low, high = pl.ds(0, HALF), pl.ds(HALF, HALF)

    def spot(i, which):
        return ring(chip, i, X) * 2 + which

    def place(digit):
        return spot(lax.div(digit, 2), lax.rem(core + lax.rem(digit, 2), 2))

    def beside(i):
        return (spot(i, core), col)

    def along(axis, i):
        target = ring(spots[axis], i, 8)
        if axis == "r":
            return target, (target, col)
        if axis == "y":
            return target, (row, target * Z + z)
        return target, (row, y * Z + target)

    def fetch(digit):
        q = place(digit)
        return pltpu.make_async_copy(dense_ref.at[q], tile.at[q], load.at[digit])

    def fetch_next(n, digits):
        fetch(lax.rem(digits, 8)).start()
        return lax.div(digits, 8)

    mine_copy = pltpu.make_async_copy(own_ref, panel.at[row], load.at[8])
    mine_copy.start()
    lax.fori_loop(0, 8, fetch_next, table(FORWARD))

    greet([(8, lambda i, axis=axis: along(axis, i)[1]) for axis in "ryz"])

    def landed(dst, sends, recvs, n):
        remote(dst, dst, sends.at[n], recvs.at[n], partner).wait_recv()

    def far_first(body):
        def step(n, carry):
            body(4 + lax.div(n + 1, 2) * (1 - 2 * lax.rem(n, 2)))
            return carry

        lax.fori_loop(0, 7, step, 0)

    prev, nxt, over = spot(3, core), spot(1, core), spot(2, core)
    last = spot(2, other)
    p = (send_p, recv_p)
    hops = [
        (own_ref, panel.at[row], partner),
        (own_ref, panel.at[row], beside(1)),
        (own_ref, panel.at[row], beside(3)),
        (panel.at[prev, low], panel.at[prev, low], beside(1)),
        (panel.at[nxt, high], panel.at[nxt, high], beside(3)),
        (panel.at[prev], panel.at[prev], partner),
        (panel.at[nxt], panel.at[nxt], partner),
        (panel.at[over, low], panel.at[over, low], partner),
        (panel.at[over, high], panel.at[over, high], partner),
    ]

    def hop(n):
        src, dst, device = hops[n]
        return remote(src, dst, send_p.at[n], recv_p.at[n], device)

    for n in (1, 2, 0):
        hop(n).start()
    acc[...] = jnp.zeros_like(acc)
    mine_copy.wait()

    def multiply(n, digits):
        digit = lax.rem(digits, 8)
        fetch(digit).wait()

        @pl.when(n == 1)
        def _():
            landed(panel.at[spot(0, other)], *p, 0)

        @pl.when(n == 2)
        def _():
            landed(panel.at[prev], *p, 1)
            hop(3).start()
            landed(panel.at[nxt], *p, 2)
            hop(4).start()
            hop(5).start()
            hop(6).start()

        @pl.when(n == 3)
        def _():
            landed(panel.at[spot(3, other)], *p, 5)

        @pl.when(n == 4)
        def _():
            landed(panel.at[over, low], *p, 3)
            hop(7).start()
            landed(panel.at[over, high], *p, 4)
            hop(8).start()

        @pl.when(n == 5)
        def _():
            landed(panel.at[spot(1, other)], *p, 6)

        @pl.when(n == 7)
        def _():
            landed(panel.at[last, low], *p, 7)
            landed(panel.at[last, high], *p, 8)

        q = place(digit)
        acc[...] += jnp.dot(tile[q], panel[q], preferred_element_type=F32)
        return lax.div(digits, 8)

    lax.fori_loop(0, 8, multiply, table(FORWARD))

    def walk(axis, source, landing, send, recv, what):
        if what == "start":
            def step(i):
                target, device = along(axis, i)
                remote(source(target), landing.at[spots[axis]], send, recv, device).start()

            far_first(step)
        else:
            seven = landing.at[pl.ds(0, 7)]
            whole = remote(seven, seven, send, recv, partner)
            if what == "arrive":
                whole.wait_recv()
            else:
                whole.wait_send()

    def u(stage, h):
        return send_u.at[stage, h], recv_u.at[stage, h]

    me, first, second = (y, z), ("y", "z"), ("z", "y")
    jobs = [
        [(first[h], lambda t, h=h: part.at[h, t], got1.at[h]) for h in range(2)],
        [(second[h], lambda t, h=h: sum1.at[h, t], got2.at[h]) for h in range(2)],
        [(second[h], lambda t, h=h: mine.at[h], wide.at[h]) for h in range(2)],
        [(first[h], lambda t, h=h: turned.at[h], users.at[h]) for h in range(2)],
    ]

    def users_step(stage, h, what):
        walk(*jobs[stage][h], *u(stage, h), what)

    for h in range(2):
        def narrow(k, carry, h=h):
            rows = pl.ds(pl.multiple_of(k * 128, 128), 128)
            part[h, k] = acc[rows, h * 128 : (h + 1) * 128].astype(BF16)
            return carry

        lax.fori_loop(0, 8, narrow, 0)
        users_step(0, h, "start")
    for h in range(2):
        got1[h, me[h]] = part[h, me[h]]
    for n in range(9):
        hop(n).wait_send()
    for h in range(2):
        users_step(0, h, "arrive")
        total = got1[h, 0].astype(F32)
        for k in range(1, 8):
            total = total + got1[h, k].astype(F32)
        sum1[h] = total.reshape(8, 16, 128)
        users_step(1, h, "start")
        got2[h, me[1 - h]] = sum1[h, me[1 - h]]
    for h in range(2):
        users_step(0, h, "leave")
    for h in range(2):
        users_step(1, h, "arrive")
        total = got2[h, 0]
        for k in range(1, 8):
            total = total + got2[h, k]
        mine[h] = total.astype(BF16)
        users_step(2, h, "start")
        wide[h, me[1 - h]] = mine[h]
    for h in range(2):
        users_step(1, h, "leave")

    for h in range(2):
        users_step(2, h, "arrive")
        turned[h] = wide[h].reshape(128, 128).astype(F32).T.astype(BF16)
        users_step(3, h, "start")
        users[h, me[h]] = turned[h]
    for h in range(2):
        users_step(2, h, "leave")
    for h in range(2):
        users_step(3, h, "arrive")

    a, b = (send_a, recv_a), (send_b, recv_b)

    def lend(i):
        return remote(value.at[2 * i + 1], near.at[i], send_a.at[i], recv_a.at[i], partner)

    moves = [
        (pack.at[2, low], relay.at[0], beside(1)),
        (pack.at[2, high], relay.at[1], beside(3)),
        (pack.at[1, high], far.at[0, high], beside(1)),
        (pack.at[3, low], far.at[1, low], beside(3)),
        (pack.at[1, low], far.at[0, low], beside(1)),
        (pack.at[3, high], far.at[1, high], beside(3)),
    ]

    def pass_on(n):
        src, dst, device = moves[n]
        return remote(src, dst, send_b.at[n], recv_b.at[n], device)

    def meet(i):
        landed(near.at[i], *a, i)
        near[i] = value[2 * i] + near[i]

    def transposed(n, digits):
        digit = lax.rem(digits, 8)
        left = jnp.concatenate(
            [jnp.concatenate([users[h, k] for k in range(8)], axis=1) for h in range(2)], axis=0
        )
        value[digit] = jnp.dot(left, tile[place(digit)], preferred_element_type=F32)
        for step, i in ((0, 2), (1, 1), (3, 3), (5, 0)):
            @pl.when(n == step)
            def _(i=i):
                lend(i).start()

        @pl.when(n == 2)
        def _():
            meet(2)
            pack[2] = near[2].astype(BF16)
            pass_on(0).start()
            pass_on(1).start()

        @pl.when(n == 4)
        def _():
            meet(1)
            pack[1, HALF:] = near[1, HALF:].astype(BF16)
            pass_on(2).start()

        @pl.when(n == 6)
        def _():
            meet(3)
            pack[3, :HALF] = near[3, :HALF].astype(BF16)
            pass_on(3).start()

        return lax.div(digits, 8)

    lax.fori_loop(0, 8, transposed, table(BACKWARD))
    landed(relay.at[0], *b, 0)
    pack[1, :HALF] = (near[1, :HALF] + relay[0].astype(F32)).astype(BF16)
    pass_on(4).start()
    landed(relay.at[1], *b, 1)
    pack[3, HALF:] = (near[3, HALF:] + relay[1].astype(F32)).astype(BF16)
    pass_on(5).start()
    meet(0)

    for h in range(2):
        users_step(3, h, "leave")
    for i in range(X):
        lend(i).wait_send()
    landed(far.at[0, high], *b, 2)
    landed(far.at[1, low], *b, 3)
    landed(far.at[0, low], *b, 4)
    landed(far.at[1, high], *b, 5)
    items = near[0] + far[0].astype(F32) + far[1].astype(F32)
    items_ref[...] = items

    gram = lax.dot_general(
        items, items, (((1,), (1,)), ((), ())), precision=HIGH, preferred_element_type=F32
    )
    for k in range(16):
        for c in range(2):
            cut[k // 2, (k % 2) * 2 + c] = gram[
                16 * k : 16 * k + 16, 128 * c : 128 * c + 128
            ].astype(BF16)

    def g(n):
        return send_g.at[n], recv_g.at[n]

    spread = [
        ("r", lambda t: cut.at[t], gram1),
        ("y", lambda t: gsum1.at[t], gram2),
        ("z", lambda t: gsum2, gram3),
        ("y", lambda t: gsum3, gwide),
        ("r", lambda t: gwide, gram_ref),
    ]

    def move(n):
        axis, source, landing = spread[n]
        walk(*spread[n], *g(n), "start")
        landing[spots[axis]] = source(spots[axis])[...]
        if n:
            walk(*spread[n - 1], *g(n - 1), "leave")
        else:
            for k in range(6):
                pass_on(k).wait_send()
        walk(*spread[n], *g(n), "arrive")

    def summed(got):
        total = got[0].astype(F32)
        for k in range(1, 8):
            total = total + got[k].astype(F32)
        return total

    move(0)
    gsum1[...] = summed(gram1).reshape(8, 8, 128)
    move(1)
    gsum2[...] = summed(gram2)
    move(2)
    gsum3[...] = summed(gram3)
    move(3)

    move(4)
    walk(*spread[4], *g(4), "leave")


def krylov(own, tile):
    cell = (8, 128)
    dma = pltpu.SemaphoreType.DMA
    pairs = [(9,), (4, 2), (X,), (6,), (5,)]
    return pl.pallas_call(
        krylov_kernel,
        out_shape=(
            jax.ShapeDtypeStruct((256, 256), F32),
            jax.ShapeDtypeStruct((8, 8) + cell, F32),
        ),
        in_specs=[pl.BlockSpec(memory_space=pl.ANY), pl.BlockSpec(memory_space=pl.ANY)],
        out_specs=(vmem(), vmem()),
        scratch_shapes=[
            pltpu.VMEM((8, 1024, 256), BF16),
            pltpu.VMEM((8, 256, 256), BF16),
            pltpu.VMEM((1024, 256), F32),
            pltpu.VMEM((2, 8, 128, 128), BF16),
            pltpu.VMEM((2, 8, 128, 128), BF16),
            pltpu.VMEM((2, 8, 16, 128), F32),
            pltpu.VMEM((2, 8, 16, 128), F32),
            pltpu.VMEM((2, 16, 128), BF16),
            pltpu.VMEM((2, 8, 16, 128), BF16),
            pltpu.VMEM((2, 128, 128), BF16),
            pltpu.VMEM((2, 8, 128, 128), BF16),
            pltpu.VMEM((8, 256, 256), F32),
            pltpu.VMEM((X, 256, 256), F32),
            pltpu.VMEM((X, 256, 256), BF16),
            pltpu.VMEM((2, HALF, 256), BF16),
            pltpu.VMEM((2, 256, 256), BF16),
            pltpu.VMEM((8, 4, 16, 128), BF16),
            pltpu.VMEM((8, 4, 16, 128), BF16),
            pltpu.VMEM((8,) + cell, F32),
            pltpu.VMEM((8,) + cell, F32),
            pltpu.VMEM(cell, F32),
            pltpu.VMEM((8,) + cell, F32),
            pltpu.VMEM(cell, F32),
            pltpu.VMEM((8,) + cell, F32),
            dma((9,)),
        ]
        + [dma(shape) for shape in pairs for _ in range(2)],
        compiler_params=pltpu.CompilerParams(
            collective_id=0, has_side_effects=True, vmem_limit_bytes=ROOM
        ),
        name="krylov",
    )(own, tile)


PANEL = 32
N = 256


def factor_kernel(gram_ref, items_ref, basis_ref, factor_ref, a_ref, d_ref):
    for k in range(32):
        for c in range(2):
            a_ref[8 * k : 8 * k + 8, 128 * c : 128 * c + 128] = gram_ref[
                k // 4, (k // 2 % 2) * 4 + c * 2 + k % 2
            ]

    for base in range(0, N, PANEL):
        w = a_ref[base : base + PANEL, :]
        d = jnp.zeros((PANEL, 128), F32)
        for low in range(0, PANEL, 8):
            part = w[low:, :]
            size = PANEL - low
            lane = lax.broadcasted_iota(jnp.int32, (size, N), 1)
            sub = lax.broadcasted_iota(jnp.int32, (size, N), 0) + low
            sub1 = sub[:, :128]
            first = base + low
            columns = [
                jnp.broadcast_to(part[:, first + b : first + b + 1], (size, 128)) for b in range(8)
            ]
            d_part = d[low:, :]
            for a in range(0, 8, 2):
                r = low + a
                one, two = columns[a], columns[a + 1]
                p11, p12 = one[a : a + 1, :], two[a : a + 1, :]
                p21, p22 = one[a + 1 : a + 2, :], two[a + 1 : a + 2, :]
                inv1 = 1.0 / p11
                inv2 = p11 * (1.0 / (p11 * p22 - p21 * p12))
                ratio = p21 * inv1
                m1 = jnp.where(sub1 > r, one * inv1, 0.0)
                m2 = jnp.where(sub1 > r + 1, (two - m1 * p12) * inv2, 0.0)
                for b in range(a + 2, 8):
                    top = columns[b][a : a + 1, :]
                    next_top = columns[b][a + 1 : a + 2, :] - ratio * top
                    columns[b] = columns[b] - m1 * top - m2 * next_top
                lane1 = lane[:1]
                line1 = jnp.where(lane1 == base + r, 1.0, part[a : a + 1, :])
                ratio2 = jnp.concatenate([ratio, ratio], axis=1)
                line2 = jnp.where(lane1 == base + r, 0.0, part[a + 1 : a + 2, :]) - ratio2 * line1
                line1 = jnp.where(lane1 == base + r + 1, 0.0, line1)
                line2 = jnp.where(lane1 == base + r + 1, 1.0, line2)
                gone = ((lane == base + r) & (sub > r)) | ((lane == base + r + 1) & (sub > r + 1))
                part = (
                    jnp.where(gone, 0.0, part)
                    - jnp.concatenate([m1, m1], axis=1) * line1
                    - jnp.concatenate([m2, m2], axis=1) * line2
                )
                d_part = jnp.where(sub1 == r, p11, d_part)
                d_part = jnp.where(sub1 == r + 1, p22 - ratio * p12, d_part)
            w = part if low == 0 else jnp.concatenate([w[:low], part], axis=0)
            d = d_part if low == 0 else jnp.concatenate([d[:low], d_part], axis=0)
        a_ref[base : base + PANEL, :] = w
        d_ref[base : base + PANEL, :] = d
        after = base + PANEL
        if after == N:
            break
        lane = lax.broadcasted_iota(jnp.int32, (PANEL, N), 1)
        sub = lax.broadcasted_iota(jnp.int32, (PANEL, N), 0) + base
        scaled = jnp.where(lane >= after, w / jnp.concatenate([d, d], axis=1), 0.0).T
        inside = (lane < after) & (lane >= sub)
        right = jnp.where(inside, jnp.where(lane == sub, 1.0, 0.0), w)
        for top, bottom in ((after, after + PANEL), (after + PANEL, N)):
            if top < bottom:
                lane = lax.broadcasted_iota(jnp.int32, (bottom - top, N), 1)
                kept = jnp.where((lane >= base) & (lane < after), 0.0, a_ref[top:bottom, :])
                a_ref[top:bottom, :] = kept - jnp.dot(
                    scaled[top:bottom], right, precision=HIGH, preferred_element_type=F32
                )

    lane = lax.broadcasted_iota(jnp.int32, (N, N), 1)
    sub = lax.broadcasted_iota(jnp.int32, (N, N), 0)
    pivots = d_ref[...]
    scale = 1.0 / jnp.sqrt(pivots)
    scale = jnp.concatenate([scale, scale], axis=1)
    full = jnp.where(lane == sub, jnp.concatenate([pivots, pivots], axis=1), a_ref[...])
    factor_ref[...] = jnp.where(lane >= sub, full, 0.0) * scale
    inverse = jnp.where(lane < sub, full, jnp.where(lane == sub, 1.0, 0.0)) * scale
    basis_ref[...] = jnp.dot(
        inverse, items_ref[...], precision=HIGH, preferred_element_type=F32
    ).T


def factor_call(gram, items):
    return pl.pallas_call(
        factor_kernel,
        out_shape=(
            jax.ShapeDtypeStruct((256, 256), F32),
            jax.ShapeDtypeStruct((256, 256), F32),
        ),
        in_specs=[vmem(), vmem()],
        out_specs=(vmem(), vmem()),
        scratch_shapes=[pltpu.VMEM((N, N), F32), pltpu.VMEM((N, 128), F32)],
        compiler_params=pltpu.CompilerParams(vmem_limit_bytes=ROOM),
        name="factor",
    )(gram, items)


def local(blocks, block_row, block_col, counts, start_block):
    tile = dense_tile(block_row[0, 0], block_col[0, 0], counts[0], blocks[0, 0])
    items, gram = krylov(start_block, tile)
    return factor_call(gram, items)


def solution(mesh):
    return jax.shard_map(
        local,
        mesh=mesh,
        in_specs=(
            P("rows", "cols", None, None, None),
            P("rows", "cols", None),
            P("rows", "cols", None),
            P("rows", "cols"),
            P(("cols", "rows"), None),
        ),
        out_specs=(P(("cols", "rows"), None), P()),
        check_vma=False,
    )
```

```python
import jax
import jax.numpy as jnp
from jax import lax
from jax.experimental import pallas as pl
from jax.experimental.pallas import tpu as pltpu
from jax.sharding import PartitionSpec as P

MESH = pl.DeviceIdType.MESH
F32 = jnp.float32
BF16 = jnp.bfloat16
HIGH = lax.Precision.HIGHEST
LIMIT = 63 * 1024 * 1024
ROOM = 53 * 1024 * 1024
NB = 96
GROUP = 8
STEP = 24
X, Y, Z = 4, 8, 8


def vmem():
    return pl.BlockSpec(memory_space=pltpu.VMEM)


def smem():
    return pl.BlockSpec(memory_space=pltpu.SMEM)


def remote(src, dst, send, recv, device):
    return pltpu.make_async_remote_copy(
        src_ref=src, dst_ref=dst, send_sem=send, recv_sem=recv, device_id=device, device_id_type=MESH
    )


def places():
    row = lax.axis_index("rows")
    col = lax.axis_index("cols")
    return row, col, lax.div(col, Z), lax.rem(col, Z)


def each(count, body):
    def step(i, carry):
        body(i)
        return carry

    lax.fori_loop(1, count, step, 0)


def ring(me, i, count):
    return lax.rem(me + i, count)


def greet(makers):
    barrier = pltpu.get_barrier_semaphore()
    total = 0
    for count, device in makers:
        each(
            count,
            lambda i, device=device: pl.semaphore_signal(
                barrier, inc=1, device_id=device(i), device_id_type=MESH
            ),
        )
        total += count - 1
    pl.semaphore_wait(barrier, total)


def dense_kernel(rows_ref, cols_ref, count_ref, tiles_ref, out_ref, acc_ref, pack_ref, sem):
    step = pl.program_id(0)

    @pl.when(step == 0)
    def _():
        acc_ref[...] = jnp.zeros_like(acc_ref)

    count = count_ref[0]

    def group(g, carry):
        for j in range(GROUP):
            at = g * GROUP + j
            slot = step * STEP + at
            tile = jnp.where(slot < count, tiles_ref[at].astype(F32), 0.0)
            col = cols_ref[slot]
            acc_ref[lax.div(col, 2), lax.rem(col, 2), rows_ref[slot]] += tile
        return carry

    lax.fori_loop(0, STEP // GROUP, group, 0)

    @pl.when(step == NB // STEP - 1)
    def _():
        def out_copy(q):
            return pltpu.make_async_copy(pack_ref.at[q], out_ref.at[q], sem.at[q])

        def chunk(q, carry):
            def block(u, inner):
                rows = pl.ds(pl.multiple_of(u * 128, 128), 128)
                for e in range(2):
                    pack_ref[q, rows, e * 128 : (e + 1) * 128] = acc_ref[q, e, u].astype(BF16)
                return inner

            lax.fori_loop(0, 8, block, 0)
            out_copy(q).start()
            return carry

        def finish(q, carry):
            out_copy(q).wait()
            return carry

        lax.fori_loop(0, 8, chunk, 0)
        lax.fori_loop(0, 8, finish, 0)


def dense_tile(rows, cols, count, tiles):
    return pl.pallas_call(
        dense_kernel,
        grid=(NB // STEP,),
        out_shape=jax.ShapeDtypeStruct((8, 1024, 256), BF16),
        in_specs=[smem(), smem(), smem(), pl.BlockSpec((STEP, 128, 128), lambda i: (i, 0, 0))],
        out_specs=pl.BlockSpec(memory_space=pl.ANY),
        scratch_shapes=[
            pltpu.VMEM((8, 2, 8, 128, 128), F32),
            pltpu.VMEM((8, 1024, 256), BF16),
            pltpu.SemaphoreType.DMA((8,)),
        ],
        compiler_params=pltpu.CompilerParams(
            dimension_semantics=("arbitrary",), vmem_limit_bytes=LIMIT
        ),
        name="dense_tile",
    )(rows, cols, count, tiles)


HALF = 128
def table(digits):
    return sum(digit * 8**n for n, digit in enumerate(digits))


FORWARD = (0, 1, 6, 7, 2, 3, 4, 5)
BACKWARD = (5, 3, 4, 7, 2, 1, 6, 0)


def krylov_kernel(
    own_ref, dense_ref, items_ref, gram_ref,
    tile, panel, turned, acc, part, got1, sum1, got2, mine, wide, whole, users,
    value, near, pack, relay, far, cut, gram1, gsum1, gram2, gsum2, gram3, gsum3, gwide,
    load, send_p, recv_p, send_u, recv_u, send_a, recv_a, send_b, recv_b, send_g, recv_g,
):
    row, col, y, z = places()
    chip, core = lax.div(row, 2), lax.rem(row, 2)
    other = 1 - core
    partner = (chip * 2 + other, col)
    spots = {"r": row, "y": y, "z": z}
    low, high = pl.ds(0, HALF), pl.ds(HALF, HALF)

    def spot(i, which):
        return ring(chip, i, X) * 2 + which

    def place(digit):
        return spot(lax.div(digit, 2), lax.rem(core + lax.rem(digit, 2), 2))

    def beside(i):
        return (spot(i, core), col)

    def along(axis, i):
        target = ring(spots[axis], i, 8)
        if axis == "r":
            return target, (target, col)
        if axis == "y":
            return target, (row, target * Z + z)
        return target, (row, y * Z + target)

    def fetch(digit):
        q = place(digit)
        return pltpu.make_async_copy(dense_ref.at[q], tile.at[q], load.at[digit])

    def fetch_next(n, digits):
        fetch(lax.rem(digits, 8)).start()
        return lax.div(digits, 8)

    lax.fori_loop(0, 8, fetch_next, table(FORWARD))
    turned[...] = own_ref[...].astype(F32).T.astype(BF16)

    greet([(8, lambda i, axis=axis: along(axis, i)[1]) for axis in "ryz"])

    def landed(dst, sends, recvs, n):
        remote(dst, dst, sends.at[n], recvs.at[n], partner).wait_recv()

    def far_first(body):
        def step(n, carry):
            body(4 + lax.div(n + 1, 2) * (1 - 2 * lax.rem(n, 2)))
            return carry

        lax.fori_loop(0, 7, step, 0)

    prev, nxt, over = spot(3, core), spot(1, core), spot(2, core)
    last = spot(2, other)
    p = (send_p, recv_p)
    hops = [
        (turned, panel.at[row], partner),
        (turned, panel.at[row], beside(1)),
        (turned, panel.at[row], beside(3)),
        (panel.at[prev, low], panel.at[prev, low], beside(1)),
        (panel.at[nxt, high], panel.at[nxt, high], beside(3)),
        (panel.at[prev], panel.at[prev], partner),
        (panel.at[nxt], panel.at[nxt], partner),
        (panel.at[over, low], panel.at[over, low], partner),
        (panel.at[over, high], panel.at[over, high], partner),
    ]

    def hop(n):
        src, dst, device = hops[n]
        return remote(src, dst, send_p.at[n], recv_p.at[n], device)

    for n in (1, 2, 0):
        hop(n).start()
    panel[row] = turned[...]
    acc[...] = jnp.zeros_like(acc)

    def multiply(n, digits):
        digit = lax.rem(digits, 8)
        fetch(digit).wait()

        @pl.when(n == 1)
        def _():
            landed(panel.at[spot(0, other)], *p, 0)

        @pl.when(n == 2)
        def _():
            landed(panel.at[prev], *p, 1)
            hop(3).start()
            landed(panel.at[nxt], *p, 2)
            hop(4).start()
            hop(5).start()
            hop(6).start()

        @pl.when(n == 3)
        def _():
            landed(panel.at[spot(3, other)], *p, 5)

        @pl.when(n == 4)
        def _():
            landed(panel.at[over, low], *p, 3)
            hop(7).start()
            landed(panel.at[over, high], *p, 4)
            hop(8).start()

        @pl.when(n == 5)
        def _():
            landed(panel.at[spot(1, other)], *p, 6)

        @pl.when(n == 7)
        def _():
            landed(panel.at[last, low], *p, 7)
            landed(panel.at[last, high], *p, 8)

        q = place(digit)
        acc[...] += lax.dot_general(
            panel[q], tile[q], (((1,), (1,)), ((), ())), preferred_element_type=F32
        )
        return lax.div(digits, 8)

    lax.fori_loop(0, 8, multiply, table(FORWARD))

    def walk(axis, source, landing, send, recv, what):
        if what == "start":
            def step(i):
                target, device = along(axis, i)
                remote(source(target), landing.at[spots[axis]], send, recv, device).start()

            far_first(step)
        else:
            seven = landing.at[pl.ds(0, 7)]
            whole = remote(seven, seven, send, recv, partner)
            if what == "arrive":
                whole.wait_recv()
            else:
                whole.wait_send()

    me, first, second = (y, z, y, z), ("y", "z", "y", "z"), ("z", "y", "z", "y")
    them = (z, y, z, y)
    jobs = [
        [(first[h], lambda t, h=h: part.at[h, t], got1.at[h]) for h in range(4)],
        [(second[h], lambda t, h=h: sum1.at[h, t], got2.at[h]) for h in range(4)],
        [(second[h], lambda t, h=h: mine.at[h], wide.at[h]) for h in range(4)],
        [(first[h], lambda t, h=h: whole.at[h], users.at[h]) for h in range(4)],
    ]

    def users_step(stage, h, what):
        walk(*jobs[stage][h], send_u.at[stage, h], recv_u.at[stage, h], what)

    def summed(got):
        total = got[0].astype(F32)
        for k in range(1, 8):
            total = total + got[k].astype(F32)
        return total

    for h in range(4):
        for k in range(8):
            part[h, k] = acc[h * 64 : (h + 1) * 64, k * 128 : (k + 1) * 128].astype(BF16)
        users_step(0, h, "start")
    for h in range(4):
        got1[h, me[h]] = part[h, me[h]]
    for n in range(9):
        hop(n).wait_send()
    for h in range(4):
        users_step(0, h, "arrive")
        sum1[h] = summed(got1.at[h]).reshape(8, 8, 128)
        users_step(1, h, "start")
        got2[h, them[h]] = sum1[h, them[h]]
    for h in range(4):
        users_step(0, h, "leave")
    for h in range(4):
        users_step(1, h, "arrive")
        mine[h] = summed(got2.at[h])
        users_step(2, h, "start")
        wide[h, them[h]] = mine[h]
    for h in range(4):
        users_step(1, h, "leave")
    for h in range(4):
        users_step(2, h, "arrive")
        whole[h] = wide[h].reshape(64, 128).astype(BF16)
        users_step(3, h, "start")
        users[h, me[h]] = whole[h]
    for h in range(4):
        users_step(2, h, "leave")
    for h in range(4):
        users_step(3, h, "arrive")

    a, b = (send_a, recv_a), (send_b, recv_b)

    def lend(i):
        return remote(value.at[2 * i + 1], near.at[i], send_a.at[i], recv_a.at[i], partner)

    moves = [
        (pack.at[2, low], relay.at[0], beside(1)),
        (pack.at[2, high], relay.at[1], beside(3)),
        (pack.at[1, high], far.at[0, high], beside(1)),
        (pack.at[3, low], far.at[1, low], beside(3)),
        (pack.at[1, low], far.at[0, low], beside(1)),
        (pack.at[3, high], far.at[1, high], beside(3)),
    ]

    def pass_on(n):
        src, dst, device = moves[n]
        return remote(src, dst, send_b.at[n], recv_b.at[n], device)

    def meet(i):
        landed(near.at[i], *a, i)
        near[i] = value[2 * i] + near[i]

    def transposed(n, digits):
        digit = lax.rem(digits, 8)
        left = jnp.concatenate(
            [jnp.concatenate([users[h, k] for k in range(8)], axis=1) for h in range(4)], axis=0
        )
        value[digit] = jnp.dot(left, tile[place(digit)], preferred_element_type=F32)
        for step, i in ((0, 2), (1, 1), (3, 3), (5, 0)):
            @pl.when(n == step)
            def _(i=i):
                lend(i).start()

        @pl.when(n == 2)
        def _():
            meet(2)
            pack[2] = near[2].astype(BF16)
            pass_on(0).start()
            pass_on(1).start()

        @pl.when(n == 4)
        def _():
            meet(1)
            pack[1, HALF:] = near[1, HALF:].astype(BF16)
            pass_on(2).start()

        @pl.when(n == 6)
        def _():
            meet(3)
            pack[3, :HALF] = near[3, :HALF].astype(BF16)
            pass_on(3).start()

        return lax.div(digits, 8)

    lax.fori_loop(0, 8, transposed, table(BACKWARD))
    landed(relay.at[0], *b, 0)
    pack[1, :HALF] = (near[1, :HALF] + relay[0].astype(F32)).astype(BF16)
    pass_on(4).start()
    landed(relay.at[1], *b, 1)
    pack[3, HALF:] = (near[3, HALF:] + relay[1].astype(F32)).astype(BF16)
    pass_on(5).start()
    meet(0)

    for h in range(4):
        users_step(3, h, "leave")
    for i in range(X):
        lend(i).wait_send()
    landed(far.at[0, high], *b, 2)
    landed(far.at[1, low], *b, 3)
    landed(far.at[0, low], *b, 4)
    landed(far.at[1, high], *b, 5)
    items = near[0] + far[0].astype(F32) + far[1].astype(F32)
    items_ref[...] = items

    gram = lax.dot_general(
        items, items, (((1,), (1,)), ((), ())), precision=HIGH, preferred_element_type=F32
    )
    for k in range(16):
        for c in range(2):
            cut[k // 2, (k % 2) * 2 + c] = gram[
                16 * k : 16 * k + 16, 128 * c : 128 * c + 128
            ].astype(BF16)

    def g(n):
        return send_g.at[n], recv_g.at[n]

    spread = [
        ("r", lambda t: cut.at[t], gram1),
        ("y", lambda t: gsum1.at[t], gram2),
        ("z", lambda t: gsum2, gram3),
        ("y", lambda t: gsum3, gwide),
        ("r", lambda t: gwide, gram_ref),
    ]

    def move(n):
        axis, source, landing = spread[n]
        walk(*spread[n], *g(n), "start")
        landing[spots[axis]] = source(spots[axis])[...]
        if n:
            walk(*spread[n - 1], *g(n - 1), "leave")
        else:
            for k in range(6):
                pass_on(k).wait_send()
        walk(*spread[n], *g(n), "arrive")

    move(0)
    gsum1[...] = summed(gram1).reshape(8, 8, 128)
    move(1)
    gsum2[...] = summed(gram2)
    move(2)
    gsum3[...] = summed(gram3)
    move(3)

    move(4)
    walk(*spread[4], *g(4), "leave")


def krylov(own, tile):
    cell = (8, 128)
    dma = pltpu.SemaphoreType.DMA
    pairs = [(9,), (4, 4), (X,), (6,), (5,)]
    return pl.pallas_call(
        krylov_kernel,
        out_shape=(
            jax.ShapeDtypeStruct((256, 256), F32),
            jax.ShapeDtypeStruct((8, 8) + cell, F32),
        ),
        in_specs=[vmem(), pl.BlockSpec(memory_space=pl.ANY)],
        out_specs=(vmem(), vmem()),
        scratch_shapes=[
            pltpu.VMEM((8, 1024, 256), BF16),
            pltpu.VMEM((8, 256, 256), BF16),
            pltpu.VMEM((256, 256), BF16),
            pltpu.VMEM((256, 1024), F32),
            pltpu.VMEM((4, 8, 64, 128), BF16),
            pltpu.VMEM((4, 8, 64, 128), BF16),
            pltpu.VMEM((4, 8) + cell, F32),
            pltpu.VMEM((4, 8) + cell, F32),
            pltpu.VMEM((4,) + cell, F32),
            pltpu.VMEM((4, 8) + cell, F32),
            pltpu.VMEM((4, 64, 128), BF16),
            pltpu.VMEM((4, 8, 64, 128), BF16),
            pltpu.VMEM((8, 256, 256), F32),
            pltpu.VMEM((X, 256, 256), F32),
            pltpu.VMEM((X, 256, 256), BF16),
            pltpu.VMEM((2, HALF, 256), BF16),
            pltpu.VMEM((2, 256, 256), BF16),
            pltpu.VMEM((8, 4, 16, 128), BF16),
            pltpu.VMEM((8, 4, 16, 128), BF16),
            pltpu.VMEM((8,) + cell, F32),
            pltpu.VMEM((8,) + cell, F32),
            pltpu.VMEM(cell, F32),
            pltpu.VMEM((8,) + cell, F32),
            pltpu.VMEM(cell, F32),
            pltpu.VMEM((8,) + cell, F32),
            dma((8,)),
        ]
        + [dma(shape) for shape in pairs for _ in range(2)],
        compiler_params=pltpu.CompilerParams(
            collective_id=0, has_side_effects=True, vmem_limit_bytes=ROOM
        ),
        name="krylov",
    )(own, tile)


PANEL = 32
N = 256


def factor_kernel(gram_ref, items_ref, basis_ref, factor_ref, a_ref, d_ref):
    for k in range(32):
        for c in range(2):
            a_ref[8 * k : 8 * k + 8, 128 * c : 128 * c + 128] = gram_ref[
                k // 4, (k // 2 % 2) * 4 + c * 2 + k % 2
            ]

    for base in range(0, N, PANEL):
        w = a_ref[base : base + PANEL, :]
        d = jnp.zeros((PANEL, 128), F32)
        for low in range(0, PANEL, 8):
            part = w[low:, :]
            size = PANEL - low
            lane = lax.broadcasted_iota(jnp.int32, (size, N), 1)
            sub = lax.broadcasted_iota(jnp.int32, (size, N), 0) + low
            sub1 = sub[:, :128]
            first = base + low
            columns = [
                jnp.broadcast_to(part[:, first + b : first + b + 1], (size, 128)) for b in range(8)
            ]
            d_part = d[low:, :]
            for a in range(0, 8, 2):
                r = low + a
                one, two = columns[a], columns[a + 1]
                p11, p12 = one[a : a + 1, :], two[a : a + 1, :]
                p21, p22 = one[a + 1 : a + 2, :], two[a + 1 : a + 2, :]
                inv1 = 1.0 / p11
                inv2 = p11 * (1.0 / (p11 * p22 - p21 * p12))
                ratio = p21 * inv1
                m1 = jnp.where(sub1 > r, one * inv1, 0.0)
                m2 = jnp.where(sub1 > r + 1, (two - m1 * p12) * inv2, 0.0)
                for b in range(a + 2, 8):
                    top = columns[b][a : a + 1, :]
                    next_top = columns[b][a + 1 : a + 2, :] - ratio * top
                    columns[b] = columns[b] - m1 * top - m2 * next_top
                lane1 = lane[:1]
                line1 = jnp.where(lane1 == base + r, 1.0, part[a : a + 1, :])
                ratio2 = jnp.concatenate([ratio, ratio], axis=1)
                line2 = jnp.where(lane1 == base + r, 0.0, part[a + 1 : a + 2, :]) - ratio2 * line1
                line1 = jnp.where(lane1 == base + r + 1, 0.0, line1)
                line2 = jnp.where(lane1 == base + r + 1, 1.0, line2)
                gone = ((lane == base + r) & (sub > r)) | ((lane == base + r + 1) & (sub > r + 1))
                part = (
                    jnp.where(gone, 0.0, part)
                    - jnp.concatenate([m1, m1], axis=1) * line1
                    - jnp.concatenate([m2, m2], axis=1) * line2
                )
                d_part = jnp.where(sub1 == r, p11, d_part)
                d_part = jnp.where(sub1 == r + 1, p22 - ratio * p12, d_part)
            w = part if low == 0 else jnp.concatenate([w[:low], part], axis=0)
            d = d_part if low == 0 else jnp.concatenate([d[:low], d_part], axis=0)
        a_ref[base : base + PANEL, :] = w
        d_ref[base : base + PANEL, :] = d
        after = base + PANEL
        if after == N:
            break
        lane = lax.broadcasted_iota(jnp.int32, (PANEL, N), 1)
        sub = lax.broadcasted_iota(jnp.int32, (PANEL, N), 0) + base
        scaled = jnp.where(lane >= after, w / jnp.concatenate([d, d], axis=1), 0.0).T
        inside = (lane < after) & (lane >= sub)
        right = jnp.where(inside, jnp.where(lane == sub, 1.0, 0.0), w)
        for top, bottom in ((after, after + PANEL), (after + PANEL, N)):
            if top < bottom:
                lane = lax.broadcasted_iota(jnp.int32, (bottom - top, N), 1)
                kept = jnp.where((lane >= base) & (lane < after), 0.0, a_ref[top:bottom, :])
                a_ref[top:bottom, :] = kept - jnp.dot(
                    scaled[top:bottom], right, precision=HIGH, preferred_element_type=F32
                )

    lane = lax.broadcasted_iota(jnp.int32, (N, N), 1)
    sub = lax.broadcasted_iota(jnp.int32, (N, N), 0)
    pivots = d_ref[...]
    scale = 1.0 / jnp.sqrt(pivots)
    scale = jnp.concatenate([scale, scale], axis=1)
    full = jnp.where(lane == sub, jnp.concatenate([pivots, pivots], axis=1), a_ref[...])
    factor_ref[...] = jnp.where(lane >= sub, full, 0.0) * scale
    inverse = jnp.where(lane < sub, full, jnp.where(lane == sub, 1.0, 0.0)) * scale
    basis_ref[...] = jnp.dot(
        inverse, items_ref[...], precision=HIGH, preferred_element_type=F32
    ).T


def factor_call(gram, items):
    return pl.pallas_call(
        factor_kernel,
        out_shape=(
            jax.ShapeDtypeStruct((256, 256), F32),
            jax.ShapeDtypeStruct((256, 256), F32),
        ),
        in_specs=[vmem(), vmem()],
        out_specs=(vmem(), vmem()),
        scratch_shapes=[pltpu.VMEM((N, N), F32), pltpu.VMEM((N, 128), F32)],
        compiler_params=pltpu.CompilerParams(vmem_limit_bytes=ROOM),
        name="factor",
    )(gram, items)


def local(blocks, block_row, block_col, counts, start_block):
    tile = dense_tile(block_row[0, 0], block_col[0, 0], counts[0], blocks[0, 0])
    items, gram = krylov(start_block, tile)
    return factor_call(gram, items)


def solution(mesh):
    return jax.shard_map(
        local,
        mesh=mesh,
        in_specs=(
            P("rows", "cols", None, None, None),
            P("rows", "cols", None),
            P("rows", "cols", None),
            P("rows", "cols"),
            P(("cols", "rows"), None),
        ),
        out_specs=(P(("cols", "rows"), None), P()),
        check_vma=False,
    )
```

```python
import jax
import jax.numpy as jnp
from jax import lax
from jax.experimental import pallas as pl
from jax.experimental.pallas import tpu as pltpu
from jax.sharding import PartitionSpec as P

MESH = pl.DeviceIdType.MESH
F32 = jnp.float32
BF16 = jnp.bfloat16
HIGH = lax.Precision.HIGHEST
LIMIT = 63 * 1024 * 1024
ROOM = 53 * 1024 * 1024
NB = 96
GROUP = 8
STEP = 24
X, Y, Z = 4, 8, 8


def vmem():
    return pl.BlockSpec(memory_space=pltpu.VMEM)


def smem():
    return pl.BlockSpec(memory_space=pltpu.SMEM)


def remote(src, dst, send, recv, device):
    return pltpu.make_async_remote_copy(
        src_ref=src, dst_ref=dst, send_sem=send, recv_sem=recv, device_id=device, device_id_type=MESH
    )


def places():
    row = lax.axis_index("rows")
    col = lax.axis_index("cols")
    return row, col, lax.div(col, Z), lax.rem(col, Z)


def each(count, body):
    def step(i, carry):
        body(i)
        return carry

    lax.fori_loop(1, count, step, 0)


def ring(me, i, count):
    return lax.rem(me + i, count)


def greet(makers):
    barrier = pltpu.get_barrier_semaphore()
    for count, device in makers:
        each(
            count,
            lambda i, device=device: pl.semaphore_signal(
                barrier, inc=1, device_id=device(i), device_id_type=MESH
            ),
        )


def dense_kernel(rows_ref, cols_ref, count_ref, tiles_ref, out_ref, acc_ref, pack_ref, sem):
    step = pl.program_id(0)

    @pl.when(step == 0)
    def _():
        acc_ref[...] = jnp.zeros_like(acc_ref)

    count = count_ref[0]

    def group(g, carry):
        for j in range(GROUP):
            at = g * GROUP + j
            slot = step * STEP + at
            tile = jnp.where(slot < count, tiles_ref[at].astype(F32), 0.0)
            col = cols_ref[slot]
            acc_ref[lax.div(col, 2), lax.rem(col, 2), rows_ref[slot]] += tile
        return carry

    lax.fori_loop(0, STEP // GROUP, group, 0)

    @pl.when(step == NB // STEP - 1)
    def _():
        def out_copy(q):
            return pltpu.make_async_copy(pack_ref.at[q], out_ref.at[q], sem.at[q])

        def chunk(q, carry):
            def block(u, inner):
                rows = pl.ds(pl.multiple_of(u * 128, 128), 128)
                for e in range(2):
                    pack_ref[q, rows, e * 128 : (e + 1) * 128] = acc_ref[q, e, u].astype(BF16)
                return inner

            lax.fori_loop(0, 8, block, 0)
            out_copy(q).start()
            return carry

        def finish(q, carry):
            out_copy(q).wait()
            return carry

        lax.fori_loop(0, 8, chunk, 0)
        lax.fori_loop(0, 8, finish, 0)


def dense_tile(rows, cols, count, tiles):
    return pl.pallas_call(
        dense_kernel,
        grid=(NB // STEP,),
        out_shape=jax.ShapeDtypeStruct((8, 1024, 256), BF16),
        in_specs=[smem(), smem(), smem(), pl.BlockSpec((STEP, 128, 128), lambda i: (i, 0, 0))],
        out_specs=pl.BlockSpec(memory_space=pl.ANY),
        scratch_shapes=[
            pltpu.VMEM((8, 2, 8, 128, 128), F32),
            pltpu.VMEM((8, 1024, 256), BF16),
            pltpu.SemaphoreType.DMA((8,)),
        ],
        compiler_params=pltpu.CompilerParams(
            dimension_semantics=("arbitrary",), vmem_limit_bytes=LIMIT
        ),
        name="dense_tile",
    )(rows, cols, count, tiles)


HALF = 128
def table(digits):
    return sum(digit * 8**n for n, digit in enumerate(digits))


FORWARD = (0, 1, 6, 7, 2, 3, 4, 5)
BACKWARD = (5, 3, 4, 7, 2, 1, 6, 0)


def krylov_kernel(
    own_ref, dense_ref, items_ref, gram_ref,
    tile, panel, turned, acc, part, got1, sum1, got2, mine, wide, whole, users,
    value, near, pack, far, cut, gram1, gsum1, gram2, gsum2, gram3, gsum3, gwide,
    load, send_p, recv_p, send_u, recv_u, send_a, recv_a, send_b, recv_b, send_g, recv_g,
):
    row, col, y, z = places()
    chip, core = lax.div(row, 2), lax.rem(row, 2)
    other = 1 - core
    partner = (chip * 2 + other, col)
    spots = {"r": row, "y": y, "z": z}

    def spot(i, which):
        return ring(chip, i, X) * 2 + which

    def place(digit):
        return spot(lax.div(digit, 2), lax.rem(core + lax.rem(digit, 2), 2))

    def beside(i):
        return (spot(i, core), col)

    def along(axis, i):
        target = ring(spots[axis], i, 8)
        if axis == "r":
            return target, (target, col)
        if axis == "y":
            return target, (row, target * Z + z)
        return target, (row, y * Z + target)

    def fetch(digit):
        q = place(digit)
        return pltpu.make_async_copy(dense_ref.at[q], tile.at[q], load.at[digit])

    def fetch_next(n, digits):
        fetch(lax.rem(digits, 8)).start()
        return lax.div(digits, 8)

    lax.fori_loop(0, 8, fetch_next, table(FORWARD))
    greet([(8, lambda i, axis=axis: along(axis, i)[1]) for axis in "ryz"])
    turned[...] = own_ref[...].astype(F32).T.astype(BF16)
    pl.semaphore_wait(pltpu.get_barrier_semaphore(), 21)

    def landed(dst, sends, recvs, n):
        remote(dst, dst, sends.at[n], recvs.at[n], partner).wait_recv()

    def far_first(body):
        def step(n, carry):
            body(4 + lax.div(n + 1, 2) * (1 - 2 * lax.rem(n, 2)))
            return carry

        lax.fori_loop(0, 7, step, 0)

    p = (send_p, recv_p)
    hops = [(turned, panel.at[row], partner)]
    hops += [(turned, panel.at[row], beside(i)) for i in (1, 2, 3)]
    hops += [(panel.at[spot(X - i, core)], panel.at[spot(X - i, core)], partner) for i in (1, 2, 3)]

    def came(n):
        chips, which = (0, other) if n == 0 else (X - n, core) if n < X else (2 * X - 1 - n, other)
        landed(panel.at[spot(chips, which)], *p, n)

    def hop(n):
        src, dst, device = hops[n]
        return remote(src, dst, send_p.at[n], recv_p.at[n], device)

    for n in (2, 1, 3, 0):
        hop(n).start()
    panel[row] = turned[...]
    acc[...] = jnp.zeros_like(acc)

    def multiply(n, digits):
        digit = lax.rem(digits, 8)
        fetch(digit).wait()

        @pl.when(n == 1)
        def _():
            came(0)

        @pl.when(n == 2)
        def _():
            came(1)
            hop(4).start()
            came(3)
            hop(6).start()

        @pl.when(n == 3)
        def _():
            came(4)

        @pl.when(n == 4)
        def _():
            came(2)
            hop(5).start()

        @pl.when(n == 5)
        def _():
            came(6)

        @pl.when(n == 7)
        def _():
            came(5)

        q = place(digit)
        acc[...] += lax.dot_general(
            panel[q], tile[q], (((1,), (1,)), ((), ())), preferred_element_type=F32
        )
        return lax.div(digits, 8)

    lax.fori_loop(0, 8, multiply, table(FORWARD))

    def launch(copies):
        def step(i):
            for axis, source, landing, send, recv in copies:
                target, device = along(axis, i)
                remote(source(target), landing.at[spots[axis]], send, recv, device).start()

        far_first(step)

    def seven(landing, send, recv):
        part_of = landing.at[pl.ds(0, 7)]
        return remote(part_of, part_of, send, recv, partner)

    me, first, second = (y, z, y, z), ("y", "z", "y", "z"), ("z", "y", "z", "y")
    them = (z, y, z, y)
    jobs = [
        [(first[h], lambda t, h=h: part.at[h, t], got1.at[h]) for h in range(4)],
        [(second[h], lambda t, h=h: sum1.at[h, t], got2.at[h]) for h in range(4)],
        [(second[h], lambda t, h=h: mine.at[h], wide.at[h]) for h in range(4)],
        [(first[h], lambda t, h=h: whole.at[h], users.at[h]) for h in range(4)],
    ]

    def users_start(stage, quarters):
        launch([jobs[stage][h] + (send_u.at[stage, h], recv_u.at[stage, h]) for h in quarters])

    def users_all(stage, h):
        return seven(jobs[stage][h][2], send_u.at[stage, h], recv_u.at[stage, h])

    def users_left(stage):
        for h in range(4):
            users_all(stage, h).wait_send()

    def summed(got):
        total = got[0].astype(F32)
        for k in range(1, 8):
            total = total + got[k].astype(F32)
        return total

    pairs = ((0, 1), (2, 3))
    for pair in pairs:
        for h in pair:
            for k in range(8):
                part[h, k] = acc[h * 64 : (h + 1) * 64, k * 128 : (k + 1) * 128].astype(BF16)
        users_start(0, pair)
    for h in range(4):
        got1[h, me[h]] = part[h, me[h]]
    for n in range(7):
        hop(n).wait_send()
    for pair in pairs:
        for h in pair:
            users_all(0, h).wait_recv()
            sum1[h] = summed(got1.at[h]).reshape(8, 8, 128)
        users_start(1, pair)
        for h in pair:
            got2[h, them[h]] = sum1[h, them[h]]
    users_left(0)
    for pair in pairs:
        for h in pair:
            users_all(1, h).wait_recv()
            mine[h] = summed(got2.at[h])
        users_start(2, pair)
        for h in pair:
            wide[h, them[h]] = mine[h]
    users_left(1)
    for pair in pairs:
        for h in pair:
            users_all(2, h).wait_recv()
            whole[h] = wide[h].reshape(64, 128).astype(BF16)
        users_start(3, pair)
        for h in pair:
            users[h, me[h]] = whole[h]
    users_left(2)
    for h in range(4):
        users_all(3, h).wait_recv()

    def lend(i):
        return remote(value.at[2 * i + 1], near.at[i], send_a.at[i], recv_a.at[i], partner)

    def pass_on(i):
        return remote(pack.at[i], far.at[i], send_b.at[i], recv_b.at[i], beside(i))

    def meet(i):
        landed(near.at[i], send_a, recv_a, i)
        near[i] = value[2 * i] + near[i]

    def transposed(n, digits):
        digit = lax.rem(digits, 8)
        left = jnp.concatenate(
            [jnp.concatenate([users[h, k] for k in range(8)], axis=1) for h in range(4)], axis=0
        )
        value[digit] = jnp.dot(left, tile[place(digit)], preferred_element_type=F32)
        for step, i in ((0, 2), (1, 1), (3, 3), (5, 0)):
            @pl.when(n == step)
            def _(i=i):
                lend(i).start()

        for step, i in ((3, 2), (5, 1), (6, 3)):
            @pl.when(n == step)
            def _(i=i):
                meet(i)
                pack[i] = near[i].astype(BF16)
                pass_on(i).start()

        return lax.div(digits, 8)

    lax.fori_loop(0, 8, transposed, table(BACKWARD))
    meet(0)
    users_left(3)
    for i in range(X):
        lend(i).wait_send()
    items = near[0]
    for i in (1, 3, 2):
        landed(far.at[i], send_b, recv_b, i)
        items = items + far[i].astype(F32)
    items_ref[...] = items

    gram = lax.dot_general(
        items, items, (((1,), (1,)), ((), ())), precision=HIGH, preferred_element_type=F32
    )
    for k in range(16):
        for c in range(2):
            cut[k // 2, (k % 2) * 2 + c] = gram[
                16 * k : 16 * k + 16, 128 * c : 128 * c + 128
            ].astype(BF16)

    spread = [
        ("r", lambda t: cut.at[t], gram1),
        ("y", lambda t: gsum1.at[t], gram2),
        ("z", lambda t: gsum2, gram3),
        ("y", lambda t: gsum3, gwide),
        ("r", lambda t: gwide, gram_ref),
    ]

    def spread_all(n):
        return seven(spread[n][2], send_g.at[n], recv_g.at[n])

    def move(n):
        axis, source, landing = spread[n]
        launch([spread[n] + (send_g.at[n], recv_g.at[n])])
        landing[spots[axis]] = source(spots[axis])[...]
        if n:
            spread_all(n - 1).wait_send()
        else:
            for i in (1, 2, 3):
                pass_on(i).wait_send()
        spread_all(n).wait_recv()

    move(0)
    gsum1[...] = summed(gram1).reshape(8, 8, 128)
    move(1)
    gsum2[...] = summed(gram2)
    move(2)
    gsum3[...] = summed(gram3)
    move(3)

    move(4)
    spread_all(4).wait_send()


def krylov(own, tile):
    cell = (8, 128)
    dma = pltpu.SemaphoreType.DMA
    pairs = [(7,), (4, 4), (X,), (X,), (5,)]
    return pl.pallas_call(
        krylov_kernel,
        out_shape=(
            jax.ShapeDtypeStruct((256, 256), F32),
            jax.ShapeDtypeStruct((8, 8) + cell, F32),
        ),
        in_specs=[vmem(), pl.BlockSpec(memory_space=pl.ANY)],
        out_specs=(vmem(), vmem()),
        scratch_shapes=[
            pltpu.VMEM((8, 1024, 256), BF16),
            pltpu.VMEM((8, 256, 256), BF16),
            pltpu.VMEM((256, 256), BF16),
            pltpu.VMEM((256, 1024), F32),
            pltpu.VMEM((4, 8, 64, 128), BF16),
            pltpu.VMEM((4, 8, 64, 128), BF16),
            pltpu.VMEM((4, 8) + cell, F32),
            pltpu.VMEM((4, 8) + cell, F32),
            pltpu.VMEM((4,) + cell, F32),
            pltpu.VMEM((4, 8) + cell, F32),
            pltpu.VMEM((4, 64, 128), BF16),
            pltpu.VMEM((4, 8, 64, 128), BF16),
            pltpu.VMEM((8, 256, 256), F32),
            pltpu.VMEM((X, 256, 256), F32),
            pltpu.VMEM((X, 256, 256), BF16),
            pltpu.VMEM((X, 256, 256), BF16),
            pltpu.VMEM((8, 4, 16, 128), BF16),
            pltpu.VMEM((8, 4, 16, 128), BF16),
            pltpu.VMEM((8,) + cell, F32),
            pltpu.VMEM((8,) + cell, F32),
            pltpu.VMEM(cell, F32),
            pltpu.VMEM((8,) + cell, F32),
            pltpu.VMEM(cell, F32),
            pltpu.VMEM((8,) + cell, F32),
            dma((8,)),
        ]
        + [dma(shape) for shape in pairs for _ in range(2)],
        compiler_params=pltpu.CompilerParams(
            collective_id=0, has_side_effects=True, vmem_limit_bytes=ROOM
        ),
        name="krylov",
    )(own, tile)


PANEL = 32
N = 256


def factor_kernel(gram_ref, items_ref, basis_ref, factor_ref, a_ref, d_ref):
    for k in range(32):
        for c in range(2):
            a_ref[8 * k : 8 * k + 8, 128 * c : 128 * c + 128] = gram_ref[
                k // 4, (k // 2 % 2) * 4 + c * 2 + k % 2
            ]

    for base in range(0, N, PANEL):
        w = a_ref[base : base + PANEL, :]
        d = jnp.zeros((PANEL, 128), F32)
        for low in range(0, PANEL, 8):
            part = w[low:, :]
            size = PANEL - low
            lane = lax.broadcasted_iota(jnp.int32, (size, N), 1)
            sub = lax.broadcasted_iota(jnp.int32, (size, N), 0) + low
            sub1 = sub[:, :128]
            first = base + low
            columns = [
                jnp.broadcast_to(part[:, first + b : first + b + 1], (size, 128)) for b in range(8)
            ]
            d_part = d[low:, :]
            for a in range(0, 8, 2):
                r = low + a
                one, two = columns[a], columns[a + 1]
                p11, p12 = one[a : a + 1, :], two[a : a + 1, :]
                p21, p22 = one[a + 1 : a + 2, :], two[a + 1 : a + 2, :]
                inv1 = 1.0 / p11
                inv2 = p11 * (1.0 / (p11 * p22 - p21 * p12))
                ratio = p21 * inv1
                m1 = jnp.where(sub1 > r, one * inv1, 0.0)
                m2 = jnp.where(sub1 > r + 1, (two - m1 * p12) * inv2, 0.0)
                for b in range(a + 2, 8):
                    top = columns[b][a : a + 1, :]
                    next_top = columns[b][a + 1 : a + 2, :] - ratio * top
                    columns[b] = columns[b] - m1 * top - m2 * next_top
                lane1 = lane[:1]
                line1 = jnp.where(lane1 == base + r, 1.0, part[a : a + 1, :])
                ratio2 = jnp.concatenate([ratio, ratio], axis=1)
                line2 = jnp.where(lane1 == base + r, 0.0, part[a + 1 : a + 2, :]) - ratio2 * line1
                line1 = jnp.where(lane1 == base + r + 1, 0.0, line1)
                line2 = jnp.where(lane1 == base + r + 1, 1.0, line2)
                gone = ((lane == base + r) & (sub > r)) | ((lane == base + r + 1) & (sub > r + 1))
                part = (
                    jnp.where(gone, 0.0, part)
                    - jnp.concatenate([m1, m1], axis=1) * line1
                    - jnp.concatenate([m2, m2], axis=1) * line2
                )
                d_part = jnp.where(sub1 == r, p11, d_part)
                d_part = jnp.where(sub1 == r + 1, p22 - ratio * p12, d_part)
            w = part if low == 0 else jnp.concatenate([w[:low], part], axis=0)
            d = d_part if low == 0 else jnp.concatenate([d[:low], d_part], axis=0)
        a_ref[base : base + PANEL, :] = w
        d_ref[base : base + PANEL, :] = d
        after = base + PANEL
        if after == N:
            break
        lane = lax.broadcasted_iota(jnp.int32, (PANEL, N), 1)
        sub = lax.broadcasted_iota(jnp.int32, (PANEL, N), 0) + base
        scaled = jnp.where(lane >= after, w / jnp.concatenate([d, d], axis=1), 0.0).T
        inside = (lane < after) & (lane >= sub)
        right = jnp.where(inside, jnp.where(lane == sub, 1.0, 0.0), w)
        for top, bottom in ((after, after + PANEL), (after + PANEL, N)):
            if top < bottom:
                lane = lax.broadcasted_iota(jnp.int32, (bottom - top, N), 1)
                kept = jnp.where((lane >= base) & (lane < after), 0.0, a_ref[top:bottom, :])
                a_ref[top:bottom, :] = kept - jnp.dot(
                    scaled[top:bottom], right, precision=HIGH, preferred_element_type=F32
                )

    lane = lax.broadcasted_iota(jnp.int32, (N, N), 1)
    sub = lax.broadcasted_iota(jnp.int32, (N, N), 0)
    pivots = d_ref[...]
    scale = 1.0 / jnp.sqrt(pivots)
    scale = jnp.concatenate([scale, scale], axis=1)
    full = jnp.where(lane == sub, jnp.concatenate([pivots, pivots], axis=1), a_ref[...])
    factor_ref[...] = jnp.where(lane >= sub, full, 0.0) * scale
    inverse = jnp.where(lane < sub, full, jnp.where(lane == sub, 1.0, 0.0)) * scale
    basis_ref[...] = jnp.dot(
        inverse, items_ref[...], precision=HIGH, preferred_element_type=F32
    ).T


def factor_call(gram, items):
    return pl.pallas_call(
        factor_kernel,
        out_shape=(
            jax.ShapeDtypeStruct((256, 256), F32),
            jax.ShapeDtypeStruct((256, 256), F32),
        ),
        in_specs=[vmem(), vmem()],
        out_specs=(vmem(), vmem()),
        scratch_shapes=[pltpu.VMEM((N, N), F32), pltpu.VMEM((N, 128), F32)],
        compiler_params=pltpu.CompilerParams(vmem_limit_bytes=ROOM),
        name="factor",
    )(gram, items)


def local(blocks, block_row, block_col, counts, start_block):
    tile = dense_tile(block_row[0, 0], block_col[0, 0], counts[0], blocks[0, 0])
    items, gram = krylov(start_block, tile)
    return factor_call(gram, items)


def solution(mesh):
    return jax.shard_map(
        local,
        mesh=mesh,
        in_specs=(
            P("rows", "cols", None, None, None),
            P("rows", "cols", None),
            P("rows", "cols", None),
            P("rows", "cols"),
            P(("cols", "rows"), None),
        ),
        out_specs=(P(("cols", "rows"), None), P()),
        check_vma=False,
    )
```

```python
import jax
import jax.numpy as jnp
from jax import lax
from jax.experimental import pallas as pl
from jax.experimental.pallas import tpu as pltpu
from jax.sharding import PartitionSpec as P

MESH = pl.DeviceIdType.MESH
F32 = jnp.float32
BF16 = jnp.bfloat16
HIGH = lax.Precision.HIGHEST
LIMIT = 63 * 1024 * 1024
ROOM = 53 * 1024 * 1024
NB = 96
GROUP = 8
STEP = 24
X, Y, Z = 4, 8, 8
HALF = 128


def vmem():
    return pl.BlockSpec(memory_space=pltpu.VMEM)


def smem():
    return pl.BlockSpec(memory_space=pltpu.SMEM)


def remote(src, dst, send, recv, device):
    return pltpu.make_async_remote_copy(
        src_ref=src, dst_ref=dst, send_sem=send, recv_sem=recv, device_id=device, device_id_type=MESH
    )


def places():
    row = lax.axis_index("rows")
    col = lax.axis_index("cols")
    return row, col, lax.div(col, Z), lax.rem(col, Z)


def each(count, body):
    def step(i, carry):
        body(i)
        return carry

    lax.fori_loop(1, count, step, 0)


def ring(me, i, count):
    return lax.rem(me + i, count)


def greet(makers):
    barrier = pltpu.get_barrier_semaphore()
    for count, device in makers:
        each(
            count,
            lambda i, device=device: pl.semaphore_signal(
                barrier, inc=1, device_id=device(i), device_id_type=MESH
            ),
        )


def dense_kernel(rows_ref, cols_ref, count_ref, tiles_ref, out_ref, acc_ref, pack_ref, sem):
    step = pl.program_id(0)

    @pl.when(step == 0)
    def _():
        acc_ref[...] = jnp.zeros_like(acc_ref)

    count = count_ref[0, 0]

    def group(g, carry):
        for j in range(GROUP):
            at = g * GROUP + j
            slot = step * STEP + at
            tile = jnp.where(slot < count, tiles_ref[at].astype(F32), 0.0)
            col = cols_ref[slot]
            acc_ref[lax.div(col, 2), lax.rem(col, 2), rows_ref[slot]] += tile
        return carry

    lax.fori_loop(0, STEP // GROUP, group, 0)

    @pl.when(step == NB // STEP - 1)
    def _():
        def out_copy(q):
            return pltpu.make_async_copy(pack_ref.at[q], out_ref.at[q], sem.at[q])

        def chunk(q, carry):
            def block(u, inner):
                rows = pl.ds(pl.multiple_of(u * 128, 128), 128)
                for e in range(2):
                    pack_ref[q, rows, e * 128 : (e + 1) * 128] = acc_ref[q, e, u].astype(BF16)
                return inner

            lax.fori_loop(0, 8, block, 0)
            out_copy(q).start()
            return carry

        def finish(q, carry):
            out_copy(q).wait()
            return carry

        lax.fori_loop(0, 8, chunk, 0)
        lax.fori_loop(0, 8, finish, 0)


def dense_tile(rows, cols, count, tiles):
    return pl.pallas_call(
        dense_kernel,
        grid=(NB // STEP,),
        out_shape=jax.ShapeDtypeStruct((8, 1024, 256), BF16),
        in_specs=[smem(), smem(), smem(), pl.BlockSpec((STEP, 128, 128), lambda i: (i, 0, 0))],
        out_specs=pl.BlockSpec(memory_space=pl.ANY),
        scratch_shapes=[
            pltpu.VMEM((8, 2, 8, 128, 128), F32),
            pltpu.VMEM((8, 1024, 256), BF16),
            pltpu.SemaphoreType.DMA((8,)),
        ],
        compiler_params=pltpu.CompilerParams(
            dimension_semantics=("arbitrary",), vmem_limit_bytes=LIMIT
        ),
        name="dense_tile",
    )(rows, cols, count, tiles)


HALF = 128
def table(digits):
    return sum(digit * 8**n for n, digit in enumerate(digits))


FORWARD = (0, 1, 6, 7, 2, 3, 4, 5)
BACKWARD = (5, 3, 4, 7, 2, 1, 6, 0)


def krylov_kernel(
    own_ref, dense_ref, items_ref, gram_ref,
    tile, panel, turned, acc, part, got1, sum1, got2, mine, wide, whole, users,
    value, near, pack, relay, far, cut, gram1, gsum1, gram2, gsum2, gram3, gsum3, gwide,
    load, send_p, recv_p, send_u, recv_u, send_a, recv_a, send_b, recv_b, send_g, recv_g,
):
    row, col, y, z = places()
    chip, core = lax.div(row, 2), lax.rem(row, 2)
    other = 1 - core
    partner = (chip * 2 + other, col)
    spots = {"r": row, "y": y, "z": z}

    low, high = pl.ds(0, HALF), pl.ds(HALF, HALF)

    def spot(i, which):
        return ring(chip, i, X) * 2 + which

    def place(digit):
        return spot(lax.div(digit, 2), lax.rem(core + lax.rem(digit, 2), 2))

    def beside(i):
        return (spot(i, core), col)

    def along(axis, i):
        target = ring(spots[axis], i, 8)
        if axis == "r":
            return target, (target, col)
        if axis == "y":
            return target, (row, target * Z + z)
        return target, (row, y * Z + target)

    def fetch(digit):
        q = place(digit)
        return pltpu.make_async_copy(dense_ref.at[q], tile.at[q], load.at[digit])

    def fetch_next(n, digits):
        fetch(lax.rem(digits, 8)).start()
        return lax.div(digits, 8)

    lax.fori_loop(0, 8, fetch_next, table(FORWARD))
    greet([(8, lambda i, axis=axis: along(axis, i)[1]) for axis in "ryz"])
    turned[...] = own_ref[...].astype(F32).T.astype(BF16)
    pl.semaphore_wait(pltpu.get_barrier_semaphore(), 21)

    def landed(dst, sends, recvs, n):
        remote(dst, dst, sends.at[n], recvs.at[n], partner).wait_recv()

    def far_first(body):
        def step(n, carry):
            body(4 + lax.div(n + 1, 2) * (1 - 2 * lax.rem(n, 2)))
            return carry

        lax.fori_loop(0, 7, step, 0)

    prev, nxt, over = spot(3, core), spot(1, core), spot(2, core)
    last = spot(2, other)
    p = (send_p, recv_p)
    hops = [
        (turned, panel.at[row], partner),
        (turned, panel.at[row], beside(1)),
        (turned, panel.at[row], beside(3)),
        (panel.at[prev, low], panel.at[prev, low], beside(1)),
        (panel.at[nxt, high], panel.at[nxt, high], beside(3)),
        (panel.at[prev], panel.at[prev], partner),
        (panel.at[nxt], panel.at[nxt], partner),
        (panel.at[over, low], panel.at[over, low], partner),
        (panel.at[over, high], panel.at[over, high], partner),
    ]

    def hop(n):
        src, dst, device = hops[n]
        return remote(src, dst, send_p.at[n], recv_p.at[n], device)

    for n in (1, 2, 0):
        hop(n).start()
    panel[row] = turned[...]
    acc[...] = jnp.zeros_like(acc)

    def multiply(n, digits):
        digit = lax.rem(digits, 8)
        fetch(digit).wait()

        @pl.when(n == 1)
        def _():
            landed(panel.at[spot(0, other)], *p, 0)

        @pl.when(n == 2)
        def _():
            landed(panel.at[prev], *p, 1)
            hop(3).start()
            landed(panel.at[nxt], *p, 2)
            hop(4).start()
            hop(5).start()
            hop(6).start()

        @pl.when(n == 3)
        def _():
            landed(panel.at[spot(3, other)], *p, 5)

        @pl.when(n == 4)
        def _():
            landed(panel.at[over, low], *p, 3)
            hop(7).start()
            landed(panel.at[over, high], *p, 4)
            hop(8).start()

        @pl.when(n == 5)
        def _():
            landed(panel.at[spot(1, other)], *p, 6)

        @pl.when(n == 7)
        def _():
            landed(panel.at[last, low], *p, 7)
            landed(panel.at[last, high], *p, 8)

        q = place(digit)
        acc[...] += lax.dot_general(
            panel[q], tile[q], (((1,), (1,)), ((), ())), preferred_element_type=F32
        )
        return lax.div(digits, 8)

    lax.fori_loop(0, 8, multiply, table(FORWARD))

    def launch(copies):
        def step(i):
            for axis, source, landing, send, recv in copies:
                target, device = along(axis, i)
                remote(source(target), landing.at[spots[axis]], send, recv, device).start()

        far_first(step)

    def seven(landing, send, recv):
        part_of = landing.at[pl.ds(0, 7)]
        return remote(part_of, part_of, send, recv, partner)

    me, first, second = (y, z, y, z), ("y", "z", "y", "z"), ("z", "y", "z", "y")
    them = (z, y, z, y)
    jobs = [
        [(first[h], lambda t, h=h: part.at[h, t], got1.at[h]) for h in range(4)],
        [(second[h], lambda t, h=h: sum1.at[h, t], got2.at[h]) for h in range(4)],
        [(second[h], lambda t, h=h: mine.at[h], wide.at[h]) for h in range(4)],
        [(first[h], lambda t, h=h: whole.at[h], users.at[h]) for h in range(4)],
    ]

    def users_start(stage, quarters):
        launch([jobs[stage][h] + (send_u.at[stage, h], recv_u.at[stage, h]) for h in quarters])

    def users_all(stage, h):
        return seven(jobs[stage][h][2], send_u.at[stage, h], recv_u.at[stage, h])

    def users_left(stage):
        for h in range(4):
            users_all(stage, h).wait_send()

    def summed(got):
        total = got[0].astype(F32)
        for k in range(1, 8):
            total = total + got[k].astype(F32)
        return total

    pairs = ((0, 1), (2, 3))
    for pair in pairs:
        for h in pair:
            for k in range(8):
                part[h, k] = acc[h * 64 : (h + 1) * 64, k * 128 : (k + 1) * 128].astype(BF16)
        users_start(0, pair)
    for h in range(4):
        got1[h, me[h]] = part[h, me[h]]
    for n in range(9):
        hop(n).wait_send()
    for pair in pairs:
        for h in pair:
            users_all(0, h).wait_recv()
            sum1[h] = summed(got1.at[h]).reshape(8, 8, 128)
        users_start(1, pair)
        for h in pair:
            got2[h, them[h]] = sum1[h, them[h]]
    users_left(0)
    for pair in pairs:
        for h in pair:
            users_all(1, h).wait_recv()
            mine[h] = summed(got2.at[h])
        users_start(2, pair)
        for h in pair:
            wide[h, them[h]] = mine[h]
    users_left(1)
    for pair in pairs:
        for h in pair:
            users_all(2, h).wait_recv()
            whole[h] = wide[h].reshape(64, 128).astype(BF16)
        users_start(3, pair)
        for h in pair:
            users[h, me[h]] = whole[h]
    users_left(2)
    for h in range(4):
        users_all(3, h).wait_recv()

    b = (send_b, recv_b)

    def lend(i):
        return remote(value.at[2 * i + 1], near.at[i], send_a.at[i], recv_a.at[i], partner)

    moves = [
        (pack.at[2, low], relay.at[0], beside(1)),
        (pack.at[2, high], relay.at[1], beside(3)),
        (pack.at[1, high], far.at[0, high], beside(1)),
        (pack.at[3, low], far.at[1, low], beside(3)),
        (pack.at[1, low], far.at[0, low], beside(1)),
        (pack.at[3, high], far.at[1, high], beside(3)),
    ]

    def pass_on(n):
        src, dst, device = moves[n]
        return remote(src, dst, send_b.at[n], recv_b.at[n], device)

    def meet(i):
        landed(near.at[i], send_a, recv_a, i)
        near[i] = value[2 * i] + near[i]

    def transposed(n, digits):
        digit = lax.rem(digits, 8)
        left = jnp.concatenate(
            [jnp.concatenate([users[h, k] for k in range(8)], axis=1) for h in range(4)], axis=0
        )
        value[digit] = jnp.dot(left, tile[place(digit)], preferred_element_type=F32)
        for step, i in ((0, 2), (1, 1), (3, 3), (5, 0)):
            @pl.when(n == step)
            def _(i=i):
                lend(i).start()

        @pl.when(n == 3)
        def _():
            meet(2)
            pack[2] = near[2].astype(BF16)
            pass_on(0).start()
            pass_on(1).start()

        @pl.when(n == 5)
        def _():
            meet(1)
            pack[1, HALF:] = near[1, HALF:].astype(BF16)
            pass_on(2).start()

        @pl.when(n == 6)
        def _():
            meet(3)
            pack[3, :HALF] = near[3, :HALF].astype(BF16)
            pass_on(3).start()

        return lax.div(digits, 8)

    lax.fori_loop(0, 8, transposed, table(BACKWARD))
    landed(relay.at[0], *b, 0)
    pack[1, :HALF] = (near[1, :HALF] + relay[0].astype(F32)).astype(BF16)
    pass_on(4).start()
    landed(relay.at[1], *b, 1)
    pack[3, HALF:] = (near[3, HALF:] + relay[1].astype(F32)).astype(BF16)
    pass_on(5).start()
    meet(0)

    users_left(3)
    for i in range(X):
        lend(i).wait_send()
    landed(far.at[0, high], *b, 2)
    landed(far.at[1, low], *b, 3)
    landed(far.at[0, low], *b, 4)
    landed(far.at[1, high], *b, 5)
    items = near[0] + far[0].astype(F32) + far[1].astype(F32)
    items_ref[...] = items

    gram = lax.dot_general(
        items, items, (((1,), (1,)), ((), ())), precision=HIGH, preferred_element_type=F32
    )
    for k in range(16):
        for c in range(2):
            cut[k // 2, (k % 2) * 2 + c] = gram[
                16 * k : 16 * k + 16, 128 * c : 128 * c + 128
            ].astype(BF16)

    spread = [
        ("r", lambda t: cut.at[t], gram1),
        ("y", lambda t: gsum1.at[t], gram2),
        ("z", lambda t: gsum2, gram3),
        ("y", lambda t: gsum3, gwide),
        ("r", lambda t: gwide, gram_ref),
    ]

    def spread_all(n):
        return seven(spread[n][2], send_g.at[n], recv_g.at[n])

    def move(n):
        axis, source, landing = spread[n]
        launch([spread[n] + (send_g.at[n], recv_g.at[n])])
        landing[spots[axis]] = source(spots[axis])[...]
        if n:
            spread_all(n - 1).wait_send()
        else:
            for k in range(6):
                pass_on(k).wait_send()
        spread_all(n).wait_recv()

    move(0)
    gsum1[...] = summed(gram1).reshape(8, 8, 128)
    move(1)
    gsum2[...] = summed(gram2)
    move(2)
    gsum3[...] = summed(gram3)
    move(3)

    move(4)
    spread_all(4).wait_send()


def krylov(own, tile):
    cell = (8, 128)
    dma = pltpu.SemaphoreType.DMA
    pairs = [(9,), (4, 4), (X,), (6,), (5,)]
    return pl.pallas_call(
        krylov_kernel,
        out_shape=(
            jax.ShapeDtypeStruct((256, 256), F32),
            jax.ShapeDtypeStruct((8, 8) + cell, F32),
        ),
        in_specs=[vmem(), pl.BlockSpec(memory_space=pl.ANY)],
        out_specs=(vmem(), vmem()),
        scratch_shapes=[
            pltpu.VMEM((8, 1024, 256), BF16),
            pltpu.VMEM((8, 256, 256), BF16),
            pltpu.VMEM((256, 256), BF16),
            pltpu.VMEM((256, 1024), F32),
            pltpu.VMEM((4, 8, 64, 128), BF16),
            pltpu.VMEM((4, 8, 64, 128), BF16),
            pltpu.VMEM((4, 8) + cell, F32),
            pltpu.VMEM((4, 8) + cell, F32),
            pltpu.VMEM((4,) + cell, F32),
            pltpu.VMEM((4, 8) + cell, F32),
            pltpu.VMEM((4, 64, 128), BF16),
            pltpu.VMEM((4, 8, 64, 128), BF16),
            pltpu.VMEM((8, 256, 256), F32),
            pltpu.VMEM((X, 256, 256), F32),
            pltpu.VMEM((X, 256, 256), BF16),
            pltpu.VMEM((2, HALF, 256), BF16),
            pltpu.VMEM((2, 256, 256), BF16),
            pltpu.VMEM((8, 4, 16, 128), BF16),
            pltpu.VMEM((8, 4, 16, 128), BF16),
            pltpu.VMEM((8,) + cell, F32),
            pltpu.VMEM((8,) + cell, F32),
            pltpu.VMEM(cell, F32),
            pltpu.VMEM((8,) + cell, F32),
            pltpu.VMEM(cell, F32),
            pltpu.VMEM((8,) + cell, F32),
            dma((8,)),
        ]
        + [dma(shape) for shape in pairs for _ in range(2)],
        compiler_params=pltpu.CompilerParams(
            collective_id=0, has_side_effects=True, vmem_limit_bytes=ROOM
        ),
        name="krylov",
    )(own, tile)


PANEL = 32
N = 256


def inverted(x):
    guess = pl.reciprocal(x, approx=True)
    guess = guess * (2.0 - x * guess)
    return guess * (2.0 - x * guess)


def factor_kernel(gram_ref, items_ref, basis_ref, factor_ref, a_ref, d_ref):
    for k in range(32):
        for c in range(2):
            a_ref[8 * k : 8 * k + 8, 128 * c : 128 * c + 128] = gram_ref[
                k // 4, (k // 2 % 2) * 4 + c * 2 + k % 2
            ]

    for base in range(0, N, PANEL):
        w = a_ref[base : base + PANEL, :]
        d = jnp.zeros((PANEL, 128), F32)
        for low in range(0, PANEL, 8):
            part = w[low:, :]
            size = PANEL - low
            lane = lax.broadcasted_iota(jnp.int32, (size, N), 1)
            sub = lax.broadcasted_iota(jnp.int32, (size, N), 0) + low
            sub1 = sub[:, :128]
            first = base + low
            columns = [
                jnp.broadcast_to(part[:, first + b : first + b + 1], (size, 128)) for b in range(8)
            ]
            d_part = d[low:, :]
            for a in range(0, 8, 2):
                r = low + a
                one, two = columns[a], columns[a + 1]
                p11, p12 = one[a : a + 1, :], two[a : a + 1, :]
                p21, p22 = one[a + 1 : a + 2, :], two[a + 1 : a + 2, :]
                inv1 = inverted(p11)
                inv2 = p11 * inverted(p11 * p22 - p21 * p12)
                ratio = p21 * inv1
                m1 = jnp.where(sub1 > r, one * inv1, 0.0)
                m2 = jnp.where(sub1 > r + 1, (two - m1 * p12) * inv2, 0.0)
                for b in range(a + 2, 8):
                    top = columns[b][a : a + 1, :]
                    next_top = columns[b][a + 1 : a + 2, :] - ratio * top
                    columns[b] = columns[b] - m1 * top - m2 * next_top
                lane1 = lane[:1]
                line1 = jnp.where(lane1 == base + r, 1.0, part[a : a + 1, :])
                ratio2 = jnp.concatenate([ratio, ratio], axis=1)
                line2 = jnp.where(lane1 == base + r, 0.0, part[a + 1 : a + 2, :]) - ratio2 * line1
                line1 = jnp.where(lane1 == base + r + 1, 0.0, line1)
                line2 = jnp.where(lane1 == base + r + 1, 1.0, line2)
                gone = ((lane == base + r) & (sub > r)) | ((lane == base + r + 1) & (sub > r + 1))
                part = (
                    jnp.where(gone, 0.0, part)
                    - jnp.concatenate([m1, m1], axis=1) * line1
                    - jnp.concatenate([m2, m2], axis=1) * line2
                )
                d_part = jnp.where(sub1 == r, p11, d_part)
                d_part = jnp.where(sub1 == r + 1, p22 - ratio * p12, d_part)
            w = part if low == 0 else jnp.concatenate([w[:low], part], axis=0)
            d = d_part if low == 0 else jnp.concatenate([d[:low], d_part], axis=0)
        a_ref[base : base + PANEL, :] = w
        d_ref[base : base + PANEL, :] = d
        after = base + PANEL
        if after == N:
            break
        lane = lax.broadcasted_iota(jnp.int32, (PANEL, N), 1)
        sub = lax.broadcasted_iota(jnp.int32, (PANEL, N), 0) + base
        scaled = jnp.where(lane >= after, w / jnp.concatenate([d, d], axis=1), 0.0).T
        inside = (lane < after) & (lane >= sub)
        right = jnp.where(inside, jnp.where(lane == sub, 1.0, 0.0), w)
        for top, bottom in ((after, after + PANEL), (after + PANEL, N)):
            if top < bottom:
                lane = lax.broadcasted_iota(jnp.int32, (bottom - top, N), 1)
                kept = jnp.where((lane >= base) & (lane < after), 0.0, a_ref[top:bottom, :])
                a_ref[top:bottom, :] = kept - jnp.dot(
                    scaled[top:bottom], right, precision=HIGH, preferred_element_type=F32
                )

    lane = lax.broadcasted_iota(jnp.int32, (N, N), 1)
    sub = lax.broadcasted_iota(jnp.int32, (N, N), 0)
    pivots = d_ref[...]
    scale = 1.0 / jnp.sqrt(pivots)
    scale = jnp.concatenate([scale, scale], axis=1)
    full = jnp.where(lane == sub, jnp.concatenate([pivots, pivots], axis=1), a_ref[...])
    factor_ref[...] = jnp.where(lane >= sub, full, 0.0) * scale
    inverse = jnp.where(lane < sub, full, jnp.where(lane == sub, 1.0, 0.0)) * scale
    basis_ref[...] = jnp.dot(
        inverse, items_ref[...], precision=HIGH, preferred_element_type=F32
    ).T


def factor_call(gram, items):
    return pl.pallas_call(
        factor_kernel,
        out_shape=(
            jax.ShapeDtypeStruct((256, 256), F32),
            jax.ShapeDtypeStruct((256, 256), F32),
        ),
        in_specs=[vmem(), vmem()],
        out_specs=(vmem(), vmem()),
        scratch_shapes=[pltpu.VMEM((N, N), F32), pltpu.VMEM((N, 128), F32)],
        compiler_params=pltpu.CompilerParams(vmem_limit_bytes=ROOM),
        name="factor",
    )(gram, items)


def local(blocks, block_row, block_col, counts, start_block):
    tile = dense_tile(block_row[0, 0], block_col[0, 0], counts, blocks[0, 0])
    items, gram = krylov(start_block, tile)
    return factor_call(gram, items)


def solution(mesh):
    return jax.shard_map(
        local,
        mesh=mesh,
        in_specs=(
            P("rows", "cols", None, None, None),
            P("rows", "cols", None),
            P("rows", "cols", None),
            P("rows", "cols"),
            P(("cols", "rows"), None),
        ),
        out_specs=(P(("cols", "rows"), None), P()),
        check_vma=False,
    )
```

```python
import jax
import jax.numpy as jnp
from jax import lax
from jax.experimental import pallas as pl
from jax.experimental.pallas import tpu as pltpu
from jax.sharding import PartitionSpec as P

MESH = pl.DeviceIdType.MESH
F32 = jnp.float32
BF16 = jnp.bfloat16
HIGH = lax.Precision.HIGHEST
LIMIT = 63 * 1024 * 1024
ROOM = 53 * 1024 * 1024
NB = 96
GROUP = 8
STEP = 24
X, Y, Z = 4, 8, 8
HALF = 128


def vmem():
    return pl.BlockSpec(memory_space=pltpu.VMEM)


def smem():
    return pl.BlockSpec(memory_space=pltpu.SMEM)


def remote(src, dst, send, recv, device):
    return pltpu.make_async_remote_copy(
        src_ref=src, dst_ref=dst, send_sem=send, recv_sem=recv, device_id=device, device_id_type=MESH
    )


def places():
    row = lax.axis_index("rows")
    col = lax.axis_index("cols")
    return row, col, lax.div(col, Z), lax.rem(col, Z)


def each(count, body):
    def step(i, carry):
        body(i)
        return carry

    lax.fori_loop(1, count, step, 0)


def ring(me, i, count):
    return lax.rem(me + i, count)


def greet(makers):
    barrier = pltpu.get_barrier_semaphore()
    for count, device in makers:
        each(
            count,
            lambda i, device=device: pl.semaphore_signal(
                barrier, inc=1, device_id=device(i), device_id_type=MESH
            ),
        )


def dense_kernel(rows_ref, cols_ref, count_ref, tiles_ref, out_ref, acc_ref, pack_ref, sem):
    step = pl.program_id(0)

    @pl.when(step == 0)
    def _():
        acc_ref[...] = jnp.zeros_like(acc_ref)

    count = count_ref[0, 0]

    def group(g, carry):
        for j in range(GROUP):
            at = g * GROUP + j
            slot = step * STEP + at
            tile = jnp.where(slot < count, tiles_ref[at].astype(F32), 0.0)
            col = cols_ref[slot]
            acc_ref[lax.div(col, 2), lax.rem(col, 2), rows_ref[slot]] += tile
        return carry

    lax.fori_loop(0, STEP // GROUP, group, 0)

    @pl.when(step == NB // STEP - 1)
    def _():
        def out_copy(q):
            return pltpu.make_async_copy(pack_ref.at[q], out_ref.at[q], sem.at[q])

        def chunk(q, carry):
            def block(u, inner):
                rows = pl.ds(pl.multiple_of(u * 128, 128), 128)
                for e in range(2):
                    pack_ref[q, rows, e * 128 : (e + 1) * 128] = acc_ref[q, e, u].astype(BF16)
                return inner

            lax.fori_loop(0, 8, block, 0)
            out_copy(q).start()
            return carry

        def finish(q, carry):
            out_copy(q).wait()
            return carry

        lax.fori_loop(0, 8, chunk, 0)
        lax.fori_loop(0, 8, finish, 0)


def dense_tile(rows, cols, count, tiles):
    return pl.pallas_call(
        dense_kernel,
        grid=(NB // STEP,),
        out_shape=jax.ShapeDtypeStruct((8, 1024, 256), BF16),
        in_specs=[smem(), smem(), smem(), pl.BlockSpec((STEP, 128, 128), lambda i: (i, 0, 0))],
        out_specs=pl.BlockSpec(memory_space=pl.ANY),
        scratch_shapes=[
            pltpu.VMEM((8, 2, 8, 128, 128), F32),
            pltpu.VMEM((8, 1024, 256), BF16),
            pltpu.SemaphoreType.DMA((8,)),
        ],
        compiler_params=pltpu.CompilerParams(
            dimension_semantics=("arbitrary",), vmem_limit_bytes=LIMIT
        ),
        name="dense_tile",
    )(rows, cols, count, tiles)


HALF = 128
def table(digits):
    return sum(digit * 8**n for n, digit in enumerate(digits))


FORWARD = (0, 1, 6, 7, 2, 3, 4, 5)
BACKWARD = (5, 3, 4, 7, 2, 1, 6, 0)


def krylov_kernel(
    own_ref, dense_ref, items_ref, gram_ref,
    tile, panel, turned, acc, part, got1, sum1, got2, mine, wide, whole, users,
    value, near, pack, relay, far, cut, gram1, gsum1, gram2, gsum2, gram3, gsum3, gwide,
    load, send_p, recv_p, send_u, recv_u, send_a, recv_a, send_b, recv_b, send_g, recv_g,
):
    row, col, y, z = places()
    chip, core = lax.div(row, 2), lax.rem(row, 2)
    other = 1 - core
    partner = (chip * 2 + other, col)
    spots = {"r": row, "y": y, "z": z}

    low, high = pl.ds(0, HALF), pl.ds(HALF, HALF)

    def spot(i, which):
        return ring(chip, i, X) * 2 + which

    def place(digit):
        return spot(lax.div(digit, 2), lax.rem(core + lax.rem(digit, 2), 2))

    def beside(i):
        return (spot(i, core), col)

    def along(axis, i):
        target = ring(spots[axis], i, 8)
        if axis == "r":
            return target, (target, col)
        if axis == "y":
            return target, (row, target * Z + z)
        return target, (row, y * Z + target)

    def fetch(digit):
        q = place(digit)
        return pltpu.make_async_copy(dense_ref.at[q], tile.at[q], load.at[digit])

    def fetch_next(n, digits):
        fetch(lax.rem(digits, 8)).start()
        return lax.div(digits, 8)

    lax.fori_loop(0, 8, fetch_next, table(FORWARD))
    greet([(8, lambda i, axis=axis: along(axis, i)[1]) for axis in "ryz"])
    turned[...] = own_ref[...].astype(F32).T.astype(BF16)
    pl.semaphore_wait(pltpu.get_barrier_semaphore(), 21)

    def landed(dst, sends, recvs, n):
        remote(dst, dst, sends.at[n], recvs.at[n], partner).wait_recv()

    def far_first(body):
        def step(n, carry):
            body(4 + lax.div(n + 1, 2) * (1 - 2 * lax.rem(n, 2)))
            return carry

        lax.fori_loop(0, 7, step, 0)

    prev, nxt, over = spot(3, core), spot(1, core), spot(2, core)
    last = spot(2, other)
    p = (send_p, recv_p)
    hops = [
        (turned, panel.at[row], partner),
        (turned, panel.at[row], beside(1)),
        (turned, panel.at[row], beside(3)),
        (panel.at[prev, low], panel.at[prev, low], beside(1)),
        (panel.at[nxt, high], panel.at[nxt, high], beside(3)),
        (panel.at[prev], panel.at[prev], partner),
        (panel.at[nxt], panel.at[nxt], partner),
        (panel.at[over, low], panel.at[over, low], partner),
        (panel.at[over, high], panel.at[over, high], partner),
    ]

    def hop(n):
        src, dst, device = hops[n]
        return remote(src, dst, send_p.at[n], recv_p.at[n], device)

    for n in (1, 2, 0):
        hop(n).start()
    panel[row] = turned[...]
    acc[...] = jnp.zeros_like(acc)

    def multiply(n, digits):
        digit = lax.rem(digits, 8)
        fetch(digit).wait()

        @pl.when(n == 1)
        def _():
            landed(panel.at[spot(0, other)], *p, 0)

        @pl.when(n == 2)
        def _():
            landed(panel.at[prev], *p, 1)
            hop(3).start()
            landed(panel.at[nxt], *p, 2)
            hop(4).start()
            hop(5).start()
            hop(6).start()

        @pl.when(n == 3)
        def _():
            landed(panel.at[spot(3, other)], *p, 5)

        @pl.when(n == 4)
        def _():
            landed(panel.at[over, low], *p, 3)
            hop(7).start()
            landed(panel.at[over, high], *p, 4)
            hop(8).start()

        @pl.when(n == 5)
        def _():
            landed(panel.at[spot(1, other)], *p, 6)

        @pl.when(n == 7)
        def _():
            landed(panel.at[last, low], *p, 7)
            landed(panel.at[last, high], *p, 8)

        q = place(digit)
        acc[...] += lax.dot_general(
            panel[q], tile[q], (((1,), (1,)), ((), ())), preferred_element_type=F32
        )
        return lax.div(digits, 8)

    lax.fori_loop(0, 8, multiply, table(FORWARD))

    def launch(copies):
        def step(i):
            for axis, source, landing, send, recv in copies:
                target, device = along(axis, i)
                remote(source(target), landing.at[spots[axis]], send, recv, device).start()

        far_first(step)

    def seven(landing, send, recv):
        part_of = landing.at[pl.ds(0, 7)]
        return remote(part_of, part_of, send, recv, partner)

    me, first, second = (y, z, y, z), ("y", "z", "y", "z"), ("z", "y", "z", "y")
    them = (z, y, z, y)
    jobs = [
        [(first[h], lambda t, h=h: part.at[h, t], got1.at[h]) for h in range(4)],
        [(second[h], lambda t, h=h: sum1.at[h, t], got2.at[h]) for h in range(4)],
        [(second[h], lambda t, h=h: mine.at[h], wide.at[h]) for h in range(4)],
        [(first[h], lambda t, h=h: whole.at[h], users.at[h]) for h in range(4)],
    ]

    def users_start(stage, quarters):
        launch([jobs[stage][h] + (send_u.at[stage, h], recv_u.at[stage, h]) for h in quarters])

    def users_all(stage, h):
        return seven(jobs[stage][h][2], send_u.at[stage, h], recv_u.at[stage, h])

    def users_left(stage):
        for h in range(4):
            users_all(stage, h).wait_send()

    def summed(got):
        total = got[0].astype(F32)
        for k in range(1, 8):
            total = total + got[k].astype(F32)
        return total

    pairs = ((0, 1), (2, 3))
    for pair in pairs:
        for h in pair:
            for k in range(8):
                part[h, k] = acc[h * 64 : (h + 1) * 64, k * 128 : (k + 1) * 128].astype(BF16)
        users_start(0, pair)
    for h in range(4):
        got1[h, me[h]] = part[h, me[h]]
    for n in range(9):
        hop(n).wait_send()
    for pair in pairs:
        for h in pair:
            users_all(0, h).wait_recv()
            sum1[h] = summed(got1.at[h]).reshape(8, 8, 128)
        users_start(1, pair)
        for h in pair:
            got2[h, them[h]] = sum1[h, them[h]]
    users_left(0)
    for pair in pairs:
        for h in pair:
            users_all(1, h).wait_recv()
            mine[h] = summed(got2.at[h])
        users_start(2, pair)
        for h in pair:
            wide[h, them[h]] = mine[h]
    users_left(1)
    for pair in pairs:
        for h in pair:
            users_all(2, h).wait_recv()
            whole[h] = wide[h].reshape(64, 128).astype(BF16)
        users_start(3, pair)
        for h in pair:
            users[h, me[h]] = whole[h]
    users_left(2)
    for h in range(4):
        users_all(3, h).wait_recv()

    b = (send_b, recv_b)

    def lend(i):
        return remote(value.at[2 * i + 1], near.at[i], send_a.at[i], recv_a.at[i], partner)

    moves = [
        (pack.at[2, low], relay.at[0], beside(1)),
        (pack.at[2, high], relay.at[1], beside(3)),
        (pack.at[1, high], far.at[0, high], beside(1)),
        (pack.at[3, low], far.at[1, low], beside(3)),
        (pack.at[1, low], far.at[0, low], beside(1)),
        (pack.at[3, high], far.at[1, high], beside(3)),
    ]

    def pass_on(n):
        src, dst, device = moves[n]
        return remote(src, dst, send_b.at[n], recv_b.at[n], device)

    def meet(i):
        landed(near.at[i], send_a, recv_a, i)
        near[i] = value[2 * i] + near[i]

    def transposed(n, digits):
        digit = lax.rem(digits, 8)
        left = jnp.concatenate(
            [jnp.concatenate([users[h, k] for k in range(8)], axis=1) for h in range(4)], axis=0
        )
        value[digit] = jnp.dot(left, tile[place(digit)], preferred_element_type=F32)
        for step, i in ((0, 2), (1, 1), (3, 3), (5, 0)):
            @pl.when(n == step)
            def _(i=i):
                lend(i).start()

        @pl.when(n == 3)
        def _():
            meet(2)
            pack[2] = near[2].astype(BF16)
            pass_on(0).start()
            pass_on(1).start()

        @pl.when(n == 5)
        def _():
            meet(1)
            pack[1, HALF:] = near[1, HALF:].astype(BF16)
            pass_on(2).start()

        @pl.when(n == 6)
        def _():
            meet(3)
            pack[3, :HALF] = near[3, :HALF].astype(BF16)
            pass_on(3).start()

        return lax.div(digits, 8)

    lax.fori_loop(0, 8, transposed, table(BACKWARD))
    landed(relay.at[0], *b, 0)
    pack[1, :HALF] = (near[1, :HALF] + relay[0].astype(F32)).astype(BF16)
    pass_on(4).start()
    landed(relay.at[1], *b, 1)
    pack[3, HALF:] = (near[3, HALF:] + relay[1].astype(F32)).astype(BF16)
    pass_on(5).start()
    meet(0)

    users_left(3)
    for i in range(X):
        lend(i).wait_send()
    landed(far.at[0, high], *b, 2)
    landed(far.at[1, low], *b, 3)
    landed(far.at[0, low], *b, 4)
    landed(far.at[1, high], *b, 5)
    items = near[0] + far[0].astype(F32) + far[1].astype(F32)
    items_ref[...] = items

    gram = lax.dot_general(
        items, items, (((1,), (1,)), ((), ())), precision=HIGH, preferred_element_type=F32
    )
    for k in range(16):
        for c in range(2):
            cut[k // 2, (k % 2) * 2 + c] = gram[
                16 * k : 16 * k + 16, 128 * c : 128 * c + 128
            ].astype(BF16)

    spread = [
        ("r", lambda t: cut.at[t], gram1),
        ("y", lambda t: gsum1.at[t], gram2),
        ("z", lambda t: gsum2, gram3),
        ("y", lambda t: gsum3, gwide),
        ("r", lambda t: gwide, gram_ref),
    ]

    def spread_all(n):
        return seven(spread[n][2], send_g.at[n], recv_g.at[n])

    def move(n):
        axis, source, landing = spread[n]
        launch([spread[n] + (send_g.at[n], recv_g.at[n])])
        landing[spots[axis]] = source(spots[axis])[...]
        if n:
            spread_all(n - 1).wait_send()
        else:
            for k in range(6):
                pass_on(k).wait_send()
        spread_all(n).wait_recv()

    move(0)
    gsum1[...] = summed(gram1).reshape(8, 8, 128)
    move(1)
    gsum2[...] = summed(gram2)
    move(2)
    gsum3[...] = summed(gram3)
    move(3)

    move(4)
    spread_all(4).wait_send()


def krylov(own, tile):
    cell = (8, 128)
    dma = pltpu.SemaphoreType.DMA
    pairs = [(9,), (4, 4), (X,), (6,), (5,)]
    return pl.pallas_call(
        krylov_kernel,
        out_shape=(
            jax.ShapeDtypeStruct((256, 256), F32),
            jax.ShapeDtypeStruct((8, 8) + cell, F32),
        ),
        in_specs=[vmem(), pl.BlockSpec(memory_space=pl.ANY)],
        out_specs=(vmem(), vmem()),
        scratch_shapes=[
            pltpu.VMEM((8, 1024, 256), BF16),
            pltpu.VMEM((8, 256, 256), BF16),
            pltpu.VMEM((256, 256), BF16),
            pltpu.VMEM((256, 1024), F32),
            pltpu.VMEM((4, 8, 64, 128), BF16),
            pltpu.VMEM((4, 8, 64, 128), BF16),
            pltpu.VMEM((4, 8) + cell, F32),
            pltpu.VMEM((4, 8) + cell, F32),
            pltpu.VMEM((4,) + cell, F32),
            pltpu.VMEM((4, 8) + cell, F32),
            pltpu.VMEM((4, 64, 128), BF16),
            pltpu.VMEM((4, 8, 64, 128), BF16),
            pltpu.VMEM((8, 256, 256), F32),
            pltpu.VMEM((X, 256, 256), F32),
            pltpu.VMEM((X, 256, 256), BF16),
            pltpu.VMEM((2, HALF, 256), BF16),
            pltpu.VMEM((2, 256, 256), BF16),
            pltpu.VMEM((8, 4, 16, 128), BF16),
            pltpu.VMEM((8, 4, 16, 128), BF16),
            pltpu.VMEM((8,) + cell, F32),
            pltpu.VMEM((8,) + cell, F32),
            pltpu.VMEM(cell, F32),
            pltpu.VMEM((8,) + cell, F32),
            pltpu.VMEM(cell, F32),
            pltpu.VMEM((8,) + cell, F32),
            dma((8,)),
        ]
        + [dma(shape) for shape in pairs for _ in range(2)],
        compiler_params=pltpu.CompilerParams(
            collective_id=0, has_side_effects=True, vmem_limit_bytes=ROOM
        ),
        name="krylov",
    )(own, tile)


PANEL = 32
N = 256


def factor_kernel(gram_ref, items_ref, basis_ref, factor_ref, a_ref, d_ref):
    for k in range(32):
        for c in range(2):
            a_ref[8 * k : 8 * k + 8, 128 * c : 128 * c + 128] = gram_ref[
                k // 4, (k // 2 % 2) * 4 + c * 2 + k % 2
            ]

    for base in range(0, N, PANEL):
        w = a_ref[base : base + PANEL, :]
        d = jnp.zeros((PANEL, 128), F32)
        for low in range(0, PANEL, 8):
            part = w[low:, :]
            size = PANEL - low
            lane = lax.broadcasted_iota(jnp.int32, (size, N), 1)
            sub = lax.broadcasted_iota(jnp.int32, (size, N), 0) + low
            sub1 = sub[:, :128]
            first = base + low
            columns = [
                jnp.broadcast_to(part[:, first + b : first + b + 1], (size, 128)) for b in range(8)
            ]
            d_part = d[low:, :]
            for a in range(0, 8, 2):
                r = low + a
                one, two = columns[a], columns[a + 1]
                p11, p12 = one[a : a + 1, :], two[a : a + 1, :]
                p21, p22 = one[a + 1 : a + 2, :], two[a + 1 : a + 2, :]
                inv1 = 1.0 / p11
                inv2 = p11 * (1.0 / (p11 * p22 - p21 * p12))
                ratio = p21 * inv1
                m1 = jnp.where(sub1 > r, one * inv1, 0.0)
                m2 = jnp.where(sub1 > r + 1, (two - m1 * p12) * inv2, 0.0)
                for b in range(a + 2, 8):
                    top = columns[b][a : a + 1, :]
                    next_top = columns[b][a + 1 : a + 2, :] - ratio * top
                    columns[b] = columns[b] - m1 * top - m2 * next_top
                lane1 = lane[:1]
                line1 = jnp.where(lane1 == base + r, 1.0, part[a : a + 1, :])
                ratio2 = jnp.concatenate([ratio, ratio], axis=1)
                line2 = jnp.where(lane1 == base + r, 0.0, part[a + 1 : a + 2, :]) - ratio2 * line1
                line1 = jnp.where(lane1 == base + r + 1, 0.0, line1)
                line2 = jnp.where(lane1 == base + r + 1, 1.0, line2)
                gone = ((lane == base + r) & (sub > r)) | ((lane == base + r + 1) & (sub > r + 1))
                part = (
                    jnp.where(gone, 0.0, part)
                    - jnp.concatenate([m1, m1], axis=1) * line1
                    - jnp.concatenate([m2, m2], axis=1) * line2
                )
                d_part = jnp.where(sub1 == r, p11, d_part)
                d_part = jnp.where(sub1 == r + 1, p22 - ratio * p12, d_part)
            w = part if low == 0 else jnp.concatenate([w[:low], part], axis=0)
            d = d_part if low == 0 else jnp.concatenate([d[:low], d_part], axis=0)
        a_ref[base : base + PANEL, :] = w
        d_ref[base : base + PANEL, :] = d
        after = base + PANEL
        if after == N:
            break
        lane = lax.broadcasted_iota(jnp.int32, (PANEL, N), 1)
        sub = lax.broadcasted_iota(jnp.int32, (PANEL, N), 0) + base
        scaled = jnp.where(lane >= after, w / jnp.concatenate([d, d], axis=1), 0.0).T
        inside = (lane < after) & (lane >= sub)
        right = jnp.where(inside, jnp.where(lane == sub, 1.0, 0.0), w)
        for top, bottom in ((after, after + PANEL), (after + PANEL, N)):
            if top < bottom:
                lane = lax.broadcasted_iota(jnp.int32, (bottom - top, N), 1)
                kept = jnp.where((lane >= base) & (lane < after), 0.0, a_ref[top:bottom, :])
                a_ref[top:bottom, :] = kept - jnp.dot(
                    scaled[top:bottom], right, precision=HIGH, preferred_element_type=F32
                )

    lane = lax.broadcasted_iota(jnp.int32, (N, N), 1)
    sub = lax.broadcasted_iota(jnp.int32, (N, N), 0)
    pivots = d_ref[...]
    scale = 1.0 / jnp.sqrt(pivots)
    scale = jnp.concatenate([scale, scale], axis=1)
    full = jnp.where(lane == sub, jnp.concatenate([pivots, pivots], axis=1), a_ref[...])
    factor_ref[...] = jnp.where(lane >= sub, full, 0.0) * scale
    inverse = jnp.where(lane < sub, full, jnp.where(lane == sub, 1.0, 0.0)) * scale
    basis_ref[...] = jnp.dot(
        inverse, items_ref[...], precision=HIGH, preferred_element_type=F32
    ).T


def factor_call(gram, items):
    return pl.pallas_call(
        factor_kernel,
        out_shape=(
            jax.ShapeDtypeStruct((256, 256), F32),
            jax.ShapeDtypeStruct((256, 256), F32),
        ),
        in_specs=[vmem(), vmem()],
        out_specs=(vmem(), vmem()),
        scratch_shapes=[pltpu.VMEM((N, N), F32), pltpu.VMEM((N, 128), F32)],
        compiler_params=pltpu.CompilerParams(vmem_limit_bytes=ROOM),
        name="factor",
    )(gram, items)


def local(blocks, block_row, block_col, counts, start_block):
    tile = dense_tile(block_row[0, 0], block_col[0, 0], counts, blocks[0, 0])
    items, gram = krylov(start_block, tile)
    return factor_call(gram, items)


def solution(mesh):
    return jax.shard_map(
        local,
        mesh=mesh,
        in_specs=(
            P("rows", "cols", None, None, None),
            P("rows", "cols", None),
            P("rows", "cols", None),
            P("rows", "cols"),
            P(("cols", "rows"), None),
        ),
        out_specs=(P(("cols", "rows"), None), P()),
        check_vma=False,
    )
```
